256 devices in a mesh: tm: 32 (over z_hi, y, x), head: 8 (over z_lo, core).
Axes of the slice: x: 4, y: 4, z: 8 (z_hi: 2, z_lo: 4; z = z_hi * 4 + z_lo), core: 2. Of those that a mesh axis runs over, the one named last changes fastest.
Arguments:
- patches: bfloat16 [384, 256, 1152], P('tm', None, 'head'), may hold values from -6 to 6
- grid_rows: int32 [384], P('tm'), may hold values from 8 to 16
- frame_ids: int32 [384], P('tm'), may hold values from 0 to 383, as said below
- ln_gain: float32 [1152], replicated, may hold values from 0.1 to 1.9
- w_qkv: bfloat16 [3, 1152, 1152], P(None, None, 'head'), may hold values from -5.9514821 to 5.9514821
- w_out: bfloat16 [1152, 1152], P('head'), may hold values from -0.1875 to 0.1875
- w_conn: bfloat16 [1152, 4096], P(None, 'head'), may hold values from -0.1875 to 0.1875
- norm_gain: float32 [4096], replicated, may hold values from 0.1 to 1.9
- w_x: bfloat16 [4096, 4096], P(None, 'head'), may hold values from -0.09375 to 0.09375
- w_b: bfloat16 [4096, 1024], P(None, 'head'), may hold values from -0.09375 to 0.09375
- w_c: bfloat16 [4096, 1024], P(None, 'head'), may hold values from -0.09375 to 0.09375
- w_dt: bfloat16 [4096, 64], P(None, 'head'), may hold values from -0.09375 to 0.09375
- dt_bias: float32 [64], P('head'), may hold values from -1 to 1
- a_log: float32 [64], P('head'), may hold values from -14 to -3.2
- d_skip: float32 [64], P('head'), may hold values from 0.5 to 1.5
- out_gain: float32 [4096], P('head'), may hold values from 0.1 to 1.9
Outputs:
- stream: bfloat16 [24576, 4096], P('tm', 'head')
- ssd_out: bfloat16 [24576, 4096], P('tm', 'head')
The draws below stay inside these ranges and needn't reach their ends.
Inputs may be any that keep to these rules, and one draw needn't show every extreme that they name: frame_ids is a permutation of the frames; the 12 slots of one tm index hold frames of 12 different time shards, time shard of a frame being frame // 12.
All inputs are finite; a program needn't handle non-finite values.
Results may differ from the reference program's by a relative error of at most 0.013.
Values may be sent and summed in bfloat16 or wider, within the bound.
No kernel may reach another device: no remote copies, remote signals or barrier semaphores. Data moves between devices by JAX's collectives and lax.ppermute only.
A program may use at most 128 MiB of HBM per device.

```python
import math
import jax
import jax.numpy as jnp
from jax import lax

GRID = 16
POOL = 4
P_SIZE = 256
PT = 64
VHEADS = 16
VHD = 72
DV = 1152
D = 4096
HEADS = 64
HDIM = 64
STATE = 128
GROUPS = 8
FR_DEV = 12
FRAMES = 384
TOKENS = 24576
STRETCH = 256
N_TM = 32


def draw_frame_ids(key, part):
    offset_key, owner_key, order_key, slot_key = jax.random.split(key, 4)
    offsets = jax.random.permutation(offset_key, N_TM)[:FR_DEV]
    owners = jax.random.permutation(owner_key, N_TM)
    within = jax.vmap(lambda subkey: jax.random.permutation(subkey, FR_DEV))(jax.random.split(order_key, N_TM))
    slot_order = jax.vmap(lambda subkey: jax.random.permutation(subkey, FR_DEV))(jax.random.split(slot_key, N_TM))
    sender = jnp.arange(N_TM)[:, None]
    column = jnp.broadcast_to(jnp.arange(FR_DEV)[None, :], (N_TM, FR_DEV))
    target = (sender + offsets[None, :]) % N_TM
    frames = target * FR_DEV + within[target, column]
    placed = jnp.zeros((N_TM, FR_DEV), jnp.int32).at[jnp.broadcast_to(owners[:, None], (N_TM, FR_DEV)), slot_order].set(frames.astype(jnp.int32))
    return placed.reshape(N_TM * FR_DEV)


def draw_w_qkv(key, part):
    base = jnp.clip(jax.random.normal(key, (3, DV, DV), jnp.float32), -5.0, 5.0) * DV ** (-0.5)
    return base.astype(jnp.bfloat16)


def draw_a_log(key, part):
    pick_key, fast_key, slow_key = jax.random.split(key, 3)
    fast_share = 5
    fast = jax.random.randint(pick_key, (HEADS,), 0, 10) < fast_share
    quick = jax.random.uniform(fast_key, (HEADS,), jnp.float32, math.log(1.0 / 50.0), math.log(1.0 / 25.0))
    gentle = jax.random.uniform(slow_key, (HEADS,), jnp.float32, math.log(0.2), math.log(2.0)) - math.log(TOKENS)
    return jnp.where(fast, quick, gentle)


def place_ends(array, rng, least, high):
    longest = array.shape.index(max(array.shape))
    spots = []
    for shift in (0, 1):
        where = [jax.random.randint(jax.random.fold_in(rng, axis), (), 0, length) for axis, length in enumerate(array.shape)]
        where[longest] = (where[longest] + shift) % array.shape[longest]
        spots.append(tuple(where))
    return array.at[spots[0]].set(least).at[spots[1]].set(high)


def levels(stream_key, dims, cuts, smallest, largest):
    loudness, own = 1.0, jax.random.fold_in(stream_key, 6)
    for position, parts in cuts:
        heights = jnp.exp(jax.random.uniform(jax.random.fold_in(own, position), (parts,), jnp.float32, smallest / len(cuts), largest / len(cuts)))
        loudness = loudness * jnp.repeat(heights, dims[position] // parts).reshape([-1 if axis == position else 1 for axis in range(len(dims))])
    return loudness


def gaussian(own_key, dims, deviation, limit, cuts=(), kind=jnp.bfloat16):
    level = levels(own_key, dims, cuts, -0.22, 0.18) if cuts else 1.0
    result = jax.random.normal(own_key, dims, jnp.float32) * deviation * level
    return jnp.minimum(jnp.maximum(result, -limit), limit).astype(kind)


def setup_inputs(seed: int = 0) -> dict:
    seeds = jax.random.split(jax.random.key(seed), 17)
    patches = gaussian(seeds[0], (FRAMES, P_SIZE, DV), 1.0, 6.0, ((0, 32), (2, 8)))
    grid_rows = place_ends(jax.random.randint(seeds[1], (FRAMES,), GRID // 2, GRID + 1), jax.random.fold_in(seeds[1], 1), GRID // 2, GRID).astype(jnp.int32)
    frame_ids = draw_frame_ids(jax.random.fold_in(seeds[16], 71), 0)
    ln_gain = jnp.clip(1.0 + 0.18 * jax.random.normal(seeds[3], (DV,), jnp.float32), 0.1, 1.9)
    w_qkv = draw_w_qkv(jax.random.fold_in(seeds[16], 71), 0)
    w_out = gaussian(seeds[5], (DV, DV), DV ** -0.5, 0.1875, ((0, 8),))
    w_conn = gaussian(seeds[6], (DV, D), DV ** -0.5, 0.1875, ((1, 8),))
    norm_gain = jnp.clip(1.0 + 0.18 * jax.random.normal(seeds[7], (D,), jnp.float32), 0.1, 1.9)
    w_x = gaussian(seeds[8], (D, HEADS * HDIM), D ** -0.5, 0.09375, ((1, 8),))
    w_b = gaussian(seeds[9], (D, GROUPS * STATE), D ** -0.5, 0.09375, ((1, 8),))
    w_c = gaussian(seeds[10], (D, GROUPS * STATE), D ** -0.5, 0.09375, ((1, 8),))
    w_dt = gaussian(seeds[11], (D, HEADS), D ** -0.5, 0.09375, ((1, 8),))
    dt_bias = jnp.clip(jax.random.uniform(seeds[12], (HEADS,), jnp.float32, -1.0, 1.0) * levels(seeds[12], (HEADS,), ((0, 8),), -0.4, 0.0), -1.0, 1.0)
    a_log = draw_a_log(jax.random.fold_in(seeds[16], 71), 0)
    d_skip = jnp.clip(0.5 + 1.0 * jax.random.uniform(seeds[14], (HEADS,), jnp.float32) ** levels(seeds[14], (HEADS,), ((0, 8),), -0.2, 0.2), 0.5, 1.5)
    out_gain = jnp.clip(1.0 + 0.18 * jax.random.normal(seeds[15], (HEADS * HDIM,), jnp.float32), 0.1, 1.9)
    return dict(patches=patches, grid_rows=grid_rows, frame_ids=frame_ids, ln_gain=ln_gain, w_qkv=w_qkv, w_out=w_out, w_conn=w_conn, norm_gain=norm_gain, w_x=w_x, w_b=w_b, w_c=w_c, w_dt=w_dt, dt_bias=dt_bias, a_log=a_log, d_skip=d_skip, out_gain=out_gain)


highest = lax.Precision.HIGHEST

def layer_norm(rows, gain):
    values = rows.astype(jnp.float32)
    centre = lax.optimization_barrier(jnp.mean(values, axis=-1, keepdims=True))
    spread = lax.optimization_barrier(jnp.mean(jnp.square(values - centre), axis=-1, keepdims=True))
    return ((values - centre) * lax.rsqrt(spread + 1e-06) * gain).astype(jnp.bfloat16)

def vision_frames(frames, grid_rows, ln_gain, w_qkv, w_out):
    frame_count = frames.shape[0]
    normed = layer_norm(frames, ln_gain).reshape(frame_count * P_SIZE, DV)
    queries, keys_all, values_all = [jnp.dot(normed, w_qkv[member], preferred_element_type=jnp.float32).astype(jnp.bfloat16).reshape(frame_count, P_SIZE, VHEADS, VHD) for member in range(3)]
    scores = jnp.einsum('fqhd,fkhd->fhqk', queries.astype(jnp.float32), keys_all.astype(jnp.float32)) * VHD ** (-0.5)
    valid_count = grid_rows * GRID
    usable = jnp.arange(P_SIZE)[None, :] < valid_count[:, None]
    scores = jnp.where(usable[:, None, None, :], scores, -1e+30)
    row_max = lax.optimization_barrier(jnp.max(scores, axis=-1, keepdims=True))
    powered = jnp.exp(scores - row_max)
    weights_soft = (powered / lax.optimization_barrier(jnp.sum(powered, axis=-1, keepdims=True))).astype(jnp.bfloat16)
    context = jnp.einsum('fhqk,fkhd->fqhd', weights_soft.astype(jnp.float32), values_all.astype(jnp.float32)).astype(jnp.bfloat16)
    attended = jnp.dot(context.reshape(frame_count * P_SIZE, DV), w_out, preferred_element_type=jnp.float32)
    summed = frames.astype(jnp.float32).reshape(frame_count * P_SIZE, DV) + attended
    pooled = lax.optimization_barrier(jnp.mean(summed.reshape(frame_count, PT, POOL, DV), axis=2))
    kept_tokens = jnp.arange(PT)[None, :] * POOL < valid_count[:, None]
    return jnp.where(kept_tokens[:, :, None], pooled, 0.0).astype(jnp.bfloat16)

def project(stream_rows, norm_gain, w_x, w_b, w_c, w_dt, dt_bias, a_log):
    values = stream_rows.astype(jnp.float32)
    normed = (values * lax.rsqrt(lax.optimization_barrier(jnp.mean(values * values, axis=-1, keepdims=True)) + 1e-05) * norm_gain).astype(jnp.bfloat16)
    inner_rows = jnp.dot(normed, w_x, preferred_element_type=jnp.float32).astype(jnp.bfloat16)
    write_keys = jnp.dot(normed, w_b, preferred_element_type=jnp.float32).astype(jnp.bfloat16)
    read_keys = jnp.dot(normed, w_c, preferred_element_type=jnp.float32).astype(jnp.bfloat16)
    step_size = jax.nn.softplus(jnp.dot(normed, w_dt, preferred_element_type=jnp.float32) + dt_bias)
    log_decay = -jnp.exp(a_log) * step_size
    return (inner_rows, write_keys, read_keys, step_size, log_decay)

def ssd_stretch(inner_rows, write_keys, read_keys, step_size, log_decay, d_skip, state):
    length = inner_rows.shape[0]
    head_count = step_size.shape[1]
    groups = write_keys.shape[1] // STATE
    per_group = head_count // groups
    cumul = jnp.cumsum(log_decay, axis=0)
    scaled = inner_rows.astype(jnp.float32).reshape(length, head_count, HDIM) * step_size[:, :, None]
    writers = write_keys.astype(jnp.float32).reshape(length, groups, STATE)
    readers = read_keys.astype(jnp.float32).reshape(length, groups, STATE)
    intersection = jnp.einsum('tgn,sgn->gts', readers, writers, precision=highest)
    causal = (jnp.arange(length)[:, None] >= jnp.arange(length)[None, :])[:, :, None]
    spans = cumul[:, None, :] - cumul[None, :, :]
    decays = jnp.where(causal, jnp.exp(jnp.where(causal, spans, 0.0)), 0.0)
    mixing = jnp.repeat(intersection, per_group, axis=0) * jnp.transpose(decays, (2, 0, 1))
    within = jnp.einsum('hts,shp->thp', mixing, scaled, precision=highest)
    carried = jnp.einsum('tgn,gkpn->tgkp', readers, state.reshape(groups, per_group, HDIM, STATE), precision=highest).reshape(length, head_count, HDIM) * jnp.exp(cumul)[:, :, None]
    remaining = jnp.exp(cumul[-1][None, :] - cumul)
    fresh_state = jnp.einsum('sgkp,sgn->gkpn', (scaled * remaining[:, :, None]).reshape(length, groups, per_group, HDIM), writers, precision=highest).reshape(head_count, HDIM, STATE)
    new_state = jnp.exp(cumul[-1])[:, None, None] * state + fresh_state
    outputs = within + carried + d_skip[None, :, None] * inner_rows.astype(jnp.float32).reshape(length, head_count, HDIM)
    return (outputs, new_state, cumul)

def group_norm(outputs, out_gain, groups):
    length = outputs.shape[0]
    grouped = outputs.reshape(length, groups, -1)
    normed = grouped * lax.rsqrt(lax.optimization_barrier(jnp.mean(grouped * grouped, axis=-1, keepdims=True)) + 1e-05)
    return (normed.reshape(length, -1) * out_gain).astype(jnp.bfloat16)

def reference(patches, grid_rows, frame_ids, ln_gain, w_qkv, w_out, w_conn, norm_gain, w_x, w_b, w_c, w_dt, dt_bias, a_log, d_skip, out_gain):

    def vision_block(block_id):
        first = (block_id * FR_DEV).astype(jnp.int32)
        frames = lax.dynamic_slice_in_dim(patches, first, FR_DEV, 0)
        rows_valid = lax.dynamic_slice_in_dim(grid_rows, first, FR_DEV, 0)
        return vision_frames(frames, rows_valid, ln_gain, w_qkv, w_out)
    owned = lax.map(vision_block, jnp.arange(FRAMES // FR_DEV, dtype=jnp.int32)).reshape(FRAMES, PT, DV)
    placement = jnp.zeros((FRAMES,), jnp.int32).at[frame_ids].set(jnp.arange(FRAMES, dtype=jnp.int32))
    in_time = owned[placement].reshape(TOKENS, DV)
    stream = jnp.dot(in_time, w_conn, preferred_element_type=jnp.float32).astype(jnp.bfloat16)

    def stretch_step(state, rows):
        inner_rows, write_keys, read_keys, step_size, log_decay = project(rows, norm_gain, w_x, w_b, w_c, w_dt, dt_bias, a_log)
        outputs, new_state, cumul = ssd_stretch(inner_rows, write_keys, read_keys, step_size, log_decay, d_skip, state)
        return (new_state, group_norm(outputs, out_gain, GROUPS))
    zero_state = jnp.zeros((HEADS, HDIM, STATE), jnp.float32)
    final_state, mixed = lax.scan(stretch_step, zero_state, stream.reshape(TOKENS // STRETCH, STRETCH, D))
    return (stream, mixed.reshape(TOKENS, HEADS * HDIM))
```

```python
import functools
import jax
import jax.numpy as jnp
from jax import lax
from jax.experimental import pallas as pl
from jax.experimental.pallas import tpu as pltpu
from jax.sharding import Mesh, PartitionSpec as P

GRID = 16
POOL = 4
VHD = 72
HDIM = 64
STATE = 128
Q = 256
XW = 640

F32 = jnp.float32
BF16 = jnp.bfloat16
highest = lax.Precision.HIGHEST
VMEM_SPEC = pl.BlockSpec(memory_space=pltpu.VMEM)
SMEM_SPEC = pl.BlockSpec(memory_space=pltpu.SMEM)
ANY_SPEC = pl.BlockSpec(memory_space=pl.ANY)


def params(mib):
    return pltpu.CompilerParams(vmem_limit_bytes=mib * 2**20)


def dot(a, b, ca, cb, precision=None):
    return lax.dot_general(
        a, b, (((ca,), (cb,)), ((), ())), preferred_element_type=F32, precision=precision
    )


def ring_shift(value, axis, size, shift):
    return lax.ppermute(value, axis, [(i, (i + shift) % size) for i in range(size)])


def swap_core(value):
    return lax.ppermute(value, "c", [(0, 1), (1, 0)])


def gather_ring(block, axis):
    half = block.shape[0] // 2
    before = ring_shift(block, axis, 4, 1)
    after = ring_shift(block, axis, 4, -1)
    far_lo = ring_shift(before[:half], axis, 4, 1)
    far_hi = ring_shift(after[half:], axis, 4, -1)
    return (block, before, far_lo, far_hi, after)


def vision_kernel(place, rows, mine, other, gain, pool, *rest):
    weights = rest[:10]
    keep, give, wx, wy, qkv, ctx, sems = rest[10:]
    frame = pl.program_id(0)
    first = place[0] == 0

    def copies():
        made = []
        for member, (held, slot) in enumerate(((wx, 1), (wy, 2))):
            own, before, far_lo, far_hi, after = weights[5 * member : 5 * member + 5]
            for k, (source, lo, size) in enumerate(
                ((own, 0, 4), (before, 0, 4), (far_lo, 0, 2), (far_hi, 2, 2), (after, 0, 4))
            ):
                distance = (0, 1, 2, 2, 3)[k]
                index = lax.rem(place[slot] + 4 - distance, 4)
                made.append(
                    pltpu.make_async_copy(
                        source, held.at[index, pl.ds(lo, size)], sems.at[5 * member + k]
                    )
                )
        return made

    @pl.when(frame == 0)
    def _():
        for copy in copies():
            copy.start()

    parts = []
    for z in range(4):
        a, b = mine[z, 0].astype(F32), other[z, 0].astype(F32)
        parts.append(jnp.where(first, a, b))
        parts.append(jnp.where(first, b, a))
    x = jnp.concatenate(parts, axis=0)
    width = x.shape[0]
    centre = jnp.sum(x, axis=0, keepdims=True) * (1.0 / width)
    x = x - centre
    spread = jnp.sum(x * x, axis=0, keepdims=True) * (1.0 / width)
    normed = (x * lax.rsqrt(spread + 1e-06) * gain[...]).astype(BF16)

    @pl.when(frame == 0)
    def _():
        for copy in copies():
            copy.wait()

    for m in range(3):
        left = wx[m].reshape(576, XW)
        right = wy[m].reshape(576, width - XW)
        qkv[m] = dot(left, normed[:XW], 1, 0) + dot(right, normed[XW:], 1, 0)
    valid = rows[frame] * GRID
    usable = lax.broadcasted_iota(jnp.int32, (256, 256), 0) < valid
    for h in range(8):
        span = pl.ds(h * VHD, VHD)
        q, k, v = (qkv[m, span, :].astype(BF16) for m in range(3))
        scores = dot(k, q, 0, 0) * VHD ** (-0.5)
        scores = jnp.where(usable, scores, -1e30)
        top = jnp.max(scores, axis=0, keepdims=True)
        powered = jnp.exp(scores - top)
        total = jnp.sum(powered, axis=0, keepdims=True)
        ctx[span, :] = dot(v, powered.astype(BF16), 1, 0) * (1.0 / total)
    pooled = dot(ctx[...].astype(BF16), pool[...], 1, 0)
    high = pooled.astype(BF16)
    low = (pooled - high.astype(F32)).astype(BF16)
    both = jnp.concatenate([high, low], axis=1)
    out_x = dot(both, wx[3].reshape(576, XW), 0, 0)
    out_y = dot(both, wy[3].reshape(576, width - XW), 0, 0)
    attended = jnp.concatenate([out_x, out_y], axis=1)
    attended = (attended[:64] + attended[64:]).T
    for z in range(4):
        a = attended[(2 * z) * 144 : (2 * z + 1) * 144]
        b = attended[(2 * z + 1) * 144 : (2 * z + 2) * 144]
        own = jnp.where(first, a, b) + dot(mine[z, 0], pool[...], 1, 0)
        far = jnp.where(first, b, a)
        keep[z, 0] = jnp.concatenate([own[:72], own[72:]], axis=1)
        give[z, 0] = jnp.concatenate([far[:72], far[72:]], axis=1)


def vision(place, rows, mine, other, ln_gain, pool, wx, wy):
    part = pl.BlockSpec((4, 1, 144, 256), lambda f: (0, f, 0, 0))
    out = pl.BlockSpec((4, 1, 72, 128), lambda f: (0, f, 0, 0))
    shape = jax.ShapeDtypeStruct((4, 3, 72, 128), F32)
    return pl.pallas_call(
        vision_kernel,
        grid=(3,),
        in_specs=[SMEM_SPEC, SMEM_SPEC, part, part, VMEM_SPEC, VMEM_SPEC] + [ANY_SPEC] * 10,
        out_specs=(out, out),
        out_shape=(shape, shape),
        scratch_shapes=[
            pltpu.VMEM((4, 4, 144, XW), BF16),
            pltpu.VMEM((4, 4, 144, 1152 - XW), BF16),
            pltpu.VMEM((3, 576, 256), F32),
            pltpu.VMEM((576, 256), F32),
            pltpu.SemaphoreType.DMA((10,)),
        ],
        compiler_params=params(48),
        name="vision",
    )(place, rows, mine, other, ln_gain, pool, *wx, *wy)


def bucket_kernel(target, seen, out):
    out[...] = jnp.zeros_like(out)
    for f in range(12):
        out[target[f]] = seen[f]


def bucket(target, seen):
    return pl.pallas_call(
        bucket_kernel,
        in_specs=[SMEM_SPEC, VMEM_SPEC],
        out_specs=VMEM_SPEC,
        out_shape=jax.ShapeDtypeStruct((32, 72, 128), BF16),
        compiler_params=params(16),
        name="bucket",
    )(target, seen)


def place_kernel(source, incoming, out):
    left = lax.broadcasted_iota(jnp.int32, (72, 128), 1) < 64
    for pair in range(6):
        a = incoming[source[2 * pair]].astype(F32)
        b = incoming[source[2 * pair + 1]].astype(F32)
        lanes = pl.ds(128 * pair, 128)
        top = jnp.where(left, a, pltpu.roll(b, 64, 1))
        bottom = jnp.where(left, pltpu.roll(a, 64, 1), b)
        out[:, lanes] = jnp.concatenate([top, bottom], axis=0).astype(BF16)


def place_frames(source, incoming):
    return pl.pallas_call(
        place_kernel,
        in_specs=[SMEM_SPEC, VMEM_SPEC],
        out_specs=VMEM_SPEC,
        out_shape=jax.ShapeDtypeStruct((144, 768), BF16),
        compiler_params=params(16),
        name="place",
    )(source, incoming)


def stream_kernel(place, mine, other, w_conn, stream, seen, squares):
    first = place[0] == 0
    for z in range(4):
        a, b = mine[z], other[z]
        seen[pl.ds(288 * z, 144), :] = jnp.where(first, a, b)
        seen[pl.ds(288 * z + 144, 144), :] = jnp.where(first, b, a)
    made = dot(w_conn[...], seen[...], 0, 0).astype(BF16)
    wide = made.astype(F32)
    squares[...] = jnp.broadcast_to(
        jnp.sum(wide * wide, axis=0, keepdims=True), squares.shape
    )
    stream[...] = wide.T.astype(BF16)


def stream_rows(place, mine, other, w_conn):
    tokens, width = mine.shape[2], w_conn.shape[1]
    return pl.pallas_call(
        stream_kernel,
        in_specs=[SMEM_SPEC, VMEM_SPEC, VMEM_SPEC, VMEM_SPEC],
        out_specs=(VMEM_SPEC, VMEM_SPEC, VMEM_SPEC),
        out_shape=(
            jax.ShapeDtypeStruct((tokens, width), BF16),
            jax.ShapeDtypeStruct((1152, tokens), BF16),
            jax.ShapeDtypeStruct((8, tokens), F32),
        ),
        compiler_params=params(40),
        name="stream",
    )(place, mine, other, w_conn)


def over_heads(rows, length):
    return jnp.concatenate(
        [jnp.broadcast_to(rows[h : h + 1], (HDIM, length)) for h in range(8)], axis=0
    )


def triangle(transposed):
    a = lax.broadcasted_iota(jnp.int32, (Q, Q), 0)
    b = lax.broadcasted_iota(jnp.int32, (Q, Q), 1)
    return jnp.where(a >= b if transposed else a <= b, 1.0, 0.0).astype(F32)


def state_kernel(
    seen, wide, squares, bias, a_log, inner, writers, readers, steps, logs, enter, payload
):
    raw = dot(wide[...], seen[...], 1, 0)
    scale = lax.rsqrt(jnp.sum(squares[...], axis=0) * (1.0 / 4096) + 1e-05)
    scale = scale[0:1]
    inner[...] = (raw[:512] * scale).astype(BF16)
    writers[...] = (raw[512:640] * scale).astype(BF16)
    readers[...] = (raw[640:768] * scale).astype(BF16)
    before = raw[768:776] * scale + bias[:, :1]
    step = jnp.maximum(before, 0.0) + jnp.log1p(jnp.exp(-jnp.abs(before)))
    log = -jnp.exp(a_log[:, :1]) * step
    steps[...] = step
    logs[...] = log
    upper = triangle(False)
    count = seen.shape[1] // Q
    state = jnp.zeros((512, STATE), F32)
    whole = jnp.zeros((8, 1), F32)
    for n in range(count):
        lanes = slice(n * Q, (n + 1) * Q)
        cumul = dot(log[:, lanes], upper, 1, 0, highest)
        total = cumul[:, Q - 1 : Q]
        enter[n] = state.astype(BF16)
        left = over_heads(step[:, lanes] * jnp.exp(total - cumul), Q)
        scaled = (inner[:, lanes].astype(F32) * left).astype(BF16)
        fresh = dot(scaled, writers[:, lanes], 1, 1)
        state = state * over_heads(jnp.broadcast_to(jnp.exp(total), (8, STATE)), STATE) + fresh
        whole = whole + total
    payload[pl.ds(0, 512), :] = state
    payload[pl.ds(512, 8), :] = jnp.broadcast_to(jnp.exp(whole), (8, STATE))


def local_states(seen, wide, squares, bias, a_log):
    tokens = seen.shape[1]
    return pl.pallas_call(
        state_kernel,
        in_specs=[VMEM_SPEC] * 5,
        out_specs=(VMEM_SPEC,) * 7,
        out_shape=(
            jax.ShapeDtypeStruct((512, tokens), BF16),
            jax.ShapeDtypeStruct((STATE, tokens), BF16),
            jax.ShapeDtypeStruct((STATE, tokens), BF16),
            jax.ShapeDtypeStruct((8, tokens), F32),
            jax.ShapeDtypeStruct((8, tokens), F32),
            jax.ShapeDtypeStruct((tokens // Q, 512, STATE), BF16),
            jax.ShapeDtypeStruct((520, STATE), F32),
        ),
        compiler_params=params(40),
        name="states",
    )(seen, wide, squares, bias, a_log)


def within_kernel(inner, writers, readers, steps, logs, enter, d_skip, out, begun):
    upper, lower = triangle(False), triangle(True)
    causal = upper > 0.0
    whole = jnp.zeros((8, 1), F32)
    for n in range(inner.shape[1] // Q):
        lanes = slice(n * Q, (n + 1) * Q)
        log = logs[:, lanes]
        cumul = dot(log, upper, 1, 0, highest)
        column = dot(lower, log, 1, 1, highest)
        begun[:, lanes] = cumul + whole
        whole = whole + cumul[:, Q - 1 : Q]
        meets = dot(writers[:, lanes], readers[:, lanes], 0, 0)
        carried = dot(enter[n], readers[:, lanes], 1, 0)
        grown = jnp.exp(cumul)
        step = steps[:, lanes]
        for h in range(8):
            span = slice(h * HDIM, (h + 1) * HDIM)
            apart = jnp.minimum(cumul[h : h + 1] - column[:, h : h + 1], 0.0)
            mixing = jnp.where(causal, meets * jnp.exp(apart), 0.0).astype(BF16)
            own = inner[span, lanes].astype(F32)
            scaled = (own * step[h : h + 1]).astype(BF16)
            out[span, lanes] = (
                dot(scaled, mixing, 1, 0)
                + carried[span] * grown[h : h + 1]
                + d_skip[span] * own
            )


def within(inner, writers, readers, steps, logs, enter, d_skip):
    tokens = inner.shape[1]
    return pl.pallas_call(
        within_kernel,
        in_specs=[VMEM_SPEC] * 7,
        out_specs=(VMEM_SPEC,) * 2,
        out_shape=(
            jax.ShapeDtypeStruct((512, tokens), F32),
            jax.ShapeDtypeStruct((8, tokens), F32),
        ),
        compiler_params=params(40),
        cost_estimate=pl.CostEstimate(
            flops=2_000_000_000, bytes_accessed=6_000_000, transcendentals=2_000_000
        ),
        name="within",
    )(inner, writers, readers, steps, logs, enter, d_skip)


def finish_kernel(local, begun, readers, state, gain, out):
    for n in range(local.shape[1] // Q):
        lanes = slice(n * Q, (n + 1) * Q)
        carried = dot(state[...], readers[:, lanes], 1, 0)
        y = local[:, lanes] + carried * over_heads(jnp.exp(begun[:, lanes]), Q)
        mean = jnp.sum(y * y, axis=0, keepdims=True) * (1.0 / 512)
        y = y * lax.rsqrt(mean + 1e-05) * gain[...]
        out[lanes, :] = y.T.astype(BF16)


def finish(local, begun, readers, state, gain):
    return pl.pallas_call(
        finish_kernel,
        in_specs=[VMEM_SPEC] * 5,
        out_specs=VMEM_SPEC,
        out_shape=jax.ShapeDtypeStruct((local.shape[1], 512), BF16),
        compiler_params=params(40),
        name="finish",
    )(local, begun, readers, state, gain)


def split_payload(payload):
    payload = payload.astype(F32)
    return payload[:512].reshape(8, HDIM, STATE), payload[512:].reshape(8, 1, STATE)


def pass_along(payload, axis, size):
    position = lax.axis_index(axis)
    sent = payload.astype(BF16)
    got = [split_payload(ring_shift(sent, axis, size, k)) for k in range(1, size)]
    own = split_payload(payload)
    ahead, shrink = jnp.zeros_like(own[0]), jnp.ones_like(own[1])
    for k in range(1, size):
        state, decay = got[k - 1]
        here = position >= k
        ahead = jnp.where(here, ahead + shrink * state, ahead)
        shrink = jnp.where(here, shrink * decay, shrink)
    total, left = ahead * own[1] + own[0], shrink * own[1]
    for k in range(size - 1, 0, -1):
        state, decay = got[k - 1]
        here = position < k
        total = jnp.where(here, total * decay + state, total)
        left = jnp.where(here, left * decay, left)
    joined = jnp.concatenate([total.reshape(512, STATE), left.reshape(8, STATE)], axis=0)
    return ahead, shrink, joined


def on_device(
    patches, grid_rows, frame_ids, ln_gain, w_qkv, w_out, w_conn, norm_gain,
    w_x, w_b, w_c, w_dt, dt_bias, a_log, d_skip, out_gain,
):
    core, x, y, zl, zh = (lax.axis_index(a) for a in ("c", "x", "y", "zl", "zh"))
    shard = zh * 16 + y * 4 + x
    place = jnp.stack([core, x, y]).astype(jnp.int32)

    block = jnp.concatenate([jnp.transpose(w_qkv, (0, 2, 1)), w_out[None]], axis=0)
    piece_x = lax.dynamic_slice(block, (x, 0, 0), (1, 144, 1152))[:, :, :XW]
    piece_y = lax.dynamic_slice(block, (y, 0, 0), (1, 144, 1152))[:, :, XW:]
    gathered = []
    for piece, axis in ((piece_x, "x"), (piece_y, "y")):
        stacked = jnp.concatenate(
            [piece] + [ring_shift(piece, "zl", 4, k) for k in (1, 2, 3)], axis=0
        )
        gathered.append(gather_ring(stacked, axis))

    turned = jnp.transpose(patches, (0, 2, 1))
    mine = lax.all_to_all(turned, "zl", split_axis=0, concat_axis=0, tiled=True)
    other = swap_core(mine)
    mine, other = mine.reshape(4, 3, 144, 256), other.reshape(4, 3, 144, 256)

    all_ids = lax.all_gather(frame_ids, ("zh", "y", "x"), axis=0, tiled=True)
    wanted = shard * 12 + jnp.arange(12)
    source = jnp.sum(
        jnp.where(all_ids[None, :] == wanted[:, None], jnp.arange(384)[None, :] // 12, 0), axis=1
    ).astype(jnp.int32)

    own_rows = lax.dynamic_slice(w_conn, ((y * 4 + x) * 72, 0), (72, 512))
    full_rows = lax.all_gather(own_rows, ("zl", "c"), axis=1, tiled=True).astype(F32) * norm_gain
    high = full_rows.astype(BF16)
    low = (full_rows - high.astype(F32)).astype(BF16)
    both = jnp.concatenate([high, low], axis=0)
    products = [dot(both, w, 1, 0) for w in (w_x, w_b, w_c, w_dt)]
    product = jnp.concatenate([p[:72] + p[72:] for p in products], axis=1)
    product = jnp.pad(product, ((0, 0), (0, 120))).astype(BF16)
    wide = lax.all_gather(product, ("y", "x"), axis=0, tiled=True).T

    pool = (
        jnp.where(jnp.arange(256)[:, None] // POOL == jnp.arange(64)[None, :], 1.0 / POOL, 0.0)
    ).astype(BF16)
    own_frames = lax.dynamic_slice(grid_rows, (zl * 3,), (3,))
    keep, give = vision(
        place, own_frames, mine, other, ln_gain[:, None], pool, gathered[0], gathered[1]
    )
    summed = keep + swap_core(give)
    token = jnp.arange(128) % 64
    kept = token[None, :] * POOL < (own_frames * GRID)[:, None]
    seen = jnp.where(kept[None, :, None, :], summed, 0.0).astype(BF16)
    seen = lax.all_to_all(seen.reshape(12, 72, 128), "zl", split_axis=0, concat_axis=0, tiled=True)

    outgoing = bucket(frame_ids // 12, seen)
    incoming = lax.all_to_all(
        outgoing, ("zh", "y", "x"), split_axis=0, concat_axis=0, tiled=True
    )
    own_features = place_frames(source, incoming)
    line = lax.all_gather(own_features, "zl", axis=0)
    stream, features, squares = stream_rows(place, line, swap_core(line), w_conn)
    squares = lax.all_gather(squares, ("zl", "c"), axis=0)

    def column(values, repeat):
        return jnp.broadcast_to(values[:, None], (values.shape[0], repeat))

    inner, writers, readers, steps, logs, enter, payload = local_states(
        features, wide, squares, column(dt_bias, 128), column(a_log, 128)
    )
    local, begun = within(
        inner, writers, readers, steps, logs, enter, jnp.repeat(d_skip, HDIM)[:, None]
    )
    ahead_x, shrink_x, row = pass_along(payload, "x", 4)
    ahead_y, shrink_y, plane = pass_along(row, "y", 4)
    ahead_z = pass_along(plane, "zh", 2)[0]
    state = ahead_x + shrink_x * (ahead_y + shrink_y * ahead_z)
    mixed = finish(
        local, begun, readers, state.reshape(512, STATE).astype(BF16), out_gain[:, None]
    )
    return stream, mixed


def solution(mesh):
    fine = Mesh(mesh.devices.reshape(2, 4, 4, 4, 2), ("zh", "y", "x", "zl", "c"))
    tm, head = ("zh", "y", "x"), ("zl", "c")
    in_specs = (
        P(tm, None, head),
        P(tm),
        P(tm),
        P(),
        P(None, None, head),
        P(head, None),
        P(None, head),
        P(),
        P(None, head),
        P(None, head),
        P(None, head),
        P(None, head),
        P(head),
        P(head),
        P(head),
        P(head),
    )
    out_specs = (P(tm, head), P(tm, head))
    return jax.shard_map(
        on_device, mesh=fine, in_specs=in_specs, out_specs=out_specs, check_vma=False
    )
```

```python
import functools
import jax
import jax.numpy as jnp
from jax import lax
from jax.experimental import pallas as pl
from jax.experimental.pallas import tpu as pltpu
from jax.sharding import Mesh, PartitionSpec as P

GRID = 16
POOL = 4
VHD = 72
HDIM = 64
STATE = 128
Q = 256
XW = 640
LOW_ROWS = 80

F32 = jnp.float32
BF16 = jnp.bfloat16
highest = lax.Precision.HIGHEST
VMEM_SPEC = pl.BlockSpec(memory_space=pltpu.VMEM)
SMEM_SPEC = pl.BlockSpec(memory_space=pltpu.SMEM)
ANY_SPEC = pl.BlockSpec(memory_space=pl.ANY)


def params(mib):
    return pltpu.CompilerParams(vmem_limit_bytes=mib * 2**20)


def dot(a, b, ca, cb, precision=None):
    return lax.dot_general(
        a, b, (((ca,), (cb,)), ((), ())), preferred_element_type=F32, precision=precision
    )


def ring_shift(value, axis, size, shift):
    return lax.ppermute(value, axis, [(i, (i + shift) % size) for i in range(size)])


def swap_core(value):
    return lax.ppermute(value, "c", [(0, 1), (1, 0)])


def spread_out(parts, axis, size):
    position = lax.axis_index(axis)
    own = parts(position)
    return [own] + [
        ring_shift(parts(lax.rem(position + k, size)), axis, size, k) for k in range(1, size)
    ]


def gather_ring(block, axis):
    before = ring_shift(block, axis, 4, 1)
    after = ring_shift(block, axis, 4, -1)
    far_lo = ring_shift(before[:, :LOW_ROWS], axis, 4, 1)
    far_hi = ring_shift(after[:, LOW_ROWS:], axis, 4, -1)
    return (block, before, far_lo, far_hi, after)


def norm_kernel(place, own, other, gain, pool, normed, residual, x):
    core, line = place[0], place[3]
    for f in range(3):
        for k in range(4):
            z = lax.rem(line + 4 - k, 4)
            for source, c in ((own, core), (other, 1 - core)):
                rows = pl.ds(pl.multiple_of((2 * z + c) * 144, 144), 144)
                x[rows, :] = source[k, f].astype(F32)
            pooled = dot(own[k, f], pool[...], 1, 0)
            residual[z, f] = jnp.concatenate([pooled[:72], pooled[72:]], axis=1)
        values = x[...]
        width = values.shape[0]
        centre = jnp.sum(values, axis=0, keepdims=True) * (1.0 / width)
        values = values - centre
        spread = jnp.sum(values * values, axis=0, keepdims=True) * (1.0 / width)
        normed[f] = (values * lax.rsqrt(spread + 1e-06) * gain[...]).astype(BF16)


def norm_frames(place, own, other, ln_gain, pool):
    return pl.pallas_call(
        norm_kernel,
        in_specs=[SMEM_SPEC] + [VMEM_SPEC] * 4,
        out_specs=(VMEM_SPEC, VMEM_SPEC),
        out_shape=(
            jax.ShapeDtypeStruct((3, 1152, 256), BF16),
            jax.ShapeDtypeStruct((4, 3, 72, 128), F32),
        ),
        scratch_shapes=[pltpu.VMEM((1152, 256), F32)],
        compiler_params=params(24),
        name="norm",
    )(place, own, other, ln_gain, pool)


def vision_kernel(place, rows, normed, pool, block, *rest):
    weights = rest[:10]
    keep, give, wx, wy, qkv, ctx, sems = rest[10:]
    frame = pl.program_id(0)
    first = place[0] == 0

    def copies():
        made = [
            pltpu.make_async_copy(block.at[:, :, pl.ds(0, XW)], wx.at[:, 0], sems.at[10]),
            pltpu.make_async_copy(block.at[:, :, pl.ds(XW, 1152 - XW)], wy.at[:, 0], sems.at[11]),
        ]
        for member, (held, slot) in enumerate(((wx, 1), (wy, 2))):
            own, before, far_lo, far_hi, after = weights[5 * member : 5 * member + 5]
            for k, (source, lo, size) in enumerate(
                (
                    (own, 0, 144),
                    (before, 0, 144),
                    (far_lo, 0, LOW_ROWS),
                    (far_hi, LOW_ROWS, 144 - LOW_ROWS),
                    (after, 0, 144),
                )
            ):
                distance = (0, 1, 2, 2, 3)[k]
                index = lax.rem(place[slot] + 4 - distance, 4)
                made.append(
                    pltpu.make_async_copy(
                        source,
                        held.at[index, pl.ds(1, 3), pl.ds(lo, size)],
                        sems.at[5 * member + k],
                    )
                )
        return made

    @pl.when(frame == 0)
    def _():
        for copy in copies():
            copy.start()
        for copy in copies():
            copy.wait()

    width = normed.shape[1]
    for m in range(3):
        left = wx[m].reshape(576, XW)
        right = wy[m].reshape(576, width - XW)
        qkv[m] = dot(left, normed[0, :XW], 1, 0) + dot(right, normed[0, XW:], 1, 0)
    valid = rows[frame] * GRID
    usable = lax.broadcasted_iota(jnp.int32, (256, 256), 0) < valid
    for h in range(8):
        span = pl.ds(h * VHD, VHD)
        q, k, v = (qkv[m, span, :].astype(BF16) for m in range(3))
        scores = dot(k, q, 0, 0) * VHD ** (-0.5)
        scores = jnp.where(usable, scores, -1e30)
        top = jnp.max(scores, axis=0, keepdims=True)
        powered = jnp.exp(scores - top)
        total = jnp.sum(powered, axis=0, keepdims=True)
        ctx[span, :] = dot(v, powered.astype(BF16), 1, 0) * (1.0 / total)
    pooled = dot(ctx[...].astype(BF16), pool[...], 1, 0)
    high = pooled.astype(BF16)
    low = (pooled - high.astype(F32)).astype(BF16)
    both = jnp.concatenate([high, low], axis=1)
    out_x = dot(both, wx[3].reshape(576, XW), 0, 0)
    out_y = dot(both, wy[3].reshape(576, width - XW), 0, 0)
    attended = jnp.concatenate([out_x, out_y], axis=1)
    attended = (attended[:64] + attended[64:]).T
    for z in range(4):
        a = attended[(2 * z) * 144 : (2 * z + 1) * 144]
        b = attended[(2 * z + 1) * 144 : (2 * z + 2) * 144]
        own = jnp.where(first, a, b)
        far = jnp.where(first, b, a)
        keep[z, 0] = jnp.concatenate([own[:72], own[72:]], axis=1)
        give[z, 0] = jnp.concatenate([far[:72], far[72:]], axis=1)


def vision(place, rows, normed, pool, block, wx, wy):
    out = pl.BlockSpec((4, 1, 72, 128), lambda f: (0, f, 0, 0))
    shape = jax.ShapeDtypeStruct((4, 3, 72, 128), F32)
    return pl.pallas_call(
        vision_kernel,
        grid=(3,),
        in_specs=[
            SMEM_SPEC,
            SMEM_SPEC,
            pl.BlockSpec((1, 1152, 256), lambda f: (f, 0, 0)),
            VMEM_SPEC,
        ]
        + [ANY_SPEC] * 11,
        out_specs=(out, out),
        out_shape=(shape, shape),
        scratch_shapes=[
            pltpu.VMEM((4, 4, 144, XW), BF16),
            pltpu.VMEM((4, 4, 144, 1152 - XW), BF16),
            pltpu.VMEM((3, 576, 256), F32),
            pltpu.VMEM((576, 256), F32),
            pltpu.SemaphoreType.DMA((12,)),
        ],
        compiler_params=params(40),
        name="vision",
    )(place, rows, normed, pool, block, *wx, *wy)


def bucket_kernel(place, target, *refs):
    out = refs[4]
    out[...] = jnp.zeros_like(out)
    for k in range(4):
        z = lax.rem(place[3] + 4 - k, 4)
        for j in range(3):
            out[target[3 * z + j]] = refs[k][j]


def bucket(place, target, seen):
    return pl.pallas_call(
        bucket_kernel,
        in_specs=[SMEM_SPEC, SMEM_SPEC] + [VMEM_SPEC] * 4,
        out_specs=VMEM_SPEC,
        out_shape=jax.ShapeDtypeStruct((32, 72, 128), BF16),
        compiler_params=params(16),
        name="bucket",
    )(place, target, *seen)


def place_kernel(source, incoming, out):
    left = lax.broadcasted_iota(jnp.int32, (72, 128), 1) < 64
    for pair in range(6):
        a = incoming[source[2 * pair]].astype(F32)
        b = incoming[source[2 * pair + 1]].astype(F32)
        lanes = pl.ds(128 * pair, 128)
        top = jnp.where(left, a, pltpu.roll(b, 64, 1))
        bottom = jnp.where(left, pltpu.roll(a, 64, 1), b)
        out[:, lanes] = jnp.concatenate([top, bottom], axis=0).astype(BF16)


def place_frames(source, incoming):
    return pl.pallas_call(
        place_kernel,
        in_specs=[SMEM_SPEC, VMEM_SPEC],
        out_specs=VMEM_SPEC,
        out_shape=jax.ShapeDtypeStruct((144, 768), BF16),
        compiler_params=params(16),
        name="place",
    )(source, incoming)


def stream_kernel(place, mine, other, w_conn, stream, seen, squares):
    first = place[0] == 0
    for z in range(4):
        a, b = mine[pl.ds(144 * z, 144), :], other[pl.ds(144 * z, 144), :]
        seen[pl.ds(288 * z, 144), :] = jnp.where(first, a, b)
        seen[pl.ds(288 * z + 144, 144), :] = jnp.where(first, b, a)
    made = dot(w_conn[...], seen[...], 0, 0).astype(BF16)
    wide = made.astype(F32)
    squares[...] = jnp.broadcast_to(
        jnp.sum(wide * wide, axis=0, keepdims=True), squares.shape
    )
    stream[...] = wide.T.astype(BF16)


def stream_rows(place, mine, other, w_conn):
    tokens, width = mine.shape[1], w_conn.shape[1]
    return pl.pallas_call(
        stream_kernel,
        in_specs=[SMEM_SPEC, VMEM_SPEC, VMEM_SPEC, VMEM_SPEC],
        out_specs=(VMEM_SPEC, VMEM_SPEC, VMEM_SPEC),
        out_shape=(
            jax.ShapeDtypeStruct((tokens, width), BF16),
            jax.ShapeDtypeStruct((1152, tokens), BF16),
            jax.ShapeDtypeStruct((8, tokens), F32),
        ),
        compiler_params=params(40),
        name="stream",
    )(place, mine, other, w_conn)


def over_heads(rows, length):
    return jnp.concatenate(
        [jnp.broadcast_to(rows[h : h + 1], (HDIM, length)) for h in range(8)], axis=0
    )


def triangle(transposed):
    a = lax.broadcasted_iota(jnp.int32, (Q, Q), 0)
    b = lax.broadcasted_iota(jnp.int32, (Q, Q), 1)
    return jnp.where(a >= b if transposed else a <= b, 1.0, 0.0).astype(F32)


def raw_kernel(seen, wide, out):
    out[...] = dot(wide[pl.ds(0, 776), :], seen[...], 1, 0)


def raw_rows(seen, wide):
    return pl.pallas_call(
        raw_kernel,
        in_specs=[VMEM_SPEC] * 2,
        out_specs=VMEM_SPEC,
        out_shape=jax.ShapeDtypeStruct((776, seen.shape[1]), F32),
        compiler_params=params(24),
        cost_estimate=pl.CostEstimate(
            flops=2_500_000_000, bytes_accessed=8_000_000, transcendentals=0
        ),
        name="raw",
    )(seen, wide)


def state_kernel(
    raw, squares, bias, a_log, inner, writers, readers, steps, logs, enter, payload
):
    scale = lax.rsqrt(squares[0:1, :] * (1.0 / 4096) + 1e-05)
    inner[...] = (raw[:512] * scale).astype(BF16)
    writers[...] = (raw[512:640] * scale).astype(BF16)
    readers[...] = (raw[640:768] * scale).astype(BF16)
    before = raw[768:776] * scale + bias[:, :1]
    step = jnp.maximum(before, 0.0) + jnp.log1p(jnp.exp(-jnp.abs(before)))
    log = -jnp.exp(a_log[:, :1]) * step
    steps[...] = step
    logs[...] = log
    upper = triangle(False)
    count = raw.shape[1] // Q
    state = jnp.zeros((512, STATE), F32)
    whole = jnp.zeros((8, 1), F32)
    for n in range(count):
        lanes = slice(n * Q, (n + 1) * Q)
        cumul = dot(log[:, lanes], upper, 1, 0, highest)
        total = cumul[:, Q - 1 : Q]
        enter[n] = state.astype(BF16)
        left = over_heads(step[:, lanes] * jnp.exp(total - cumul), Q)
        scaled = (inner[:, lanes].astype(F32) * left).astype(BF16)
        fresh = dot(scaled, writers[:, lanes], 1, 1)
        state = state * over_heads(jnp.broadcast_to(jnp.exp(total), (8, STATE)), STATE) + fresh
        whole = whole + total
    for part in range(4):
        payload[part, pl.ds(0, 128), :] = state[128 * part : 128 * (part + 1)]
        for j in range(2):
            row = 2 * part + j
            payload[part, pl.ds(128 + 8 * j, 8), :] = jnp.broadcast_to(
                jnp.exp(whole[row : row + 1]), (8, STATE)
            )


def local_states(raw, squares, bias, a_log):
    tokens = raw.shape[1]
    return pl.pallas_call(
        state_kernel,
        in_specs=[VMEM_SPEC] * 4,
        out_specs=(VMEM_SPEC,) * 7,
        out_shape=(
            jax.ShapeDtypeStruct((512, tokens), BF16),
            jax.ShapeDtypeStruct((STATE, tokens), BF16),
            jax.ShapeDtypeStruct((STATE, tokens), BF16),
            jax.ShapeDtypeStruct((8, tokens), F32),
            jax.ShapeDtypeStruct((8, tokens), F32),
            jax.ShapeDtypeStruct((tokens // Q, 512, STATE), BF16),
            jax.ShapeDtypeStruct((4, 144, STATE), F32),
        ),
        compiler_params=params(40),
        name="states",
    )(raw, squares, bias, a_log)


def within_kernel(inner, writers, readers, steps, logs, enter, d_skip, out, begun):
    upper, lower = triangle(False), triangle(True)
    causal = upper > 0.0
    whole = jnp.zeros((8, 1), F32)
    for n in range(inner.shape[1] // Q):
        lanes = slice(n * Q, (n + 1) * Q)
        log = logs[:, lanes]
        cumul = dot(log, upper, 1, 0, highest)
        column = dot(lower, log, 1, 1, highest)
        begun[:, lanes] = cumul + whole
        whole = whole + cumul[:, Q - 1 : Q]
        meets = dot(writers[:, lanes], readers[:, lanes], 0, 0)
        carried = dot(enter[n], readers[:, lanes], 1, 0)
        grown = jnp.exp(cumul)
        step = steps[:, lanes]
        for h in range(8):
            span = slice(h * HDIM, (h + 1) * HDIM)
            apart = jnp.minimum(cumul[h : h + 1] - column[:, h : h + 1], 0.0)
            mixing = jnp.where(causal, meets * jnp.exp(apart), 0.0).astype(BF16)
            own = inner[span, lanes].astype(F32)
            scaled = (own * step[h : h + 1]).astype(BF16)
            out[span, lanes] = (
                dot(scaled, mixing, 1, 0)
                + carried[span] * grown[h : h + 1]
                + d_skip[span] * own
            )


def within(inner, writers, readers, steps, logs, enter, d_skip):
    tokens = inner.shape[1]
    return pl.pallas_call(
        within_kernel,
        in_specs=[VMEM_SPEC] * 7,
        out_specs=(VMEM_SPEC,) * 2,
        out_shape=(
            jax.ShapeDtypeStruct((512, tokens), F32),
            jax.ShapeDtypeStruct((8, tokens), F32),
        ),
        compiler_params=params(40),
        cost_estimate=pl.CostEstimate(
            flops=2_000_000_000, bytes_accessed=6_000_000, transcendentals=2_000_000
        ),
        name="within",
    )(inner, writers, readers, steps, logs, enter, d_skip)


def finish_kernel(place, local, begun, readers, *refs):
    gain, out, state = refs[4:]
    for k in range(4):
        rows = pl.ds(pl.multiple_of(lax.rem(place[1] + 4 - k, 4) * 128, 128), 128)
        state[rows, :] = refs[k][...]
    for n in range(local.shape[1] // Q):
        lanes = slice(n * Q, (n + 1) * Q)
        carried = dot(state[...], readers[:, lanes], 1, 0)
        y = local[:, lanes] + carried * over_heads(jnp.exp(begun[:, lanes]), Q)
        mean = jnp.sum(y * y, axis=0, keepdims=True) * (1.0 / 512)
        y = y * lax.rsqrt(mean + 1e-05) * gain[...]
        out[lanes, :] = y.T.astype(BF16)


def finish(place, local, begun, readers, states, gain):
    return pl.pallas_call(
        finish_kernel,
        in_specs=[SMEM_SPEC] + [VMEM_SPEC] * 8,
        out_specs=VMEM_SPEC,
        out_shape=jax.ShapeDtypeStruct((local.shape[1], 512), BF16),
        scratch_shapes=[pltpu.VMEM((512, STATE), BF16)],
        compiler_params=params(24),
        name="finish",
    )(place, local, begun, readers, *states, gain)


def two_heads(decays):
    return jnp.concatenate(
        [jnp.broadcast_to(decays[8 * j : 8 * j + 1], (HDIM, STATE)) for j in range(2)], axis=0
    )


def prefix_kernel(size, slot, place, *refs):
    got, (before, total, held) = refs[:size], refs[size:]
    for k in range(size):
        held[lax.rem(place[slot] + size - k, size)] = got[k][...].astype(F32)
    state, decay = jnp.zeros((128, STATE), F32), jnp.ones((16, STATE), F32)
    for i in range(size):
        before[i, pl.ds(0, 128), :] = state
        before[i, pl.ds(128, 16), :] = decay
        left = held[i, pl.ds(128, 16), :]
        state = state * two_heads(left) + held[i, pl.ds(0, 128), :]
        decay = decay * left
    total[...] = jnp.concatenate([state, decay], axis=0).astype(BF16)


def prefix(place, slot, got):
    size = len(got)
    return pl.pallas_call(
        functools.partial(prefix_kernel, size, slot),
        in_specs=[SMEM_SPEC] + [VMEM_SPEC] * size,
        out_specs=(VMEM_SPEC, VMEM_SPEC),
        out_shape=(
            jax.ShapeDtypeStruct((size, 144, STATE), F32),
            jax.ShapeDtypeStruct((144, STATE), BF16),
        ),
        scratch_shapes=[pltpu.VMEM((size, 144, STATE), F32)],
        compiler_params=params(16),
        name="prefix",
    )(place, *got)


def join_kernel(place, in_row, in_plane, plane, out):
    y = place[2]
    later = place[4] > 0
    begun = jnp.where(later, plane[pl.ds(0, 128), :].astype(F32), 0.0)
    begun = in_plane[y, pl.ds(0, 128), :] + two_heads(in_plane[y, pl.ds(128, 16), :]) * begun
    for i in range(4):
        made = in_row[i, pl.ds(0, 128), :] + two_heads(in_row[i, pl.ds(128, 16), :]) * begun
        out[i] = made.astype(BF16)


def join(place, in_row, in_plane, plane):
    return pl.pallas_call(
        join_kernel,
        in_specs=[SMEM_SPEC] + [VMEM_SPEC] * 3,
        out_specs=VMEM_SPEC,
        out_shape=jax.ShapeDtypeStruct((4, 128, STATE), BF16),
        compiler_params=params(16),
        name="join",
    )(place, in_row, in_plane, plane)


def on_device(
    patches, grid_rows, frame_ids, ln_gain, w_qkv, w_out, w_conn, norm_gain,
    w_x, w_b, w_c, w_dt, dt_bias, a_log, d_skip, out_gain,
):
    core, x, y, zl, zh = (lax.axis_index(a) for a in ("c", "x", "y", "zl", "zh"))
    shard = zh * 16 + y * 4 + x
    place = jnp.stack([core, x, y, zl, zh]).astype(jnp.int32)
    pool = (
        jnp.where(jnp.arange(256)[:, None] // POOL == jnp.arange(64)[None, :], 1.0 / POOL, 0.0)
    ).astype(BF16)

    block = jnp.concatenate([jnp.transpose(w_qkv, (0, 2, 1)), w_out[None]], axis=0)
    piece = jnp.concatenate(
        [
            lax.dynamic_slice(block, (x, 0, 0), (1, 144, XW)),
            lax.dynamic_slice(block, (y, 0, XW), (1, 144, 1152 - XW)),
        ],
        axis=2,
    )
    along = [ring_shift(piece, "zl", 4, k) for k in (1, 2, 3)]
    ring_x = gather_ring(jnp.concatenate([p[:, :, :XW] for p in along], axis=0), "x")
    ring_y = gather_ring(jnp.concatenate([p[:, :, XW:] for p in along], axis=0), "y")

    turned = jnp.transpose(patches, (0, 2, 1))
    turned, _ = lax.optimization_barrier((turned, along))
    own = spread_out(lambda i: lax.dynamic_slice(turned, (3 * i, 0, 0), (3, 144, 256)), "zl", 4)
    own = jnp.stack(own)
    normed, residual = norm_frames(place, own, swap_core(own), ln_gain[:, None], pool)

    ids = frame_ids[None]
    for axis, size in (("x", 4), ("y", 4), ("zh", 2)):
        ids = jnp.concatenate([ids] + [ring_shift(ids, axis, size, k) for k in range(1, size)], axis=0)
    away = jnp.arange(32)
    holder = (
        lax.rem(zh + 2 - away // 16, 2) * 16
        + lax.rem(y + 4 - away // 4 % 4, 4) * 4
        + lax.rem(x + 4 - away % 4, 4)
    )
    wanted = shard * 12 + jnp.arange(12)
    source = jnp.sum(
        jnp.where(ids[None] == wanted[:, None, None], holder[None, :, None], 0), axis=(1, 2)
    ).astype(jnp.int32)

    some = lax.dynamic_slice(w_conn, ((y * 4 + x) * 72, 0), (72, 512))
    some, _ = lax.optimization_barrier((some, own))
    some = jnp.stack([some] + [ring_shift(some, "zl", 4, k) for k in (1, 2, 3)])
    far = swap_core(some)
    columns = []
    for z in range(4):
        which = lax.rem(zl + 4 - z, 4)
        a, b = (lax.dynamic_index_in_dim(part, which, 0, False) for part in (some, far))
        columns += [jnp.where(core == 0, a, b), jnp.where(core == 0, b, a)]
    full_rows = jnp.concatenate(columns, axis=1).astype(F32) * norm_gain
    high = full_rows.astype(BF16)
    low = (full_rows - high.astype(F32)).astype(BF16)
    both = jnp.concatenate([high, low], axis=0)
    products = [dot(both, w, 1, 0) for w in (w_x, w_b, w_c, w_dt)]
    product = jnp.concatenate([p[:72] + p[72:] for p in products], axis=1)
    product = jnp.pad(product, ((0, 0), (0, 120))).astype(BF16)
    product, _ = lax.optimization_barrier((product, (ring_x, ring_y)))
    wide = lax.all_gather(product, ("y", "x"), axis=0, tiled=True).T

    own_frames = lax.dynamic_slice(grid_rows, (zl * 3,), (3,))
    keep, give = vision(place, own_frames, normed, pool, block, ring_x, ring_y)
    summed = keep + residual + swap_core(give)
    token = jnp.arange(128) % 64
    kept = token[None, :] * POOL < (own_frames * GRID)[:, None]
    seen = jnp.where(kept[None, :, None, :], summed, 0.0).astype(BF16)
    seen = spread_out(lambda i: lax.dynamic_index_in_dim(seen, i, 0, False), "zl", 4)

    outgoing = bucket(place, frame_ids // 12, seen)
    incoming = lax.all_to_all(
        outgoing, ("zh", "y", "x"), split_axis=0, concat_axis=0, tiled=True
    )
    own_features = place_frames(source, incoming)
    line = lax.all_gather(own_features, "zl", axis=0, tiled=True)
    stream, features, squares = stream_rows(place, line, swap_core(line), w_conn)
    squares = squares + swap_core(squares)
    squares = squares + sum(ring_shift(squares, "zl", 4, k) for k in (1, 2, 3))

    def column(values, repeat):
        return jnp.broadcast_to(values[:, None], (values.shape[0], repeat))

    raw = raw_rows(features, wide)
    inner, writers, readers, steps, logs, enter, payload = local_states(
        raw, squares, column(dt_bias, 128), column(a_log, 128)
    )
    local, begun = within(
        inner, writers, readers, steps, logs, enter, jnp.repeat(d_skip, HDIM)[:, None]
    )
    sent = payload.astype(BF16)
    in_row, row = prefix(
        place, 1, spread_out(lambda i: lax.dynamic_index_in_dim(sent, i, 0, False), "x", 4)
    )
    in_plane, plane = prefix(place, 2, spread_out(lambda i: row, "y", 4))
    states = join(place, in_row, in_plane, ring_shift(plane, "zh", 2, 1))
    states = spread_out(lambda i: lax.dynamic_index_in_dim(states, i, 0, False), "x", 4)
    mixed = finish(place, local, begun, readers, states, out_gain[:, None])
    return stream, mixed


def solution(mesh):
    fine = Mesh(mesh.devices.reshape(2, 4, 4, 4, 2), ("zh", "y", "x", "zl", "c"))
    tm, head = ("zh", "y", "x"), ("zl", "c")
    in_specs = (
        P(tm, None, head),
        P(tm),
        P(tm),
        P(),
        P(None, None, head),
        P(head, None),
        P(None, head),
        P(),
        P(None, head),
        P(None, head),
        P(None, head),
        P(None, head),
        P(head),
        P(head),
        P(head),
        P(head),
    )
    out_specs = (P(tm, head), P(tm, head))
    return jax.shard_map(
        on_device, mesh=fine, in_specs=in_specs, out_specs=out_specs, check_vma=False
    )
```

```python
import functools
import jax
import jax.numpy as jnp
from jax import lax
from jax.experimental import pallas as pl
from jax.experimental.pallas import tpu as pltpu
from jax.sharding import Mesh, PartitionSpec as P

GRID = 16
POOL = 4
VHD = 72
HDIM = 64
STATE = 128
Q = 256
XW = 512
LOW = 5

F32 = jnp.float32
BF16 = jnp.bfloat16
highest = lax.Precision.HIGHEST
VMEM_SPEC = pl.BlockSpec(memory_space=pltpu.VMEM)
SMEM_SPEC = pl.BlockSpec(memory_space=pltpu.SMEM)
ANY_SPEC = pl.BlockSpec(memory_space=pl.ANY)


def params(mib):
    return pltpu.CompilerParams(vmem_limit_bytes=mib * 2**20)


def dot(a, b, ca, cb, precision=None):
    return lax.dot_general(
        a, b, (((ca,), (cb,)), ((), ())), preferred_element_type=F32, precision=precision
    )


def ring_shift(value, axis, size, shift):
    return lax.ppermute(value, axis, [(i, (i + shift) % size) for i in range(size)])


def swap_core(value):
    return lax.ppermute(value, "c", [(0, 1), (1, 0)])


def spread_out(parts, axis, size):
    position = lax.axis_index(axis)
    own = parts(position)
    return [own] + [
        ring_shift(parts(lax.rem(position + k, size)), axis, size, k) for k in range(1, size)
    ]


def gather_ring(block, axis, later):
    before = ring_shift(block, axis, 4, 1)
    after = ring_shift(block, axis, 4, -1)
    low, high, later = lax.optimization_barrier((before[:LOW], after[LOW:], later))
    far_lo = ring_shift(low, axis, 4, 1)
    far_hi = ring_shift(high, axis, 4, -1)
    return (block, before, far_lo, far_hi, after), later


def split_kernel(a, b, c, left, right):
    for k, source in enumerate((a, b, c)):
        for third in range(3):
            rows = source[pl.ds(48 * third, 48), :]
            left[3 * k + third] = rows[:, :XW]
            right[3 * k + third] = rows[:, XW:]


def split_pieces(pieces):
    return pl.pallas_call(
        split_kernel,
        in_specs=[VMEM_SPEC] * 3,
        out_specs=(VMEM_SPEC, VMEM_SPEC),
        out_shape=(
            jax.ShapeDtypeStruct((9, 48, XW), BF16),
            jax.ShapeDtypeStruct((9, 48, 1152 - XW), BF16),
        ),
        compiler_params=params(8),
        name="split",
    )(*pieces)


def norm_kernel(place, own, other, gain, pool, normed, residual, x):
    first = place[0] == 0
    for f in range(3):
        frame = pl.ds(144 * f, 144)
        for z in range(4):
            k = lax.rem(place[3] + 4 - z, 4)
            mine = own[k, frame, :]
            a, b = mine.astype(F32), other[k, frame, :].astype(F32)
            x[pl.ds(288 * z, 144), :] = jnp.where(first, a, b)
            x[pl.ds(288 * z + 144, 144), :] = jnp.where(first, b, a)
            pooled = dot(mine, pool[...], 1, 0)
            residual[z, f] = jnp.concatenate([pooled[:72], pooled[72:]], axis=1)
        values = x[...]
        width = values.shape[0]
        centre = jnp.sum(values, axis=0, keepdims=True) * (1.0 / width)
        values = values - centre
        spread = jnp.sum(values * values, axis=0, keepdims=True) * (1.0 / width)
        normed[f] = (values * lax.rsqrt(spread + 1e-06) * gain[...]).astype(BF16)


def norm_frames(place, own, other, ln_gain, pool):
    return pl.pallas_call(
        norm_kernel,
        in_specs=[SMEM_SPEC] + [VMEM_SPEC] * 4,
        out_specs=(VMEM_SPEC, VMEM_SPEC),
        out_shape=(
            jax.ShapeDtypeStruct((3, 1152, 256), BF16),
            jax.ShapeDtypeStruct((4, 3, 72, 128), F32),
        ),
        scratch_shapes=[pltpu.VMEM((1152, 256), F32)],
        compiler_params=params(16),
        cost_estimate=pl.CostEstimate(
            flops=1_000_000, bytes_accessed=100_000, transcendentals=0
        ),
        name="norm",
    )(place, own, other, ln_gain, pool)


def vision_kernel(place, rows, normed, pool, block, *rest):
    whole, *ring = rest[:6]
    keep, give, wx, wy, qkv, ctx, sems = rest[6:]
    frame = pl.program_id(0)
    first = place[0] == 0

    def copies():
        pairs = [
            (block.at[:, :, :, pl.ds(0, XW)], wx.at[:, pl.ds(0, 3)]),
            (block.at[:, :, :, pl.ds(XW, 1152 - XW)], wy.at[:, pl.ds(0, 3)]),
            (whole, wx.at[:, pl.ds(3, 9)]),
        ]
        for source, distance, lo, size in zip(
            ring, (0, 1, 2, 2, 3), (0, 0, 0, LOW, 0), (9, 9, LOW, 9 - LOW, 9)
        ):
            index = lax.rem(place[2] + 4 - distance, 4)
            pairs.append((source, wy.at[index, pl.ds(3 + lo, size)]))
        return [
            pltpu.make_async_copy(source, held, sems.at[n])
            for n, (source, held) in enumerate(pairs)
        ]

    @pl.when(frame == 0)
    def _():
        for copy in copies():
            copy.start()
        for copy in copies():
            copy.wait()

    width = normed.shape[1]
    for m in range(3):
        left = wx[m].reshape(576, XW)
        right = wy[m].reshape(576, width - XW)
        qkv[m] = dot(left, normed[0, :XW], 1, 0) + dot(right, normed[0, XW:], 1, 0)
    valid = rows[frame] * GRID
    usable = lax.broadcasted_iota(jnp.int32, (256, 256), 0) < valid
    for h in range(8):
        span = pl.ds(h * VHD, VHD)
        q, k, v = (qkv[m, span, :].astype(BF16) for m in range(3))
        scores = dot(k, q, 0, 0) * VHD ** (-0.5)
        scores = jnp.where(usable, scores, -1e30)
        top = jnp.max(scores, axis=0, keepdims=True)
        powered = jnp.exp(scores - top)
        total = jnp.sum(powered, axis=0, keepdims=True)
        ctx[span, :] = dot(v, powered.astype(BF16), 1, 0) * (1.0 / total)
    pooled = dot(ctx[...].astype(BF16), pool[...], 1, 0)
    high = pooled.astype(BF16)
    low = (pooled - high.astype(F32)).astype(BF16)
    both = jnp.concatenate([high, low], axis=1)
    out_x = dot(both, wx[3].reshape(576, XW), 0, 0)
    out_y = dot(both, wy[3].reshape(576, width - XW), 0, 0)
    attended = jnp.concatenate([out_x, out_y], axis=1)
    attended = (attended[:64] + attended[64:]).T
    for z in range(4):
        a = attended[(2 * z) * 144 : (2 * z + 1) * 144]
        b = attended[(2 * z + 1) * 144 : (2 * z + 2) * 144]
        own = jnp.where(first, a, b)
        far = jnp.where(first, b, a)
        keep[z, 0] = jnp.concatenate([own[:72], own[72:]], axis=1)
        give[z, 0] = jnp.concatenate([far[:72], far[72:]], axis=1)


def vision(place, rows, normed, pool, block, whole, ring):
    out = pl.BlockSpec((4, 1, 72, 128), lambda f: (0, f, 0, 0))
    shape = jax.ShapeDtypeStruct((4, 3, 72, 128), F32)
    return pl.pallas_call(
        vision_kernel,
        grid=(3,),
        in_specs=[
            SMEM_SPEC,
            SMEM_SPEC,
            pl.BlockSpec((1, 1152, 256), lambda f: (f, 0, 0)),
            VMEM_SPEC,
        ]
        + [ANY_SPEC] * 7,
        out_specs=(out, out),
        out_shape=(shape, shape),
        scratch_shapes=[
            pltpu.VMEM((4, 12, 48, XW), BF16),
            pltpu.VMEM((4, 12, 48, 1152 - XW), BF16),
            pltpu.VMEM((3, 576, 256), F32),
            pltpu.VMEM((576, 256), F32),
            pltpu.SemaphoreType.DMA((8,)),
        ],
        compiler_params=params(56),
        name="vision",
    )(place, rows, normed, pool, block, whole, *ring)


def bucket_kernel(place, target, *refs):
    out = refs[4]
    out[...] = jnp.zeros_like(out)
    for k in range(4):
        z = lax.rem(place[3] + 4 - k, 4)
        for j in range(3):
            out[target[3 * z + j]] = refs[k][j]


def bucket(place, target, seen):
    return pl.pallas_call(
        bucket_kernel,
        in_specs=[SMEM_SPEC, SMEM_SPEC] + [VMEM_SPEC] * 4,
        out_specs=VMEM_SPEC,
        out_shape=jax.ShapeDtypeStruct((32, 72, 128), BF16),
        compiler_params=params(16),
        name="bucket",
    )(place, target, *seen)


def place_kernel(source, incoming, out):
    left = lax.broadcasted_iota(jnp.int32, (72, 128), 1) < 64
    for pair in range(6):
        a = incoming[source[2 * pair]].astype(F32)
        b = incoming[source[2 * pair + 1]].astype(F32)
        lanes = pl.ds(128 * pair, 128)
        top = jnp.where(left, a, pltpu.roll(b, 64, 1))
        bottom = jnp.where(left, pltpu.roll(a, 64, 1), b)
        out[:, lanes] = jnp.concatenate([top, bottom], axis=0).astype(BF16)


def place_frames(source, incoming):
    return pl.pallas_call(
        place_kernel,
        in_specs=[SMEM_SPEC, VMEM_SPEC],
        out_specs=VMEM_SPEC,
        out_shape=jax.ShapeDtypeStruct((144, 768), BF16),
        compiler_params=params(16),
        name="place",
    )(source, incoming)


def product_kernel(place, own, other, gain, w_x, w_b, w_c, w_dt, out, total):
    i = pl.program_id(0)

    @pl.when(i == 0)
    def _():
        total[...] = jnp.zeros_like(total)

    k = lax.rem(place[3] + 4 - i // 2, 4)
    a, b = own[k].astype(F32), other[k].astype(F32)
    part = jnp.where(lax.rem(i, 2) == place[0], a, b)
    part = jnp.concatenate([part[:72], part[72:]], axis=1) * gain[...]
    high = part.astype(BF16).astype(F32)
    both = jnp.concatenate([high, part - high], axis=0).astype(BF16)
    begun = 0
    for w in (w_x, w_b, w_c, w_dt):
        span = pl.ds(begun, w.shape[1])
        total[:, span] += dot(both, w[...], 1, 0)
        begun += w.shape[1]

    @pl.when(i == 7)
    def _():
        out[...] = (total[pl.ds(0, 72), :] + total[pl.ds(72, 72), :]).astype(BF16)


def weight_product(place, own, other, gain, w_x, w_b, w_c, w_dt):
    some = pl.BlockSpec((4, 144, 256), lambda i: (0, 3, 0))
    return pl.pallas_call(
        product_kernel,
        grid=(8,),
        in_specs=[SMEM_SPEC, some, some, pl.BlockSpec((1, 512), lambda i: (0, i))]
        + [pl.BlockSpec((512, w.shape[1]), lambda i: (i, 0)) for w in (w_x, w_b, w_c, w_dt)],
        out_specs=pl.BlockSpec((72, 896), lambda i: (0, 0)),
        out_shape=jax.ShapeDtypeStruct((72, 896), BF16),
        scratch_shapes=[pltpu.VMEM((144, 896), F32)],
        compiler_params=params(56),
        cost_estimate=pl.CostEstimate(flops=1_000_000, bytes_accessed=100_000, transcendentals=0),
        name="product",
    )(place, own, other, gain, w_x, w_b, w_c, w_dt)


def stream_kernel(place, mine, other, w_conn, stream, seen, squares):
    first = place[0] == 0
    for z in range(4):
        a, b = mine[pl.ds(144 * z, 144), :], other[pl.ds(144 * z, 144), :]
        seen[pl.ds(288 * z, 144), :] = jnp.where(first, a, b)
        seen[pl.ds(288 * z + 144, 144), :] = jnp.where(first, b, a)
    made = dot(w_conn[...], seen[...], 0, 0).astype(BF16)
    wide = made.astype(F32)
    squares[...] = jnp.broadcast_to(
        jnp.sum(wide * wide, axis=0, keepdims=True), squares.shape
    )
    stream[...] = wide.T.astype(BF16)


def stream_rows(place, mine, other, w_conn):
    tokens, width = mine.shape[1], w_conn.shape[1]
    return pl.pallas_call(
        stream_kernel,
        in_specs=[SMEM_SPEC, VMEM_SPEC, VMEM_SPEC, VMEM_SPEC],
        out_specs=(VMEM_SPEC, VMEM_SPEC, VMEM_SPEC),
        out_shape=(
            jax.ShapeDtypeStruct((tokens, width), BF16),
            jax.ShapeDtypeStruct((1152, tokens), BF16),
            jax.ShapeDtypeStruct((8, tokens), F32),
        ),
        compiler_params=params(16),
        name="stream",
    )(place, mine, other, w_conn)


def over_heads(rows, length):
    return jnp.concatenate(
        [jnp.broadcast_to(rows[h : h + 1], (HDIM, length)) for h in range(8)], axis=0
    )


def triangle(transposed):
    a = lax.broadcasted_iota(jnp.int32, (Q, Q), 0)
    b = lax.broadcasted_iota(jnp.int32, (Q, Q), 1)
    return jnp.where(a >= b if transposed else a <= b, 1.0, 0.0).astype(F32)


def raw_kernel(seen, wide, out):
    out[...] = dot(wide[...], seen[...], 0, 0)


def raw_rows(seen, wide):
    return pl.pallas_call(
        raw_kernel,
        in_specs=[VMEM_SPEC] * 2,
        out_specs=VMEM_SPEC,
        out_shape=jax.ShapeDtypeStruct((896, seen.shape[1]), F32),
        compiler_params=params(16),
        cost_estimate=pl.CostEstimate(
            flops=2_500_000_000, bytes_accessed=8_000_000, transcendentals=0
        ),
        name="raw",
    )(seen, wide)


def state_kernel(
    raw, squares, bias, a_log, inner, writers, readers, steps, logs, enter, payload
):
    scale = lax.rsqrt(squares[0:1, :] * (1.0 / 4096) + 1e-05)
    inner[...] = (raw[:512] * scale).astype(BF16)
    writers[...] = (raw[512:640] * scale).astype(BF16)
    readers[...] = (raw[640:768] * scale).astype(BF16)
    before = raw[768:776] * scale + bias[:, :1]
    step = jnp.maximum(before, 0.0) + jnp.log1p(jnp.exp(-jnp.abs(before)))
    log = -jnp.exp(a_log[:, :1]) * step
    steps[...] = step
    logs[...] = log
    upper = triangle(False)
    count = raw.shape[1] // Q
    state = jnp.zeros((512, STATE), F32)
    whole = jnp.zeros((8, 1), F32)
    for n in range(count):
        lanes = slice(n * Q, (n + 1) * Q)
        cumul = dot(log[:, lanes], upper, 1, 0, highest)
        total = cumul[:, Q - 1 : Q]
        enter[n] = state.astype(BF16)
        left = over_heads(step[:, lanes] * jnp.exp(total - cumul), Q)
        scaled = (inner[:, lanes].astype(F32) * left).astype(BF16)
        fresh = dot(scaled, writers[:, lanes], 1, 1)
        state = state * over_heads(jnp.broadcast_to(jnp.exp(total), (8, STATE)), STATE) + fresh
        whole = whole + total
    for part in range(4):
        payload[part, pl.ds(0, 128), :] = state[128 * part : 128 * (part + 1)]
        for j in range(2):
            row = 2 * part + j
            payload[part, pl.ds(128 + 8 * j, 8), :] = jnp.broadcast_to(
                jnp.exp(whole[row : row + 1]), (8, STATE)
            )


def local_states(raw, squares, bias, a_log):
    tokens = raw.shape[1]
    return pl.pallas_call(
        state_kernel,
        in_specs=[VMEM_SPEC] * 4,
        out_specs=(VMEM_SPEC,) * 7,
        out_shape=(
            jax.ShapeDtypeStruct((512, tokens), BF16),
            jax.ShapeDtypeStruct((STATE, tokens), BF16),
            jax.ShapeDtypeStruct((STATE, tokens), BF16),
            jax.ShapeDtypeStruct((8, tokens), F32),
            jax.ShapeDtypeStruct((8, tokens), F32),
            jax.ShapeDtypeStruct((tokens // Q, 512, STATE), BF16),
            jax.ShapeDtypeStruct((4, 144, STATE), F32),
        ),
        compiler_params=params(16),
        name="states",
    )(raw, squares, bias, a_log)


def within_kernel(inner, writers, readers, steps, logs, enter, d_skip, out, begun):
    upper, lower = triangle(False), triangle(True)
    causal = upper > 0.0
    whole = jnp.zeros((8, 1), F32)
    for n in range(inner.shape[1] // Q):
        lanes = slice(n * Q, (n + 1) * Q)
        log = logs[:, lanes]
        cumul = dot(log, upper, 1, 0, highest)
        column = dot(lower, log, 1, 1, highest)
        begun[:, lanes] = cumul + whole
        whole = whole + cumul[:, Q - 1 : Q]
        meets = dot(writers[:, lanes], readers[:, lanes], 0, 0)
        carried = dot(enter[n], readers[:, lanes], 1, 0)
        grown = jnp.exp(cumul)
        step = steps[:, lanes]
        for h in range(8):
            span = slice(h * HDIM, (h + 1) * HDIM)
            apart = jnp.minimum(cumul[h : h + 1] - column[:, h : h + 1], 0.0)
            mixing = jnp.where(causal, meets * jnp.exp(apart), 0.0).astype(BF16)
            own = inner[span, lanes].astype(F32)
            scaled = (own * step[h : h + 1]).astype(BF16)
            out[span, lanes] = (
                dot(scaled, mixing, 1, 0)
                + carried[span] * grown[h : h + 1]
                + d_skip[span] * own
            )


def within(inner, writers, readers, steps, logs, enter, d_skip):
    tokens = inner.shape[1]
    return pl.pallas_call(
        within_kernel,
        in_specs=[VMEM_SPEC] * 7,
        out_specs=(VMEM_SPEC,) * 2,
        out_shape=(
            jax.ShapeDtypeStruct((512, tokens), F32),
            jax.ShapeDtypeStruct((8, tokens), F32),
        ),
        compiler_params=params(16),
        cost_estimate=pl.CostEstimate(
            flops=6_000_000_000, bytes_accessed=6_000_000, transcendentals=2_000_000
        ),
        name="within",
    )(inner, writers, readers, steps, logs, enter, d_skip)


def finish_kernel(place, local, begun, readers, *refs):
    gain, out, state = refs[4:]
    for k in range(4):
        rows = pl.ds(pl.multiple_of(lax.rem(place[1] + 4 - k, 4) * 128, 128), 128)
        state[rows, :] = refs[k][...]
    for n in range(local.shape[1] // Q):
        lanes = slice(n * Q, (n + 1) * Q)
        carried = dot(state[...], readers[:, lanes], 1, 0)
        y = local[:, lanes] + carried * over_heads(jnp.exp(begun[:, lanes]), Q)
        mean = jnp.sum(y * y, axis=0, keepdims=True) * (1.0 / 512)
        y = y * lax.rsqrt(mean + 1e-05) * gain[...]
        out[lanes, :] = y.T.astype(BF16)


def finish(place, local, begun, readers, states, gain):
    return pl.pallas_call(
        finish_kernel,
        in_specs=[SMEM_SPEC] + [VMEM_SPEC] * 8,
        out_specs=VMEM_SPEC,
        out_shape=jax.ShapeDtypeStruct((local.shape[1], 512), BF16),
        scratch_shapes=[pltpu.VMEM((512, STATE), BF16)],
        compiler_params=params(16),
        name="finish",
    )(place, local, begun, readers, *states, gain)


def two_heads(decays):
    return jnp.concatenate(
        [jnp.broadcast_to(decays[8 * j : 8 * j + 1], (HDIM, STATE)) for j in range(2)], axis=0
    )


def prefix_kernel(size, slot, place, *refs):
    got, (before, total, held) = refs[:size], refs[size:]
    for k in range(size):
        held[lax.rem(place[slot] + size - k, size)] = got[k][...].astype(F32)
    state, decay = jnp.zeros((128, STATE), F32), jnp.ones((16, STATE), F32)
    for i in range(size):
        before[i, pl.ds(0, 128), :] = state
        before[i, pl.ds(128, 16), :] = decay
        left = held[i, pl.ds(128, 16), :]
        state = state * two_heads(left) + held[i, pl.ds(0, 128), :]
        decay = decay * left
    total[...] = jnp.concatenate([state, decay], axis=0).astype(BF16)


def prefix(place, slot, got):
    size = len(got)
    return pl.pallas_call(
        functools.partial(prefix_kernel, size, slot),
        in_specs=[SMEM_SPEC] + [VMEM_SPEC] * size,
        out_specs=(VMEM_SPEC, VMEM_SPEC),
        out_shape=(
            jax.ShapeDtypeStruct((size, 144, STATE), F32),
            jax.ShapeDtypeStruct((144, STATE), BF16),
        ),
        scratch_shapes=[pltpu.VMEM((size, 144, STATE), F32)],
        compiler_params=params(16),
        name="prefix",
    )(place, *got)


def join_kernel(place, in_row, in_plane, plane, out):
    y = place[2]
    later = place[4] > 0
    begun = jnp.where(later, plane[pl.ds(0, 128), :].astype(F32), 0.0)
    begun = in_plane[y, pl.ds(0, 128), :] + two_heads(in_plane[y, pl.ds(128, 16), :]) * begun
    for i in range(4):
        made = in_row[i, pl.ds(0, 128), :] + two_heads(in_row[i, pl.ds(128, 16), :]) * begun
        out[i] = made.astype(BF16)


def join(place, in_row, in_plane, plane):
    return pl.pallas_call(
        join_kernel,
        in_specs=[SMEM_SPEC] + [VMEM_SPEC] * 3,
        out_specs=VMEM_SPEC,
        out_shape=jax.ShapeDtypeStruct((4, 128, STATE), BF16),
        compiler_params=params(16),
        name="join",
    )(place, in_row, in_plane, plane)


def on_device(
    patches, grid_rows, frame_ids, ln_gain, w_qkv, w_out, w_conn, norm_gain,
    w_x, w_b, w_c, w_dt, dt_bias, a_log, d_skip, out_gain,
):
    core, x, y, zl, zh = (lax.axis_index(a) for a in ("c", "x", "y", "zl", "zh"))
    shard = zh * 16 + y * 4 + x
    place = jnp.stack([core, x, y, zl, zh]).astype(jnp.int32)
    pool = (
        jnp.where(jnp.arange(256)[:, None] // POOL == jnp.arange(64)[None, :], 1.0 / POOL, 0.0)
    ).astype(BF16)

    block = jnp.concatenate([jnp.transpose(w_qkv, (0, 2, 1)), w_out[None]], axis=0)
    piece = jnp.concatenate(
        [
            lax.dynamic_slice(block, (x, 0, 0), (1, 144, XW)),
            lax.dynamic_slice(block, (y, 0, XW), (1, 144, 1152 - XW)),
        ],
        axis=2,
    )
    along = [ring_shift(piece, "zl", 4, k) for k in (1, 2, 3)]

    ids, _ = lax.optimization_barrier((frame_ids[None], piece))
    for axis, size in (("zh", 2), ("x", 4), ("y", 4)):
        ids = jnp.concatenate([ids] + [ring_shift(ids, axis, size, k) for k in range(1, size)], axis=0)
    away = jnp.arange(32)
    holder = (
        lax.rem(zh + 2 - away % 2, 2) * 16
        + lax.rem(y + 4 - away // 8, 4) * 4
        + lax.rem(x + 4 - away // 2 % 4, 4)
    )
    wanted = shard * 12 + jnp.arange(12)
    source = jnp.sum(
        jnp.where(ids[None] == wanted[:, None, None], holder[None, :, None], 0), axis=(1, 2)
    ).astype(jnp.int32)

    block_x, block_y = split_pieces([p[0] for p in along])
    some = lax.dynamic_slice(w_conn, ((y * 4 + x) * 72, 0), (72, 512))
    some = jnp.concatenate([some[:, :256], some[:, 256:]], axis=0)
    turned = jnp.transpose(patches, (0, 2, 1)).reshape(4, 432, 256)
    turned = jnp.concatenate([turned, jnp.broadcast_to(some[None], (4, 144, 256))], axis=1)
    own_frames = lax.dynamic_slice(grid_rows, (zl * 3,), (3,))
    block = block.reshape(4, 3, 48, 1152)
    gain = ln_gain[:, None]
    wide_gain = norm_gain[None]
    (turned, block_x, block_y, source, block, gain, wide_gain, w_dt, pool, place, own_frames) = (
        lax.optimization_barrier(
            (turned, block_x, block_y, source, block, gain, wide_gain, w_dt, pool, place, own_frames)
        )
    )
    whole_x = lax.all_gather(block_x, "x", axis=0)

    own = spread_out(lambda i: lax.dynamic_index_in_dim(turned, i, 0, False), "zl", 4)
    ring_y, own = gather_ring(block_y, "y", own)
    own = jnp.stack(own)
    other = swap_core(own)
    normed, residual = norm_frames(place, own, other, gain, pool)
    product = weight_product(place, own, other, wide_gain, w_x, w_b, w_c, w_dt)
    product, _ = lax.optimization_barrier((product, (whole_x, ring_y)))
    wide = lax.all_gather(product, ("y", "x"), axis=0, tiled=True)

    keep, give = vision(place, own_frames, normed, pool, block, whole_x, ring_y)
    summed = keep + residual + swap_core(give)
    token = jnp.arange(128) % 64
    kept = token[None, :] * POOL < (own_frames * GRID)[:, None]
    seen = jnp.where(kept[None, :, None, :], summed, 0.0).astype(BF16)
    seen = spread_out(lambda i: lax.dynamic_index_in_dim(seen, i, 0, False), "zl", 4)

    outgoing = bucket(place, frame_ids // 12, seen)
    incoming = lax.all_to_all(
        outgoing, ("zh", "y", "x"), split_axis=0, concat_axis=0, tiled=True
    )
    own_features = place_frames(source, incoming)
    line = lax.all_gather(own_features, "zl", axis=0, tiled=True)
    stream, features, squares = stream_rows(place, line, swap_core(line), w_conn)
    raw = raw_rows(features, wide)
    squares, raw = lax.optimization_barrier((squares + swap_core(squares), raw))
    squares = squares + sum(ring_shift(squares, "zl", 4, k) for k in (1, 2, 3))

    def column(values, repeat):
        return jnp.broadcast_to(values[:, None], (values.shape[0], repeat))

    inner, writers, readers, steps, logs, enter, payload = local_states(
        raw, squares, column(dt_bias, 128), column(a_log, 128)
    )
    local, begun = within(
        inner, writers, readers, steps, logs, enter, jnp.repeat(d_skip, HDIM)[:, None]
    )
    sent = payload.astype(BF16)
    in_row, row = prefix(
        place, 1, spread_out(lambda i: lax.dynamic_index_in_dim(sent, i, 0, False), "x", 4)
    )
    in_plane, plane = prefix(place, 2, spread_out(lambda i: row, "y", 4))
    states = join(place, in_row, in_plane, ring_shift(plane, "zh", 2, 1))
    states = spread_out(lambda i: lax.dynamic_index_in_dim(states, i, 0, False), "x", 4)
    mixed = finish(place, local, begun, readers, states, out_gain[:, None])
    return stream, mixed


def solution(mesh):
    fine = Mesh(mesh.devices.reshape(2, 4, 4, 4, 2), ("zh", "y", "x", "zl", "c"))
    tm, head = ("zh", "y", "x"), ("zl", "c")
    in_specs = (
        P(tm, None, head),
        P(tm),
        P(tm),
        P(),
        P(None, None, head),
        P(head, None),
        P(None, head),
        P(),
        P(None, head),
        P(None, head),
        P(None, head),
        P(None, head),
        P(head),
        P(head),
        P(head),
        P(head),
    )
    out_specs = (P(tm, head), P(tm, head))
    return jax.shard_map(
        on_device, mesh=fine, in_specs=in_specs, out_specs=out_specs, check_vma=False
    )
```

```python
import functools
import jax
import jax.numpy as jnp
from jax import lax
from jax.experimental import pallas as pl
from jax.experimental.pallas import tpu as pltpu
from jax.sharding import Mesh, PartitionSpec as P

GRID = 16
POOL = 4
VHD = 72
HDIM = 64
STATE = 128
Q = 256
XW = 512
LOW = 5

F32 = jnp.float32
BF16 = jnp.bfloat16
highest = lax.Precision.HIGHEST
VMEM_SPEC = pl.BlockSpec(memory_space=pltpu.VMEM)
SMEM_SPEC = pl.BlockSpec(memory_space=pltpu.SMEM)
ANY_SPEC = pl.BlockSpec(memory_space=pl.ANY)


def params(mib):
    return pltpu.CompilerParams(vmem_limit_bytes=mib * 2**20)


def dot(a, b, ca, cb, precision=None):
    return lax.dot_general(
        a, b, (((ca,), (cb,)), ((), ())), preferred_element_type=F32, precision=precision
    )


def ring_shift(value, axis, size, shift):
    return lax.ppermute(value, axis, [(i, (i + shift) % size) for i in range(size)])


def swap_core(value):
    return lax.ppermute(value, "c", [(0, 1), (1, 0)])


def spread_out(parts, axis, size):
    position = lax.axis_index(axis)
    own = parts(position)
    return [own] + [
        ring_shift(parts(lax.rem(position + k, size)), axis, size, k) for k in range(1, size)
    ]


def gather_ring(block, axis, later):
    before = ring_shift(block, axis, 4, 1)
    after = ring_shift(block, axis, 4, -1)
    low, high, later = lax.optimization_barrier((before[:LOW], after[LOW:], later))
    far_lo = ring_shift(low, axis, 4, 1)
    far_hi = ring_shift(high, axis, 4, -1)
    return (block, before, far_lo, far_hi, after), later


def split_kernel(a, b, c, left, right):
    for k, source in enumerate((a, b, c)):
        for third in range(3):
            rows = source[pl.ds(48 * third, 48), :]
            left[3 * k + third] = rows[:, :XW]
            right[3 * k + third] = rows[:, XW:]


def split_pieces(pieces):
    return pl.pallas_call(
        split_kernel,
        in_specs=[VMEM_SPEC] * 3,
        out_specs=(VMEM_SPEC, VMEM_SPEC),
        out_shape=(
            jax.ShapeDtypeStruct((9, 48, XW), BF16),
            jax.ShapeDtypeStruct((9, 48, 1152 - XW), BF16),
        ),
        compiler_params=params(8),
        name="split",
    )(*pieces)


def norm_kernel(
    place, own, other, gain, pool, wide_gain, w_dt, w_x, w_b, w_c,
    normed, residual, product, x, big_x, big_b, big_c, sems,
):
    copies = [
        pltpu.make_async_copy(source, held, sems.at[n])
        for n, (source, held) in enumerate(((w_x, big_x), (w_b, big_b), (w_c, big_c)))
    ]
    for copy in copies:
        copy.start()
    first = place[0] == 0
    for f in range(3):
        frame = pl.ds(144 * f, 144)
        for z in range(4):
            k = lax.rem(place[3] + 4 - z, 4)
            mine = own[k, frame, :]
            a, b = mine.astype(F32), other[k, frame, :].astype(F32)
            x[pl.ds(288 * z, 144), :] = jnp.where(first, a, b)
            x[pl.ds(288 * z + 144, 144), :] = jnp.where(first, b, a)
            pooled = dot(mine, pool[...], 1, 0)
            residual[z, f] = jnp.concatenate([pooled[:72], pooled[72:]], axis=1)
        values = x[...]
        width = values.shape[0]
        centre = jnp.sum(values, axis=0, keepdims=True) * (1.0 / width)
        values = values - centre
        spread = jnp.sum(values * values, axis=0, keepdims=True) * (1.0 / width)
        normed[f] = (values * lax.rsqrt(spread + 1e-06) * gain[...]).astype(BF16)
    for copy in copies:
        copy.wait()
    sums = [jnp.zeros((144, width), F32) for width in (512, 128, 128, 8)]
    rows = pl.ds(432, 144)
    for z in range(4):
        k = lax.rem(place[3] + 4 - z, 4)
        a, b = own[k, rows, :].astype(F32), other[k, rows, :].astype(F32)
        for i, part in ((2 * z, jnp.where(first, a, b)), (2 * z + 1, jnp.where(first, b, a))):
            span = pl.ds(512 * i, 512)
            part = jnp.concatenate([part[:72], part[72:]], axis=1) * wide_gain[:, span]
            high = part.astype(BF16).astype(F32)
            both = jnp.concatenate([high, part - high], axis=0).astype(BF16)
            made = [dot(both, w[span, :], 1, 0) for w in (big_x, big_b, big_c)]
            made.append(dot(both, w_dt[:, span], 1, 1))
            sums = [total + extra for total, extra in zip(sums, made)]
    product[...] = jnp.zeros_like(product)
    begun = 0
    for total in sums:
        width = total.shape[1]
        product[:, pl.ds(begun, width)] = (total[:72] + total[72:]).astype(BF16)
        begun += width


def norm_frames(place, own, other, ln_gain, pool, wide_gain, w_dt, w_x, w_b, w_c):
    return pl.pallas_call(
        norm_kernel,
        in_specs=[SMEM_SPEC] + [VMEM_SPEC] * 6 + [ANY_SPEC] * 3,
        out_specs=(VMEM_SPEC, VMEM_SPEC, VMEM_SPEC),
        out_shape=(
            jax.ShapeDtypeStruct((3, 1152, 256), BF16),
            jax.ShapeDtypeStruct((4, 3, 72, 128), F32),
            jax.ShapeDtypeStruct((72, 896), BF16),
        ),
        scratch_shapes=[
            pltpu.VMEM((1152, 256), F32),
            pltpu.VMEM(w_x.shape, BF16),
            pltpu.VMEM(w_b.shape, BF16),
            pltpu.VMEM(w_c.shape, BF16),
            pltpu.SemaphoreType.DMA((3,)),
        ],
        compiler_params=params(56),
        name="norm",
    )(place, own, other, ln_gain, pool, wide_gain, w_dt, w_x, w_b, w_c)


def vision_kernel(place, rows, normed, pool, block, *rest):
    whole, *ring = rest[:6]
    keep, give, wx, wy, qkv, ctx, sems = rest[6:]
    frame = pl.program_id(0)
    first = place[0] == 0

    def copies():
        pairs = [
            (block.at[:, :, :, pl.ds(0, XW)], wx.at[:, pl.ds(0, 3)]),
            (block.at[:, :, :, pl.ds(XW, 1152 - XW)], wy.at[:, pl.ds(0, 3)]),
            (whole, wx.at[:, pl.ds(3, 9)]),
        ]
        for source, distance, lo, size in zip(
            ring, (0, 1, 2, 2, 3), (0, 0, 0, LOW, 0), (9, 9, LOW, 9 - LOW, 9)
        ):
            index = lax.rem(place[2] + 4 - distance, 4)
            pairs.append((source, wy.at[index, pl.ds(3 + lo, size)]))
        return [
            pltpu.make_async_copy(source, held, sems.at[n])
            for n, (source, held) in enumerate(pairs)
        ]

    @pl.when(frame == 0)
    def _():
        for copy in copies():
            copy.start()
        for copy in copies():
            copy.wait()

    width = normed.shape[1]
    for m in range(3):
        left = wx[m].reshape(576, XW)
        right = wy[m].reshape(576, width - XW)
        qkv[m] = dot(left, normed[0, :XW], 1, 0) + dot(right, normed[0, XW:], 1, 0)
    valid = rows[frame] * GRID
    usable = lax.broadcasted_iota(jnp.int32, (256, 256), 0) < valid
    for h in range(8):
        span = pl.ds(h * VHD, VHD)
        q, k, v = (qkv[m, span, :].astype(BF16) for m in range(3))
        scores = dot(k, q, 0, 0) * VHD ** (-0.5)
        scores = jnp.where(usable, scores, -1e30)
        top = jnp.max(scores, axis=0, keepdims=True)
        powered = jnp.exp(scores - top)
        total = jnp.sum(powered, axis=0, keepdims=True)
        ctx[span, :] = dot(v, powered.astype(BF16), 1, 0) * (1.0 / total)
    pooled = dot(ctx[...].astype(BF16), pool[...], 1, 0)
    high = pooled.astype(BF16)
    low = (pooled - high.astype(F32)).astype(BF16)
    both = jnp.concatenate([high, low], axis=1)
    out_x = dot(both, wx[3].reshape(576, XW), 0, 0)
    out_y = dot(both, wy[3].reshape(576, width - XW), 0, 0)
    attended = jnp.concatenate([out_x, out_y], axis=1)
    attended = (attended[:64] + attended[64:]).T
    for z in range(4):
        a = attended[(2 * z) * 144 : (2 * z + 1) * 144]
        b = attended[(2 * z + 1) * 144 : (2 * z + 2) * 144]
        own = jnp.where(first, a, b)
        far = jnp.where(first, b, a)
        keep[z, 0] = jnp.concatenate([own[:72], own[72:]], axis=1)
        give[z, 0] = jnp.concatenate([far[:72], far[72:]], axis=1)


def vision(place, rows, normed, pool, block, whole, ring):
    out = pl.BlockSpec((4, 1, 72, 128), lambda f: (0, f, 0, 0))
    shape = jax.ShapeDtypeStruct((4, 3, 72, 128), F32)
    return pl.pallas_call(
        vision_kernel,
        grid=(3,),
        in_specs=[
            SMEM_SPEC,
            SMEM_SPEC,
            pl.BlockSpec((1, 1152, 256), lambda f: (f, 0, 0)),
            VMEM_SPEC,
        ]
        + [ANY_SPEC] * 7,
        out_specs=(out, out),
        out_shape=(shape, shape),
        scratch_shapes=[
            pltpu.VMEM((4, 12, 48, XW), BF16),
            pltpu.VMEM((4, 12, 48, 1152 - XW), BF16),
            pltpu.VMEM((3, 576, 256), F32),
            pltpu.VMEM((576, 256), F32),
            pltpu.SemaphoreType.DMA((8,)),
        ],
        compiler_params=params(56),
        name="vision",
    )(place, rows, normed, pool, block, whole, *ring)


def bucket_kernel(place, ids, *refs):
    out = refs[4]
    out[...] = jnp.zeros_like(out)
    for k in range(4):
        z = lax.rem(place[3] + 4 - k, 4)
        for j in range(3):
            frame = ids[3 * z + j]
            spot = lax.rem(frame, 12) + 1
            label = jnp.zeros((8, 128), F32) + spot.astype(F32)
            whole = jnp.concatenate([refs[k][j].astype(F32), label], axis=0)
            out[lax.div(frame, 12)] = whole.astype(BF16)


def bucket(place, ids, seen):
    return pl.pallas_call(
        bucket_kernel,
        in_specs=[SMEM_SPEC, SMEM_SPEC] + [VMEM_SPEC] * 4,
        out_specs=VMEM_SPEC,
        out_shape=jax.ShapeDtypeStruct((32, 80, 128), BF16),
        compiler_params=params(16),
        name="bucket",
    )(place, ids, *seen)


def place_kernel(incoming, out, held):
    held[...] = incoming[...].astype(F32)
    left = lax.broadcasted_iota(jnp.int32, (72, 128), 1) < 64

    def frame(p):
        found = jnp.zeros((72, 128), F32)
        for s in range(32):
            here = held[s, pl.ds(72, 1), :] == float(p + 1)
            found = jnp.where(here, held[s, pl.ds(0, 72), :], found)
        return found

    for pair in range(6):
        a, b = frame(2 * pair), frame(2 * pair + 1)
        lanes = pl.ds(128 * pair, 128)
        top = jnp.where(left, a, pltpu.roll(b, 64, 1))
        bottom = jnp.where(left, pltpu.roll(a, 64, 1), b)
        out[:, lanes] = jnp.concatenate([top, bottom], axis=0).astype(BF16)


def place_frames(incoming):
    return pl.pallas_call(
        place_kernel,
        in_specs=[VMEM_SPEC],
        out_specs=VMEM_SPEC,
        out_shape=jax.ShapeDtypeStruct((144, 768), BF16),
        scratch_shapes=[pltpu.VMEM((32, 80, 128), F32)],
        compiler_params=params(16),
        name="place",
    )(incoming)


def stream_kernel(place, mine, other, w_conn, wide, stream, raw, squares, seen):
    first = place[0] == 0
    for z in range(4):
        a, b = mine[pl.ds(144 * z, 144), :], other[pl.ds(144 * z, 144), :]
        seen[pl.ds(288 * z, 144), :] = jnp.where(first, a, b)
        seen[pl.ds(288 * z + 144, 144), :] = jnp.where(first, b, a)
    made = dot(w_conn[...], seen[...], 0, 0).astype(BF16)
    values = made.astype(F32)
    squares[...] = jnp.broadcast_to(
        jnp.sum(values * values, axis=0, keepdims=True), squares.shape
    )
    stream[...] = values.T.astype(BF16)
    raw[...] = dot(wide[...], seen[...], 0, 0)


def stream_rows(place, mine, other, w_conn, wide):
    tokens, width = mine.shape[1], w_conn.shape[1]
    return pl.pallas_call(
        stream_kernel,
        in_specs=[SMEM_SPEC] + [VMEM_SPEC] * 4,
        out_specs=(VMEM_SPEC, VMEM_SPEC, VMEM_SPEC),
        out_shape=(
            jax.ShapeDtypeStruct((tokens, width), BF16),
            jax.ShapeDtypeStruct((896, tokens), F32),
            jax.ShapeDtypeStruct((8, tokens), F32),
        ),
        scratch_shapes=[pltpu.VMEM((1152, tokens), BF16)],
        compiler_params=params(20),
        name="stream",
    )(place, mine, other, w_conn, wide)


def over_heads(rows, length):
    return jnp.concatenate(
        [jnp.broadcast_to(rows[h : h + 1], (HDIM, length)) for h in range(8)], axis=0
    )


def triangle(transposed):
    a = lax.broadcasted_iota(jnp.int32, (Q, Q), 0)
    b = lax.broadcasted_iota(jnp.int32, (Q, Q), 1)
    return jnp.where(a >= b if transposed else a <= b, 1.0, 0.0).astype(F32)


def state_kernel(
    raw, squares, bias, a_log, inner, writers, readers, steps, logs, enter, payload
):
    scale = lax.rsqrt(squares[0:1, :] * (1.0 / 4096) + 1e-05)
    inner[...] = (raw[:512] * scale).astype(BF16)
    writers[...] = (raw[512:640] * scale).astype(BF16)
    readers[...] = (raw[640:768] * scale).astype(BF16)
    before = raw[768:776] * scale + bias[:, :1]
    step = jnp.maximum(before, 0.0) + jnp.log1p(jnp.exp(-jnp.abs(before)))
    log = -jnp.exp(a_log[:, :1]) * step
    steps[...] = step
    logs[...] = log
    upper = triangle(False)
    count = raw.shape[1] // Q
    state = jnp.zeros((512, STATE), F32)
    whole = jnp.zeros((8, 1), F32)
    for n in range(count):
        lanes = slice(n * Q, (n + 1) * Q)
        cumul = dot(log[:, lanes], upper, 1, 0, highest)
        total = cumul[:, Q - 1 : Q]
        enter[n] = state.astype(BF16)
        left = over_heads(step[:, lanes] * jnp.exp(total - cumul), Q)
        scaled = (inner[:, lanes].astype(F32) * left).astype(BF16)
        fresh = dot(scaled, writers[:, lanes], 1, 1)
        state = state * over_heads(jnp.broadcast_to(jnp.exp(total), (8, STATE)), STATE) + fresh
        whole = whole + total
    for part in range(4):
        payload[part, pl.ds(0, 128), :] = state[128 * part : 128 * (part + 1)]
        for j in range(2):
            row = 2 * part + j
            payload[part, pl.ds(128 + 8 * j, 8), :] = jnp.broadcast_to(
                jnp.exp(whole[row : row + 1]), (8, STATE)
            )


def local_states(raw, squares, bias, a_log):
    tokens = raw.shape[1]
    return pl.pallas_call(
        state_kernel,
        in_specs=[VMEM_SPEC] * 4,
        out_specs=(VMEM_SPEC,) * 7,
        out_shape=(
            jax.ShapeDtypeStruct((512, tokens), BF16),
            jax.ShapeDtypeStruct((STATE, tokens), BF16),
            jax.ShapeDtypeStruct((STATE, tokens), BF16),
            jax.ShapeDtypeStruct((8, tokens), F32),
            jax.ShapeDtypeStruct((8, tokens), F32),
            jax.ShapeDtypeStruct((tokens // Q, 512, STATE), BF16),
            jax.ShapeDtypeStruct((4, 144, STATE), F32),
        ),
        compiler_params=params(16),
        name="states",
    )(raw, squares, bias, a_log)


def within_kernel(inner, writers, readers, steps, logs, enter, d_skip, out, begun):
    upper, lower = triangle(False), triangle(True)
    causal = upper > 0.0
    whole = jnp.zeros((8, 1), F32)
    for n in range(inner.shape[1] // Q):
        lanes = slice(n * Q, (n + 1) * Q)
        log = logs[:, lanes]
        cumul = dot(log, upper, 1, 0, highest)
        column = dot(lower, log, 1, 1, highest)
        begun[:, lanes] = cumul + whole
        whole = whole + cumul[:, Q - 1 : Q]
        meets = dot(writers[:, lanes], readers[:, lanes], 0, 0)
        carried = dot(enter[n], readers[:, lanes], 1, 0)
        grown = jnp.exp(cumul)
        step = steps[:, lanes]
        for h in range(8):
            span = slice(h * HDIM, (h + 1) * HDIM)
            apart = jnp.minimum(cumul[h : h + 1] - column[:, h : h + 1], 0.0)
            mixing = jnp.where(causal, meets * jnp.exp(apart), 0.0).astype(BF16)
            own = inner[span, lanes].astype(F32)
            scaled = (own * step[h : h + 1]).astype(BF16)
            out[span, lanes] = (
                dot(scaled, mixing, 1, 0)
                + carried[span] * grown[h : h + 1]
                + d_skip[span] * own
            )


def within(inner, writers, readers, steps, logs, enter, d_skip):
    tokens = inner.shape[1]
    return pl.pallas_call(
        within_kernel,
        in_specs=[VMEM_SPEC] * 7,
        out_specs=(VMEM_SPEC,) * 2,
        out_shape=(
            jax.ShapeDtypeStruct((512, tokens), F32),
            jax.ShapeDtypeStruct((8, tokens), F32),
        ),
        compiler_params=params(16),
        cost_estimate=pl.CostEstimate(
            flops=6_000_000_000, bytes_accessed=6_000_000, transcendentals=2_000_000
        ),
        name="within",
    )(inner, writers, readers, steps, logs, enter, d_skip)


def finish_kernel(place, local, begun, readers, *refs):
    gain, out, state = refs[4:]
    for k in range(4):
        rows = pl.ds(pl.multiple_of(lax.rem(place[1] + 4 - k, 4) * 128, 128), 128)
        state[rows, :] = refs[k][...]
    for n in range(local.shape[1] // Q):
        lanes = slice(n * Q, (n + 1) * Q)
        carried = dot(state[...], readers[:, lanes], 1, 0)
        y = local[:, lanes] + carried * over_heads(jnp.exp(begun[:, lanes]), Q)
        mean = jnp.sum(y * y, axis=0, keepdims=True) * (1.0 / 512)
        y = y * lax.rsqrt(mean + 1e-05) * gain[...]
        out[lanes, :] = y.T.astype(BF16)


def finish(place, local, begun, readers, states, gain):
    return pl.pallas_call(
        finish_kernel,
        in_specs=[SMEM_SPEC] + [VMEM_SPEC] * 8,
        out_specs=VMEM_SPEC,
        out_shape=jax.ShapeDtypeStruct((local.shape[1], 512), BF16),
        scratch_shapes=[pltpu.VMEM((512, STATE), BF16)],
        compiler_params=params(16),
        name="finish",
    )(place, local, begun, readers, *states, gain)


def two_heads(decays):
    return jnp.concatenate(
        [jnp.broadcast_to(decays[8 * j : 8 * j + 1], (HDIM, STATE)) for j in range(2)], axis=0
    )


def prefix_kernel(size, slot, place, *refs):
    got, (before, total, held) = refs[:size], refs[size:]
    for k in range(size):
        held[lax.rem(place[slot] + size - k, size)] = got[k][...].astype(F32)
    state, decay = jnp.zeros((128, STATE), F32), jnp.ones((16, STATE), F32)
    for i in range(size):
        before[i, pl.ds(0, 128), :] = state
        before[i, pl.ds(128, 16), :] = decay
        left = held[i, pl.ds(128, 16), :]
        state = state * two_heads(left) + held[i, pl.ds(0, 128), :]
        decay = decay * left
    total[...] = jnp.concatenate([state, decay], axis=0).astype(BF16)


def prefix(place, slot, got):
    size = len(got)
    return pl.pallas_call(
        functools.partial(prefix_kernel, size, slot),
        in_specs=[SMEM_SPEC] + [VMEM_SPEC] * size,
        out_specs=(VMEM_SPEC, VMEM_SPEC),
        out_shape=(
            jax.ShapeDtypeStruct((size, 144, STATE), F32),
            jax.ShapeDtypeStruct((144, STATE), BF16),
        ),
        scratch_shapes=[pltpu.VMEM((size, 144, STATE), F32)],
        compiler_params=params(16),
        name="prefix",
    )(place, *got)


def join_kernel(place, in_row, rows, out):
    begun = rows[place[5], pl.ds(0, 128), :]
    for i in range(4):
        made = in_row[i, pl.ds(0, 128), :] + two_heads(in_row[i, pl.ds(128, 16), :]) * begun
        out[i] = made.astype(BF16)


def join(place, in_row, rows):
    return pl.pallas_call(
        join_kernel,
        in_specs=[SMEM_SPEC] + [VMEM_SPEC] * 2,
        out_specs=VMEM_SPEC,
        out_shape=jax.ShapeDtypeStruct((4, 128, STATE), BF16),
        compiler_params=params(16),
        name="join",
    )(place, in_row, rows)


def on_device(
    patches, grid_rows, frame_ids, ln_gain, w_qkv, w_out, w_conn, norm_gain,
    w_x, w_b, w_c, w_dt, dt_bias, a_log, d_skip, out_gain,
):
    core, x, y, zl, zh = (lax.axis_index(a) for a in ("c", "x", "y", "zl", "zh"))
    place = jnp.stack([core, x, y, zl, zh, zh * 4 + y]).astype(jnp.int32)
    pool = (
        jnp.where(jnp.arange(256)[:, None] // POOL == jnp.arange(64)[None, :], 1.0 / POOL, 0.0)
    ).astype(BF16)

    block = jnp.concatenate([jnp.transpose(w_qkv, (0, 2, 1)), w_out[None]], axis=0)
    piece = jnp.concatenate(
        [
            lax.dynamic_slice(block, (x, 0, 0), (1, 144, XW)),
            lax.dynamic_slice(block, (y, 0, XW), (1, 144, 1152 - XW)),
        ],
        axis=2,
    )
    along = [ring_shift(piece, "zl", 4, k) for k in (1, 2, 3)]

    block_x, block_y = split_pieces([p[0] for p in along])
    some = lax.dynamic_slice(w_conn, ((y * 4 + x) * 72, 0), (72, 512))
    some = jnp.concatenate([some[:, :256], some[:, 256:]], axis=0)
    turned = jnp.transpose(patches, (0, 2, 1)).reshape(4, 432, 256)
    turned = jnp.concatenate([turned, jnp.broadcast_to(some[None], (4, 144, 256))], axis=1)
    own_frames = lax.dynamic_slice(grid_rows, (zl * 3,), (3,))
    block = block.reshape(4, 3, 48, 1152)
    gain = ln_gain[:, None]
    wide_gain = norm_gain[None]
    (turned, block_x, block_y, block, gain, wide_gain, pool, place, own_frames) = (
        lax.optimization_barrier(
            (turned, block_x, block_y, block, gain, wide_gain, pool, place, own_frames)
        )
    )
    whole_x = lax.all_gather(block_x, "x", axis=0)

    own = spread_out(lambda i: lax.dynamic_index_in_dim(turned, i, 0, False), "zl", 4)
    ring_y, own = gather_ring(block_y, "y", own)
    own = jnp.stack(own)
    other = swap_core(own)
    normed, residual, product = norm_frames(
        place, own, other, gain, pool, wide_gain, w_dt.T, w_x, w_b, w_c
    )
    product, _ = lax.optimization_barrier((product, (whole_x, ring_y)))
    wide = lax.all_gather(product, ("y", "x"), axis=0, tiled=True)

    keep, give = vision(place, own_frames, normed, pool, block, whole_x, ring_y)
    summed = keep + residual + swap_core(give)
    token = jnp.arange(128) % 64
    kept = token[None, :] * POOL < (own_frames * GRID)[:, None]
    seen = jnp.where(kept[None, :, None, :], summed, 0.0).astype(BF16)
    seen = spread_out(lambda i: lax.dynamic_index_in_dim(seen, i, 0, False), "zl", 4)

    outgoing = bucket(place, frame_ids, seen)
    incoming = lax.all_to_all(
        outgoing, ("zh", "y", "x"), split_axis=0, concat_axis=0, tiled=True
    )
    own_features = place_frames(incoming)
    line = lax.all_gather(own_features, "zl", axis=0, tiled=True)
    stream, raw, squares = stream_rows(place, line, swap_core(line), w_conn, wide)
    squares = squares + swap_core(squares)
    squares = squares + sum(ring_shift(squares, "zl", 4, k) for k in (1, 2, 3))

    def column(values, repeat):
        return jnp.broadcast_to(values[:, None], (values.shape[0], repeat))

    inner, writers, readers, steps, logs, enter, payload = local_states(
        raw, squares, column(dt_bias, 128), column(a_log, 128)
    )
    local, begun = within(
        inner, writers, readers, steps, logs, enter, jnp.repeat(d_skip, HDIM)[:, None]
    )
    sent = payload.astype(BF16)
    in_row, row = prefix(
        place, 1, spread_out(lambda i: lax.dynamic_index_in_dim(sent, i, 0, False), "x", 4)
    )
    rows = prefix(place, 5, spread_out(lambda i: row, ("zh", "y"), 8))[0]
    states = join(place, in_row, rows)
    states = spread_out(lambda i: lax.dynamic_index_in_dim(states, i, 0, False), "x", 4)
    mixed = finish(place, local, begun, readers, states, out_gain[:, None])
    return stream, mixed


def solution(mesh):
    fine = Mesh(mesh.devices.reshape(2, 4, 4, 4, 2), ("zh", "y", "x", "zl", "c"))
    tm, head = ("zh", "y", "x"), ("zl", "c")
    in_specs = (
        P(tm, None, head),
        P(tm),
        P(tm),
        P(),
        P(None, None, head),
        P(head, None),
        P(None, head),
        P(),
        P(None, head),
        P(None, head),
        P(None, head),
        P(None, head),
        P(head),
        P(head),
        P(head),
        P(head),
    )
    out_specs = (P(tm, head), P(tm, head))
    return jax.shard_map(
        on_device, mesh=fine, in_specs=in_specs, out_specs=out_specs, check_vma=False
    )
```

```python
import functools
import jax
import jax.numpy as jnp
from jax import lax
from jax.experimental import pallas as pl
from jax.experimental.pallas import tpu as pltpu
from jax.sharding import Mesh, PartitionSpec as P

GRID = 16
POOL = 4
VHD = 72
HDIM = 64
STATE = 128
Q = 256
XW = 512
LOW = 5

F32 = jnp.float32
BF16 = jnp.bfloat16
highest = lax.Precision.HIGHEST
VMEM_SPEC = pl.BlockSpec(memory_space=pltpu.VMEM)
SMEM_SPEC = pl.BlockSpec(memory_space=pltpu.SMEM)
ANY_SPEC = pl.BlockSpec(memory_space=pl.ANY)


def params(mib):
    return pltpu.CompilerParams(vmem_limit_bytes=mib * 2**20)


def dot(a, b, ca, cb, precision=None):
    return lax.dot_general(
        a, b, (((ca,), (cb,)), ((), ())), preferred_element_type=F32, precision=precision
    )


def ring_shift(value, axis, size, shift):
    return lax.ppermute(value, axis, [(i, (i + shift) % size) for i in range(size)])


def swap_core(value):
    return lax.ppermute(value, "c", [(0, 1), (1, 0)])


def spread_out(parts, axis, size):
    position = lax.axis_index(axis)
    own = parts(position)
    return [own] + [
        ring_shift(parts(lax.rem(position + k, size)), axis, size, k) for k in range(1, size)
    ]


def gather_ring(block, axis, later):
    before = ring_shift(block, axis, 4, 1)
    after = ring_shift(block, axis, 4, -1)
    low, high, later = lax.optimization_barrier((before[:LOW], after[LOW:], later))
    far_lo = ring_shift(low, axis, 4, 1)
    far_hi = ring_shift(high, axis, 4, -1)
    return (block, before, far_lo, far_hi, after), later


def split_kernel(a, b, c, left, right):
    for k, source in enumerate((a, b, c)):
        for third in range(3):
            rows = source[pl.ds(48 * third, 48), :]
            left[3 * k + third] = rows[:, :XW]
            right[3 * k + third] = rows[:, XW:]


def split_pieces(pieces):
    return pl.pallas_call(
        split_kernel,
        in_specs=[VMEM_SPEC] * 3,
        out_specs=(VMEM_SPEC, VMEM_SPEC),
        out_shape=(
            jax.ShapeDtypeStruct((9, 48, XW), BF16),
            jax.ShapeDtypeStruct((9, 48, 1152 - XW), BF16),
        ),
        compiler_params=params(8),
        name="split",
    )(*pieces)


def norm_kernel(
    place, own, other, gain, pool, wide_gain, w_dt, w_x, w_b, w_c,
    normed, residual, product, x, big_x, big_b, big_c, sems,
):
    copies = [
        pltpu.make_async_copy(source, held, sems.at[n])
        for n, (source, held) in enumerate(((w_x, big_x), (w_b, big_b), (w_c, big_c)))
    ]
    for copy in copies:
        copy.start()
    first = place[0] == 0
    for f in range(3):
        frame = pl.ds(144 * f, 144)
        for z in range(4):
            k = lax.rem(place[3] + 4 - z, 4)
            mine = own[k, frame, :]
            a, b = mine.astype(F32), other[k, frame, :].astype(F32)
            x[pl.ds(288 * z, 144), :] = jnp.where(first, a, b)
            x[pl.ds(288 * z + 144, 144), :] = jnp.where(first, b, a)
            pooled = dot(mine, pool[...], 1, 0)
            residual[z, f] = jnp.concatenate([pooled[:72], pooled[72:]], axis=1)
        values = x[...]
        width = values.shape[0]
        centre = jnp.sum(values, axis=0, keepdims=True) * (1.0 / width)
        values = values - centre
        spread = jnp.sum(values * values, axis=0, keepdims=True) * (1.0 / width)
        normed[f] = (values * lax.rsqrt(spread + 1e-06) * gain[...]).astype(BF16)
    for copy in copies:
        copy.wait()
    sums = [jnp.zeros((144, width), F32) for width in (512, 128, 128, 8)]
    rows = pl.ds(432, 144)
    for z in range(4):
        k = lax.rem(place[3] + 4 - z, 4)
        a, b = own[k, rows, :].astype(F32), other[k, rows, :].astype(F32)
        for i, part in ((2 * z, jnp.where(first, a, b)), (2 * z + 1, jnp.where(first, b, a))):
            span = pl.ds(512 * i, 512)
            part = jnp.concatenate([part[:72], part[72:]], axis=1) * wide_gain[:, span]
            high = part.astype(BF16).astype(F32)
            both = jnp.concatenate([high, part - high], axis=0).astype(BF16)
            made = [dot(both, w[span, :], 1, 0) for w in (big_x, big_b, big_c)]
            made.append(dot(both, w_dt[:, span], 1, 1))
            sums = [total + extra for total, extra in zip(sums, made)]
    product[...] = jnp.zeros_like(product)
    begun = 0
    for total in sums:
        width = total.shape[1]
        product[:, pl.ds(begun, width)] = (total[:72] + total[72:]).astype(BF16)
        begun += width


def norm_frames(place, own, other, ln_gain, pool, wide_gain, w_dt, w_x, w_b, w_c):
    return pl.pallas_call(
        norm_kernel,
        in_specs=[SMEM_SPEC] + [VMEM_SPEC] * 6 + [ANY_SPEC] * 3,
        out_specs=(VMEM_SPEC, VMEM_SPEC, VMEM_SPEC),
        out_shape=(
            jax.ShapeDtypeStruct((3, 1152, 256), BF16),
            jax.ShapeDtypeStruct((4, 3, 72, 128), F32),
            jax.ShapeDtypeStruct((72, 896), BF16),
        ),
        scratch_shapes=[
            pltpu.VMEM((1152, 256), F32),
            pltpu.VMEM(w_x.shape, BF16),
            pltpu.VMEM(w_b.shape, BF16),
            pltpu.VMEM(w_c.shape, BF16),
            pltpu.SemaphoreType.DMA((3,)),
        ],
        compiler_params=params(56),
        name="norm",
    )(place, own, other, ln_gain, pool, wide_gain, w_dt, w_x, w_b, w_c)


def vision_kernel(place, rows, normed, pool, block, *rest):
    whole, *ring = rest[:6]
    keep, give, wx, wy, qkv, ctx, scores, powered, sems = rest[6:]
    frame = pl.program_id(0)
    first = place[0] == 0

    def copies():
        pairs = [
            (block.at[:, :, :, pl.ds(0, XW)], wx.at[:, pl.ds(0, 3)]),
            (block.at[:, :, :, pl.ds(XW, 1152 - XW)], wy.at[:, pl.ds(0, 3)]),
            (whole, wx.at[:, pl.ds(3, 9)]),
        ]
        for source, distance, lo, size in zip(
            ring, (0, 1, 2, 2, 3), (0, 0, 0, LOW, 0), (9, 9, LOW, 9 - LOW, 9)
        ):
            index = lax.rem(place[2] + 4 - distance, 4)
            pairs.append((source, wy.at[index, pl.ds(3 + lo, size)]))
        return [
            pltpu.make_async_copy(source, held, sems.at[n])
            for n, (source, held) in enumerate(pairs)
        ]

    @pl.when(frame == 0)
    def _():
        for copy in copies():
            copy.start()
        for copy in copies():
            copy.wait()

    width = normed.shape[1]
    for m in range(3):
        left = wx[m].reshape(576, XW)
        right = wy[m].reshape(576, width - XW)
        qkv[m] = dot(left, normed[0, :XW], 1, 0) + dot(right, normed[0, XW:], 1, 0)
    valid = rows[frame] * GRID
    usable = lax.broadcasted_iota(jnp.int32, (256, 256), 0) < valid
    for h in range(8):
        span = pl.ds(h * VHD, VHD)
        q, k = (qkv[m, span, :].astype(BF16) for m in range(2))
        scores[h] = dot(k, q, 0, 0)
    shares = []
    for h in range(8):
        values = jnp.where(usable, scores[h], -1e30)
        top = jnp.max(values, axis=0, keepdims=True)
        values = jnp.exp((values - top) * VHD ** (-0.5))
        shares.append(1.0 / jnp.sum(values, axis=0, keepdims=True))
        powered[h] = values.astype(BF16)
    for h in range(8):
        span = pl.ds(h * VHD, VHD)
        ctx[span, :] = dot(qkv[2, span, :].astype(BF16), powered[h], 1, 0) * shares[h]
    pooled = dot(ctx[...].astype(BF16), pool[...], 1, 0)
    high = pooled.astype(BF16)
    low = (pooled - high.astype(F32)).astype(BF16)
    both = jnp.concatenate([high, low], axis=1)
    out_x = dot(both, wx[3].reshape(576, XW), 0, 0)
    out_y = dot(both, wy[3].reshape(576, width - XW), 0, 0)
    attended = jnp.concatenate([out_x, out_y], axis=1)
    attended = (attended[:64] + attended[64:]).T
    for z in range(4):
        a = attended[(2 * z) * 144 : (2 * z + 1) * 144]
        b = attended[(2 * z + 1) * 144 : (2 * z + 2) * 144]
        own = jnp.where(first, a, b)
        far = jnp.where(first, b, a)
        keep[z, 0] = jnp.concatenate([own[:72], own[72:]], axis=1)
        give[z, 0] = jnp.concatenate([far[:72], far[72:]], axis=1)


def vision(place, rows, normed, pool, block, whole, ring):
    out = pl.BlockSpec((4, 1, 72, 128), lambda f: (0, f, 0, 0))
    shape = jax.ShapeDtypeStruct((4, 3, 72, 128), F32)
    return pl.pallas_call(
        vision_kernel,
        grid=(3,),
        in_specs=[
            SMEM_SPEC,
            SMEM_SPEC,
            pl.BlockSpec((1, 1152, 256), lambda f: (f, 0, 0)),
            VMEM_SPEC,
        ]
        + [ANY_SPEC] * 7,
        out_specs=(out, out),
        out_shape=(shape, shape),
        scratch_shapes=[
            pltpu.VMEM((4, 12, 48, XW), BF16),
            pltpu.VMEM((4, 12, 48, 1152 - XW), BF16),
            pltpu.VMEM((3, 576, 256), F32),
            pltpu.VMEM((576, 256), F32),
            pltpu.VMEM((8, 256, 256), F32),
            pltpu.VMEM((8, 256, 256), BF16),
            pltpu.SemaphoreType.DMA((8,)),
        ],
        compiler_params=params(56),
        name="vision",
    )(place, rows, normed, pool, block, whole, *ring)


def bucket_kernel(place, ids, *refs):
    out = refs[4]
    out[...] = jnp.zeros_like(out)
    for k in range(4):
        z = lax.rem(place[3] + 4 - k, 4)
        for j in range(3):
            frame = ids[3 * z + j]
            spot = lax.rem(frame, 12) + 1
            label = jnp.zeros((8, 128), F32) + spot.astype(F32)
            whole = jnp.concatenate([refs[k][j].astype(F32), label], axis=0)
            out[lax.div(frame, 12)] = whole.astype(BF16)


def bucket(place, ids, seen):
    return pl.pallas_call(
        bucket_kernel,
        in_specs=[SMEM_SPEC, SMEM_SPEC] + [VMEM_SPEC] * 4,
        out_specs=VMEM_SPEC,
        out_shape=jax.ShapeDtypeStruct((32, 80, 128), BF16),
        compiler_params=params(16),
        name="bucket",
    )(place, ids, *seen)


def place_kernel(incoming, out, held):
    held[...] = incoming[...].astype(F32)
    left = lax.broadcasted_iota(jnp.int32, (72, 128), 1) < 64

    def frame(p):
        found = jnp.zeros((72, 128), F32)
        for s in range(32):
            here = held[s, pl.ds(72, 1), :] == float(p + 1)
            found = jnp.where(here, held[s, pl.ds(0, 72), :], found)
        return found

    for pair in range(6):
        a, b = frame(2 * pair), frame(2 * pair + 1)
        lanes = pl.ds(128 * pair, 128)
        top = jnp.where(left, a, pltpu.roll(b, 64, 1))
        bottom = jnp.where(left, pltpu.roll(a, 64, 1), b)
        out[:, lanes] = jnp.concatenate([top, bottom], axis=0).astype(BF16)


def place_frames(incoming):
    return pl.pallas_call(
        place_kernel,
        in_specs=[VMEM_SPEC],
        out_specs=VMEM_SPEC,
        out_shape=jax.ShapeDtypeStruct((144, 768), BF16),
        scratch_shapes=[pltpu.VMEM((32, 80, 128), F32)],
        compiler_params=params(16),
        name="place",
    )(incoming)


def stream_kernel(place, mine, other, w_conn, wide, stream, raw, squares, seen, held, sem):
    first = place[0] == 0
    for z in range(4):
        a, b = mine[pl.ds(144 * z, 144), :], other[pl.ds(144 * z, 144), :]
        seen[pl.ds(288 * z, 144), :] = jnp.where(first, a, b)
        seen[pl.ds(288 * z + 144, 144), :] = jnp.where(first, b, a)
    held[pl.ds(0, 768), :] = dot(wide[:, pl.ds(0, 768)], seen[...], 0, 0)
    held[pl.ds(768, 8), :] = dot(wide[:, pl.ds(768, 128)], seen[...], 0, 0)[:8]
    copy = pltpu.make_async_copy(held, raw, sem)
    copy.start()
    made = dot(w_conn[...], seen[...], 0, 0).astype(BF16)
    values = made.astype(F32)
    squares[...] = jnp.broadcast_to(
        jnp.sum(values * values, axis=0, keepdims=True), squares.shape
    )
    stream[...] = values.T.astype(BF16)
    copy.wait()


def stream_rows(place, mine, other, w_conn, wide):
    tokens, width = mine.shape[1], w_conn.shape[1]
    return pl.pallas_call(
        stream_kernel,
        in_specs=[SMEM_SPEC] + [VMEM_SPEC] * 4,
        out_specs=(VMEM_SPEC, ANY_SPEC, VMEM_SPEC),
        out_shape=(
            jax.ShapeDtypeStruct((tokens, width), BF16),
            jax.ShapeDtypeStruct((776, tokens), F32),
            jax.ShapeDtypeStruct((8, tokens), F32),
        ),
        scratch_shapes=[
            pltpu.VMEM((1152, tokens), BF16),
            pltpu.VMEM((776, tokens), F32),
            pltpu.SemaphoreType.DMA(()),
        ],
        compiler_params=params(24),
        name="stream",
    )(place, mine, other, w_conn, wide)


def over_heads(rows, length):
    return jnp.concatenate(
        [jnp.broadcast_to(rows[h : h + 1], (HDIM, length)) for h in range(8)], axis=0
    )


def triangle(transposed):
    a = lax.broadcasted_iota(jnp.int32, (Q, Q), 0)
    b = lax.broadcasted_iota(jnp.int32, (Q, Q), 1)
    return jnp.where(a >= b if transposed else a <= b, 1.0, 0.0).astype(F32)


def state_kernel(
    raw, squares, bias, a_log, inner, writers, readers, steps, logs, enter, payload
):
    scale = lax.rsqrt(squares[0:1, :] * (1.0 / 4096) + 1e-05)
    inner[...] = (raw[:512] * scale).astype(BF16)
    writers[...] = (raw[512:640] * scale).astype(BF16)
    readers[...] = (raw[640:768] * scale).astype(BF16)
    before = raw[768:776] * scale + bias[:, :1]
    step = jnp.maximum(before, 0.0) + jnp.log1p(jnp.exp(-jnp.abs(before)))
    log = -jnp.exp(a_log[:, :1]) * step
    steps[...] = step
    logs[...] = log
    upper = triangle(False)
    count = raw.shape[1] // Q
    state = jnp.zeros((512, STATE), F32)
    whole = jnp.zeros((8, 1), F32)
    for n in range(count):
        lanes = slice(n * Q, (n + 1) * Q)
        cumul = dot(log[:, lanes], upper, 1, 0, highest)
        total = cumul[:, Q - 1 : Q]
        enter[n] = state.astype(BF16)
        left = over_heads(step[:, lanes] * jnp.exp(total - cumul), Q)
        scaled = (inner[:, lanes].astype(F32) * left).astype(BF16)
        fresh = dot(scaled, writers[:, lanes], 1, 1)
        state = state * over_heads(jnp.broadcast_to(jnp.exp(total), (8, STATE)), STATE) + fresh
        whole = whole + total
    for part in range(4):
        payload[part, pl.ds(0, 128), :] = state[128 * part : 128 * (part + 1)]
        for j in range(2):
            row = 2 * part + j
            payload[part, pl.ds(128 + 8 * j, 8), :] = jnp.broadcast_to(
                jnp.exp(whole[row : row + 1]), (8, STATE)
            )


def local_states(raw, squares, bias, a_log):
    tokens = raw.shape[1]
    return pl.pallas_call(
        state_kernel,
        in_specs=[VMEM_SPEC] * 4,
        out_specs=(VMEM_SPEC,) * 7,
        out_shape=(
            jax.ShapeDtypeStruct((512, tokens), BF16),
            jax.ShapeDtypeStruct((STATE, tokens), BF16),
            jax.ShapeDtypeStruct((STATE, tokens), BF16),
            jax.ShapeDtypeStruct((8, tokens), F32),
            jax.ShapeDtypeStruct((8, tokens), F32),
            jax.ShapeDtypeStruct((tokens // Q, 512, STATE), BF16),
            jax.ShapeDtypeStruct((4, 144, STATE), F32),
        ),
        compiler_params=params(16),
        name="states",
    )(raw, squares, bias, a_log)


def within_kernel(inner, writers, readers, steps, logs, enter, d_skip, out, begun):
    upper, lower = triangle(False), triangle(True)
    causal = upper > 0.0
    whole = jnp.zeros((8, 1), F32)
    for n in range(inner.shape[1] // Q):
        lanes = slice(n * Q, (n + 1) * Q)
        log = logs[:, lanes]
        cumul = dot(log, upper, 1, 0, highest)
        column = dot(lower, log, 1, 1, highest)
        begun[:, lanes] = cumul + whole
        whole = whole + cumul[:, Q - 1 : Q]
        meets = dot(writers[:, lanes], readers[:, lanes], 0, 0)
        carried = dot(enter[n], readers[:, lanes], 1, 0)
        grown = jnp.exp(cumul)
        step = steps[:, lanes]
        for h in range(8):
            span = slice(h * HDIM, (h + 1) * HDIM)
            apart = jnp.minimum(cumul[h : h + 1] - column[:, h : h + 1], 0.0)
            mixing = jnp.where(causal, meets * jnp.exp(apart), 0.0).astype(BF16)
            own = inner[span, lanes].astype(F32)
            scaled = (own * step[h : h + 1]).astype(BF16)
            out[span, lanes] = (
                dot(scaled, mixing, 1, 0)
                + carried[span] * grown[h : h + 1]
                + d_skip[span] * own
            )


def within(inner, writers, readers, steps, logs, enter, d_skip):
    tokens = inner.shape[1]
    return pl.pallas_call(
        within_kernel,
        in_specs=[VMEM_SPEC] * 7,
        out_specs=(VMEM_SPEC,) * 2,
        out_shape=(
            jax.ShapeDtypeStruct((512, tokens), F32),
            jax.ShapeDtypeStruct((8, tokens), F32),
        ),
        compiler_params=params(16),
        cost_estimate=pl.CostEstimate(
            flops=6_000_000_000, bytes_accessed=6_000_000, transcendentals=2_000_000
        ),
        name="within",
    )(inner, writers, readers, steps, logs, enter, d_skip)


def finish_kernel(place, local, begun, readers, *refs):
    gain, out, state = refs[4:]
    for k in range(4):
        rows = pl.ds(pl.multiple_of(lax.rem(place[1] + 4 - k, 4) * 128, 128), 128)
        state[rows, :] = refs[k][...]
    for n in range(local.shape[1] // Q):
        lanes = slice(n * Q, (n + 1) * Q)
        carried = dot(state[...], readers[:, lanes], 1, 0)
        y = local[:, lanes] + carried * over_heads(jnp.exp(begun[:, lanes]), Q)
        mean = jnp.sum(y * y, axis=0, keepdims=True) * (1.0 / 512)
        y = y * lax.rsqrt(mean + 1e-05) * gain[...]
        out[lanes, :] = y.T.astype(BF16)


def finish(place, local, begun, readers, states, gain):
    return pl.pallas_call(
        finish_kernel,
        in_specs=[SMEM_SPEC] + [VMEM_SPEC] * 8,
        out_specs=VMEM_SPEC,
        out_shape=jax.ShapeDtypeStruct((local.shape[1], 512), BF16),
        scratch_shapes=[pltpu.VMEM((512, STATE), BF16)],
        compiler_params=params(16),
        name="finish",
    )(place, local, begun, readers, *states, gain)


def two_heads(decays):
    return jnp.concatenate(
        [jnp.broadcast_to(decays[8 * j : 8 * j + 1], (HDIM, STATE)) for j in range(2)], axis=0
    )


def prefix_kernel(size, slot, place, *refs):
    got, (before, total, held) = refs[:size], refs[size:]
    for k in range(size):
        held[lax.rem(place[slot] + size - k, size)] = got[k][...].astype(F32)
    state, decay = jnp.zeros((128, STATE), F32), jnp.ones((16, STATE), F32)
    for i in range(size):
        before[i, pl.ds(0, 128), :] = state
        before[i, pl.ds(128, 16), :] = decay
        left = held[i, pl.ds(128, 16), :]
        state = state * two_heads(left) + held[i, pl.ds(0, 128), :]
        decay = decay * left
    total[...] = jnp.concatenate([state, decay], axis=0).astype(BF16)


def prefix(place, slot, got):
    size = len(got)
    return pl.pallas_call(
        functools.partial(prefix_kernel, size, slot),
        in_specs=[SMEM_SPEC] + [VMEM_SPEC] * size,
        out_specs=(VMEM_SPEC, VMEM_SPEC),
        out_shape=(
            jax.ShapeDtypeStruct((size, 144, STATE), F32),
            jax.ShapeDtypeStruct((144, STATE), BF16),
        ),
        scratch_shapes=[pltpu.VMEM((size, 144, STATE), F32)],
        compiler_params=params(4),
        name="prefix",
    )(place, *got)


def join_kernel(place, in_row, in_plane, plane, out):
    y = place[2]
    begun = jnp.where(place[4] > 0, plane[pl.ds(0, 128), :].astype(F32), 0.0)
    begun = in_plane[y, pl.ds(0, 128), :] + two_heads(in_plane[y, pl.ds(128, 16), :]) * begun
    for i in range(4):
        made = in_row[i, pl.ds(0, 128), :] + two_heads(in_row[i, pl.ds(128, 16), :]) * begun
        out[i] = made.astype(BF16)


def join(place, in_row, in_plane, plane):
    return pl.pallas_call(
        join_kernel,
        in_specs=[SMEM_SPEC] + [VMEM_SPEC] * 3,
        out_specs=VMEM_SPEC,
        out_shape=jax.ShapeDtypeStruct((4, 128, STATE), BF16),
        compiler_params=params(4),
        name="join",
    )(place, in_row, in_plane, plane)


def on_device(
    patches, grid_rows, frame_ids, ln_gain, w_qkv, w_out, w_conn, norm_gain,
    w_x, w_b, w_c, w_dt, dt_bias, a_log, d_skip, out_gain,
):
    core, x, y, zl, zh = (lax.axis_index(a) for a in ("c", "x", "y", "zl", "zh"))
    place = jnp.stack([core, x, y, zl, zh]).astype(jnp.int32)
    pool = (
        jnp.where(jnp.arange(256)[:, None] // POOL == jnp.arange(64)[None, :], 1.0 / POOL, 0.0)
    ).astype(BF16)

    block = jnp.concatenate([jnp.transpose(w_qkv, (0, 2, 1)), w_out[None]], axis=0)
    piece = jnp.concatenate(
        [
            lax.dynamic_slice(block, (x, 0, 0), (1, 144, XW)),
            lax.dynamic_slice(block, (y, 0, XW), (1, 144, 1152 - XW)),
        ],
        axis=2,
    )
    along = [ring_shift(piece, "zl", 4, k) for k in (1, 2, 3)]

    block_x, block_y = split_pieces([p[0] for p in along])
    some = lax.dynamic_slice(w_conn, ((y * 4 + x) * 72, 0), (72, 512))
    some = jnp.concatenate([some[:, :256], some[:, 256:]], axis=0)
    turned = jnp.transpose(patches, (0, 2, 1)).reshape(4, 432, 256)
    turned = jnp.concatenate([turned, jnp.broadcast_to(some[None], (4, 144, 256))], axis=1)
    own_frames = lax.dynamic_slice(grid_rows, (zl * 3,), (3,))
    block = block.reshape(4, 3, 48, 1152)
    gain = ln_gain[:, None]
    wide_gain = norm_gain[None]
    (turned, block_x, block_y, block, gain, wide_gain, pool, place, own_frames) = (
        lax.optimization_barrier(
            (turned, block_x, block_y, block, gain, wide_gain, pool, place, own_frames)
        )
    )
    whole_x = lax.all_gather(block_x, "x", axis=0)

    own = spread_out(lambda i: lax.dynamic_index_in_dim(turned, i, 0, False), "zl", 4)
    ring_y, own = gather_ring(block_y, "y", own)
    own = jnp.stack(own)
    other = swap_core(own)
    normed, residual, product = norm_frames(
        place, own, other, gain, pool, wide_gain, w_dt.T, w_x, w_b, w_c
    )
    product, _ = lax.optimization_barrier((product, (whole_x, ring_y)))
    wide = lax.all_gather(product, ("y", "x"), axis=0, tiled=True)

    keep, give = vision(place, own_frames, normed, pool, block, whole_x, ring_y)
    summed = keep + residual + swap_core(give)
    token = jnp.arange(128) % 64
    kept = token[None, :] * POOL < (own_frames * GRID)[:, None]
    seen = jnp.where(kept[None, :, None, :], summed, 0.0).astype(BF16)
    seen = spread_out(lambda i: lax.dynamic_index_in_dim(seen, i, 0, False), "zl", 4)

    outgoing = bucket(place, frame_ids, seen)
    incoming = lax.all_to_all(
        outgoing, ("zh", "y", "x"), split_axis=0, concat_axis=0, tiled=True
    )
    own_features = place_frames(incoming)
    line = lax.all_gather(own_features, "zl", axis=0, tiled=True)
    stream, raw, squares = stream_rows(place, line, swap_core(line), w_conn, wide)
    squares = squares + swap_core(squares)
    squares = squares + sum(ring_shift(squares, "zl", 4, k) for k in (1, 2, 3))

    def column(values, repeat):
        return jnp.broadcast_to(values[:, None], (values.shape[0], repeat))

    inner, writers, readers, steps, logs, enter, payload = local_states(
        raw, squares, column(dt_bias, 128), column(a_log, 128)
    )
    local, begun = within(
        inner, writers, readers, steps, logs, enter, jnp.repeat(d_skip, HDIM)[:, None]
    )
    sent = payload.astype(BF16)
    in_row, row = prefix(
        place, 1, spread_out(lambda i: lax.dynamic_index_in_dim(sent, i, 0, False), "x", 4)
    )
    in_plane, plane = prefix(place, 2, spread_out(lambda i: row, "y", 4))
    states = join(place, in_row, in_plane, ring_shift(plane, "zh", 2, 1))
    states = spread_out(lambda i: lax.dynamic_index_in_dim(states, i, 0, False), "x", 4)
    mixed = finish(place, local, begun, readers, states, out_gain[:, None])
    return stream, mixed


def solution(mesh):
    fine = Mesh(mesh.devices.reshape(2, 4, 4, 4, 2), ("zh", "y", "x", "zl", "c"))
    tm, head = ("zh", "y", "x"), ("zl", "c")
    in_specs = (
        P(tm, None, head),
        P(tm),
        P(tm),
        P(),
        P(None, None, head),
        P(head, None),
        P(None, head),
        P(),
        P(None, head),
        P(None, head),
        P(None, head),
        P(None, head),
        P(head),
        P(head),
        P(head),
        P(head),
    )
    out_specs = (P(tm, head), P(tm, head))
    return jax.shard_map(
        on_device, mesh=fine, in_specs=in_specs, out_specs=out_specs, check_vma=False
    )
```

```python
import functools
import jax
import jax.numpy as jnp
from jax import lax
from jax.experimental import pallas as pl
from jax.experimental.pallas import tpu as pltpu
from jax.sharding import Mesh, PartitionSpec as P

GRID = 16
POOL = 4
VHD = 72
HDIM = 64
STATE = 128
Q = 256
XW = 512

F32 = jnp.float32
BF16 = jnp.bfloat16
highest = lax.Precision.HIGHEST
VMEM_SPEC = pl.BlockSpec(memory_space=pltpu.VMEM)
SMEM_SPEC = pl.BlockSpec(memory_space=pltpu.SMEM)
ANY_SPEC = pl.BlockSpec(memory_space=pl.ANY)


def params(mib):
    return pltpu.CompilerParams(vmem_limit_bytes=mib * 2**20)


def dot(a, b, ca, cb, precision=None):
    return lax.dot_general(
        a, b, (((ca,), (cb,)), ((), ())), preferred_element_type=F32, precision=precision
    )


def ring_shift(value, axis, size, shift):
    return lax.ppermute(value, axis, [(i, (i + shift) % size) for i in range(size)])


def swap_core(value):
    return lax.ppermute(value, "c", [(0, 1), (1, 0)])


def spread_out(parts, axis, size):
    position = lax.axis_index(axis)
    own = parts(position)
    return [own] + [
        ring_shift(parts(lax.rem(position + k, size)), axis, size, k) for k in range(1, size)
    ]


def norm_kernel(
    place, own, other, gain, pool, wide_gain, w_dt, w_x, w_b, w_c,
    normed, residual, product, x, big_x, big_b, big_c, sems,
):
    copies = [
        pltpu.make_async_copy(source, held, sems.at[n])
        for n, (source, held) in enumerate(((w_x, big_x), (w_b, big_b), (w_c, big_c)))
    ]
    for copy in copies:
        copy.start()
    first = place[0] == 0
    for f in range(3):
        frame = pl.ds(144 * f, 144)
        for z in range(4):
            k = lax.rem(place[3] + 4 - z, 4)
            mine = own[k, frame, :]
            a, b = mine.astype(F32), other[k, frame, :].astype(F32)
            x[pl.ds(288 * z, 144), :] = jnp.where(first, a, b)
            x[pl.ds(288 * z + 144, 144), :] = jnp.where(first, b, a)
            pooled = dot(mine, pool[...], 1, 0)
            residual[z, f] = jnp.concatenate([pooled[:72], pooled[72:]], axis=1)
        values = x[...]
        width = values.shape[0]
        centre = jnp.sum(values, axis=0, keepdims=True) * (1.0 / width)
        values = values - centre
        spread = jnp.sum(values * values, axis=0, keepdims=True) * (1.0 / width)
        normed[f] = (values * lax.rsqrt(spread + 1e-06) * gain[...]).astype(BF16)
    for copy in copies:
        copy.wait()
    sums = [jnp.zeros((144, width), F32) for width in (512, 128, 128, 8)]
    rows = pl.ds(432, 144)
    for z in range(4):
        k = lax.rem(place[3] + 4 - z, 4)
        a, b = own[k, rows, :].astype(F32), other[k, rows, :].astype(F32)
        for i, part in ((2 * z, jnp.where(first, a, b)), (2 * z + 1, jnp.where(first, b, a))):
            span = pl.ds(512 * i, 512)
            part = jnp.concatenate([part[:72], part[72:]], axis=1) * wide_gain[:, span]
            high = part.astype(BF16).astype(F32)
            both = jnp.concatenate([high, part - high], axis=0).astype(BF16)
            made = [dot(both, w[span, :], 1, 0) for w in (big_x, big_b, big_c)]
            made.append(dot(both, w_dt[:, span], 1, 1))
            sums = [total + extra for total, extra in zip(sums, made)]
    product[...] = jnp.zeros_like(product)
    begun = 0
    for total in sums:
        width = total.shape[1]
        product[:, pl.ds(begun, width)] = (total[:72] + total[72:]).astype(BF16)
        begun += width


def norm_frames(place, own, other, ln_gain, pool, wide_gain, w_dt, w_x, w_b, w_c):
    return pl.pallas_call(
        norm_kernel,
        in_specs=[SMEM_SPEC] + [VMEM_SPEC] * 6 + [ANY_SPEC] * 3,
        out_specs=(VMEM_SPEC, VMEM_SPEC, VMEM_SPEC),
        out_shape=(
            jax.ShapeDtypeStruct((3, 1152, 256), BF16),
            jax.ShapeDtypeStruct((4, 3, 72, 128), F32),
            jax.ShapeDtypeStruct((72, 896), BF16),
        ),
        scratch_shapes=[
            pltpu.VMEM((1152, 256), F32),
            pltpu.VMEM(w_x.shape, BF16),
            pltpu.VMEM(w_b.shape, BF16),
            pltpu.VMEM(w_c.shape, BF16),
            pltpu.SemaphoreType.DMA((3,)),
        ],
        compiler_params=params(56),
        name="norm",
    )(place, own, other, ln_gain, pool, wide_gain, w_dt, w_x, w_b, w_c)


def vision_kernel(place, rows, normed, pool, block, *rest):
    ring = rest[:4]
    keep, give, wx, wy, qkv, ctx, scores, powered, sems = rest[4:]
    frame = pl.program_id(0)
    first = place[0] == 0

    def copies():
        pairs = [
            (block.at[:, :, :, pl.ds(0, XW)], wx.at[:, pl.ds(0, 3)]),
            (block.at[:, :, :, pl.ds(XW, 1152 - XW)], wy.at[:, pl.ds(0, 3)]),
        ]
        for source, ahead in zip(ring, (0, 3, 1, 2)):
            index = lax.rem(place[5] + ahead, 4)
            rows = pl.ds(3, 9)
            pairs.append((source.at[:, :, pl.ds(0, XW)], wx.at[index, rows]))
            pairs.append((source.at[:, :, pl.ds(XW, 1152 - XW)], wy.at[index, rows]))
        return [
            pltpu.make_async_copy(source, held, sems.at[n])
            for n, (source, held) in enumerate(pairs)
        ]

    @pl.when(frame == 0)
    def _():
        for copy in copies():
            copy.start()
        for copy in copies():
            copy.wait()

    width = normed.shape[1]
    for m in range(3):
        left = wx[m].reshape(576, XW)
        right = wy[m].reshape(576, width - XW)
        qkv[m] = dot(left, normed[0, :XW], 1, 0) + dot(right, normed[0, XW:], 1, 0)
    valid = rows[frame] * GRID
    usable = lax.broadcasted_iota(jnp.int32, (256, 256), 0) < valid
    for h in range(8):
        span = pl.ds(h * VHD, VHD)
        q, k = (qkv[m, span, :].astype(BF16) for m in range(2))
        scores[h] = dot(k, q, 0, 0)
    shares = []
    for h in range(8):
        values = jnp.where(usable, scores[h], -1e30)
        top = jnp.max(values, axis=0, keepdims=True)
        values = jnp.exp((values - top) * VHD ** (-0.5))
        shares.append(1.0 / jnp.sum(values, axis=0, keepdims=True))
        powered[h] = values.astype(BF16)
    for h in range(8):
        span = pl.ds(h * VHD, VHD)
        ctx[span, :] = dot(qkv[2, span, :].astype(BF16), powered[h], 1, 0) * shares[h]
    pooled = dot(ctx[...].astype(BF16), pool[...], 1, 0)
    high = pooled.astype(BF16)
    low = (pooled - high.astype(F32)).astype(BF16)
    both = jnp.concatenate([high, low], axis=1)
    out_x = dot(both, wx[3].reshape(576, XW), 0, 0)
    out_y = dot(both, wy[3].reshape(576, width - XW), 0, 0)
    attended = jnp.concatenate([out_x, out_y], axis=1)
    attended = (attended[:64] + attended[64:]).T
    for z in range(4):
        a = attended[(2 * z) * 144 : (2 * z + 1) * 144]
        b = attended[(2 * z + 1) * 144 : (2 * z + 2) * 144]
        own = jnp.where(first, a, b)
        far = jnp.where(first, b, a)
        keep[z, 0] = jnp.concatenate([own[:72], own[72:]], axis=1)
        give[z, 0] = jnp.concatenate([far[:72], far[72:]], axis=1)


def vision(place, rows, normed, pool, block, ring):
    out = pl.BlockSpec((4, 1, 72, 128), lambda f: (0, f, 0, 0))
    shape = jax.ShapeDtypeStruct((4, 3, 72, 128), F32)
    return pl.pallas_call(
        vision_kernel,
        grid=(3,),
        in_specs=[
            SMEM_SPEC,
            SMEM_SPEC,
            pl.BlockSpec((1, 1152, 256), lambda f: (f, 0, 0)),
            VMEM_SPEC,
        ]
        + [ANY_SPEC] * 5,
        out_specs=(out, out),
        out_shape=(shape, shape),
        scratch_shapes=[
            pltpu.VMEM((4, 12, 48, XW), BF16),
            pltpu.VMEM((4, 12, 48, 1152 - XW), BF16),
            pltpu.VMEM((3, 576, 256), F32),
            pltpu.VMEM((576, 256), F32),
            pltpu.VMEM((8, 256, 256), F32),
            pltpu.VMEM((8, 256, 256), BF16),
            pltpu.SemaphoreType.DMA((10,)),
        ],
        compiler_params=params(56),
        name="vision",
    )(place, rows, normed, pool, block, *ring)


def bucket_kernel(place, ids, *refs):
    out = refs[4]
    out[...] = jnp.zeros_like(out)
    for k in range(4):
        z = lax.rem(place[3] + 4 - k, 4)
        for j in range(3):
            frame = ids[3 * z + j]
            spot = lax.rem(frame, 12) + 1
            label = jnp.zeros((8, 128), F32) + spot.astype(F32)
            whole = jnp.concatenate([refs[k][j].astype(F32), label], axis=0)
            out[lax.div(frame, 12)] = whole.astype(BF16)


def bucket(place, ids, seen):
    return pl.pallas_call(
        bucket_kernel,
        in_specs=[SMEM_SPEC, SMEM_SPEC] + [VMEM_SPEC] * 4,
        out_specs=VMEM_SPEC,
        out_shape=jax.ShapeDtypeStruct((32, 80, 128), BF16),
        compiler_params=params(16),
        name="bucket",
    )(place, ids, *seen)


def place_kernel(incoming, out, held):
    held[...] = incoming[...].astype(F32)
    left = lax.broadcasted_iota(jnp.int32, (72, 128), 1) < 64

    def frame(p):
        found = jnp.zeros((72, 128), F32)
        for s in range(32):
            here = held[s, pl.ds(72, 1), :] == float(p + 1)
            found = jnp.where(here, held[s, pl.ds(0, 72), :], found)
        return found

    for pair in range(6):
        a, b = frame(2 * pair), frame(2 * pair + 1)
        lanes = pl.ds(128 * pair, 128)
        top = jnp.where(left, a, pltpu.roll(b, 64, 1))
        bottom = jnp.where(left, pltpu.roll(a, 64, 1), b)
        out[:, lanes] = jnp.concatenate([top, bottom], axis=0).astype(BF16)


def place_frames(incoming):
    return pl.pallas_call(
        place_kernel,
        in_specs=[VMEM_SPEC],
        out_specs=VMEM_SPEC,
        out_shape=jax.ShapeDtypeStruct((144, 768), BF16),
        scratch_shapes=[pltpu.VMEM((32, 80, 128), F32)],
        compiler_params=params(16),
        name="place",
    )(incoming)


def stream_kernel(place, mine, other, w_conn, *rest):
    pieces = rest[:5]
    stream, raw, squares, seen, wide, conn, held, sems = rest[5:]
    copies = [pltpu.make_async_copy(w_conn, conn, sems.at[0])]
    for n, (k, lo, size) in enumerate(
        ((0, 0, 288), (1, 0, 288), (2, 0, 144), (2, 144, 144), (3, 0, 288))
    ):
        begun = pl.multiple_of(lax.rem(place[2] + 4 - k, 4) * 288 + lo, 144)
        held_rows = wide.at[pl.ds(begun, size)]
        copies.append(pltpu.make_async_copy(pieces[n], held_rows, sems.at[n + 1]))
    for copy in copies:
        copy.start()
    first = place[0] == 0
    for z in range(4):
        a, b = mine[pl.ds(144 * z, 144), :], other[pl.ds(144 * z, 144), :]
        seen[pl.ds(288 * z, 144), :] = jnp.where(first, a, b)
        seen[pl.ds(288 * z + 144, 144), :] = jnp.where(first, b, a)
    for copy in copies:
        copy.wait()
    held[pl.ds(0, 768), :] = dot(wide[:, pl.ds(0, 768)], seen[...], 0, 0)
    held[pl.ds(768, 8), :] = dot(wide[:, pl.ds(768, 128)], seen[...], 0, 0)[:8]
    out = pltpu.make_async_copy(held, raw, sems.at[6])
    out.start()
    made = dot(conn[...], seen[...], 0, 0).astype(BF16)
    values = made.astype(F32)
    squares[...] = jnp.broadcast_to(
        jnp.sum(values * values, axis=0, keepdims=True), squares.shape
    )
    stream[...] = values.T.astype(BF16)
    out.wait()


def stream_rows(place, mine, other, w_conn, wide):
    tokens, width = mine.shape[1], w_conn.shape[1]
    return pl.pallas_call(
        stream_kernel,
        in_specs=[SMEM_SPEC] + [VMEM_SPEC] * 2 + [ANY_SPEC] * 6,
        out_specs=(VMEM_SPEC, ANY_SPEC, VMEM_SPEC),
        out_shape=(
            jax.ShapeDtypeStruct((tokens, width), BF16),
            jax.ShapeDtypeStruct((776, tokens), F32),
            jax.ShapeDtypeStruct((8, tokens), F32),
        ),
        scratch_shapes=[
            pltpu.VMEM((1152, tokens), BF16),
            pltpu.VMEM((1152, 896), BF16),
            pltpu.VMEM(w_conn.shape, BF16),
            pltpu.VMEM((776, tokens), F32),
            pltpu.SemaphoreType.DMA((7,)),
        ],
        compiler_params=params(52),
        name="stream",
    )(place, mine, other, w_conn, *wide)


def over_heads(rows, length):
    return jnp.concatenate(
        [jnp.broadcast_to(rows[h : h + 1], (HDIM, length)) for h in range(8)], axis=0
    )


def triangle(transposed):
    a = lax.broadcasted_iota(jnp.int32, (Q, Q), 0)
    b = lax.broadcasted_iota(jnp.int32, (Q, Q), 1)
    return jnp.where(a >= b if transposed else a <= b, 1.0, 0.0).astype(F32)


def state_kernel(
    raw, squares, bias, a_log, inner, writers, readers, steps, logs, enter, payload
):
    scale = lax.rsqrt(squares[0:1, :] * (1.0 / 4096) + 1e-05)
    inner[...] = (raw[:512] * scale).astype(BF16)
    writers[...] = (raw[512:640] * scale).astype(BF16)
    readers[...] = (raw[640:768] * scale).astype(BF16)
    before = raw[768:776] * scale + bias[:, :1]
    step = jnp.maximum(before, 0.0) + jnp.log1p(jnp.exp(-jnp.abs(before)))
    log = -jnp.exp(a_log[:, :1]) * step
    steps[...] = step
    logs[...] = log
    upper = triangle(False)
    count = raw.shape[1] // Q
    state = jnp.zeros((512, STATE), F32)
    whole = jnp.zeros((8, 1), F32)
    for n in range(count):
        lanes = slice(n * Q, (n + 1) * Q)
        cumul = dot(log[:, lanes], upper, 1, 0, highest)
        total = cumul[:, Q - 1 : Q]
        enter[n] = state.astype(BF16)
        left = over_heads(step[:, lanes] * jnp.exp(total - cumul), Q)
        scaled = (inner[:, lanes].astype(F32) * left).astype(BF16)
        fresh = dot(scaled, writers[:, lanes], 1, 1)
        state = state * over_heads(jnp.broadcast_to(jnp.exp(total), (8, STATE)), STATE) + fresh
        whole = whole + total
    for part in range(4):
        payload[part, pl.ds(0, 128), :] = state[128 * part : 128 * (part + 1)]
        for j in range(2):
            row = 2 * part + j
            payload[part, pl.ds(128 + 8 * j, 8), :] = jnp.broadcast_to(
                jnp.exp(whole[row : row + 1]), (8, STATE)
            )


def local_states(raw, squares, bias, a_log):
    tokens = raw.shape[1]
    return pl.pallas_call(
        state_kernel,
        in_specs=[VMEM_SPEC] * 4,
        out_specs=(VMEM_SPEC,) * 7,
        out_shape=(
            jax.ShapeDtypeStruct((512, tokens), BF16),
            jax.ShapeDtypeStruct((STATE, tokens), BF16),
            jax.ShapeDtypeStruct((STATE, tokens), BF16),
            jax.ShapeDtypeStruct((8, tokens), F32),
            jax.ShapeDtypeStruct((8, tokens), F32),
            jax.ShapeDtypeStruct((tokens // Q, 512, STATE), BF16),
            jax.ShapeDtypeStruct((4, 144, STATE), F32),
        ),
        compiler_params=params(16),
        name="states",
    )(raw, squares, bias, a_log)


def within_kernel(inner, writers, readers, steps, logs, enter, d_skip, out, begun):
    upper, lower = triangle(False), triangle(True)
    causal = upper > 0.0
    whole = jnp.zeros((8, 1), F32)
    for n in range(inner.shape[1] // Q):
        lanes = slice(n * Q, (n + 1) * Q)
        log = logs[:, lanes]
        cumul = dot(log, upper, 1, 0, highest)
        column = dot(lower, log, 1, 1, highest)
        begun[:, lanes] = cumul + whole
        whole = whole + cumul[:, Q - 1 : Q]
        meets = dot(writers[:, lanes], readers[:, lanes], 0, 0)
        carried = dot(enter[n], readers[:, lanes], 1, 0)
        grown = jnp.exp(cumul)
        step = steps[:, lanes]
        for h in range(8):
            span = slice(h * HDIM, (h + 1) * HDIM)
            apart = jnp.minimum(cumul[h : h + 1] - column[:, h : h + 1], 0.0)
            mixing = jnp.where(causal, meets * jnp.exp(apart), 0.0).astype(BF16)
            own = inner[span, lanes].astype(F32)
            scaled = (own * step[h : h + 1]).astype(BF16)
            out[span, lanes] = (
                dot(scaled, mixing, 1, 0)
                + carried[span] * grown[h : h + 1]
                + d_skip[span] * own
            )


def within(inner, writers, readers, steps, logs, enter, d_skip):
    tokens = inner.shape[1]
    return pl.pallas_call(
        within_kernel,
        in_specs=[VMEM_SPEC] * 7,
        out_specs=(VMEM_SPEC,) * 2,
        out_shape=(
            jax.ShapeDtypeStruct((512, tokens), F32),
            jax.ShapeDtypeStruct((8, tokens), F32),
        ),
        compiler_params=params(16),
        cost_estimate=pl.CostEstimate(
            flops=6_000_000_000, bytes_accessed=6_000_000, transcendentals=2_000_000
        ),
        name="within",
    )(inner, writers, readers, steps, logs, enter, d_skip)


def finish_kernel(place, local, begun, readers, *refs):
    gain, out, state = refs[4:]
    for k in range(4):
        rows = pl.ds(pl.multiple_of(lax.rem(place[1] + 4 - k, 4) * 128, 128), 128)
        state[rows, :] = refs[k][...]
    for n in range(local.shape[1] // Q):
        lanes = slice(n * Q, (n + 1) * Q)
        carried = dot(state[...], readers[:, lanes], 1, 0)
        y = local[:, lanes] + carried * over_heads(jnp.exp(begun[:, lanes]), Q)
        mean = jnp.sum(y * y, axis=0, keepdims=True) * (1.0 / 512)
        y = y * lax.rsqrt(mean + 1e-05) * gain[...]
        out[lanes, :] = y.T.astype(BF16)


def finish(place, local, begun, readers, states, gain):
    return pl.pallas_call(
        finish_kernel,
        in_specs=[SMEM_SPEC] + [VMEM_SPEC] * 8,
        out_specs=VMEM_SPEC,
        out_shape=jax.ShapeDtypeStruct((local.shape[1], 512), BF16),
        scratch_shapes=[pltpu.VMEM((512, STATE), BF16)],
        compiler_params=params(16),
        name="finish",
    )(place, local, begun, readers, *states, gain)


def two_heads(decays):
    return jnp.concatenate(
        [jnp.broadcast_to(decays[8 * j : 8 * j + 1], (HDIM, STATE)) for j in range(2)], axis=0
    )


def prefix_kernel(size, slot, place, *refs):
    got, (before, total, held) = refs[:size], refs[size:]
    for k in range(size):
        held[lax.rem(place[slot] + size - k, size)] = got[k][...].astype(F32)
    state, decay = jnp.zeros((128, STATE), F32), jnp.ones((16, STATE), F32)
    for i in range(size):
        before[i, pl.ds(0, 128), :] = state
        before[i, pl.ds(128, 16), :] = decay
        left = held[i, pl.ds(128, 16), :]
        state = state * two_heads(left) + held[i, pl.ds(0, 128), :]
        decay = decay * left
    total[...] = jnp.concatenate([state, decay], axis=0).astype(BF16)


def prefix(place, slot, got):
    size = len(got)
    return pl.pallas_call(
        functools.partial(prefix_kernel, size, slot),
        in_specs=[SMEM_SPEC] + [VMEM_SPEC] * size,
        out_specs=(VMEM_SPEC, VMEM_SPEC),
        out_shape=(
            jax.ShapeDtypeStruct((size, 144, STATE), F32),
            jax.ShapeDtypeStruct((144, STATE), BF16),
        ),
        scratch_shapes=[pltpu.VMEM((size, 144, STATE), F32)],
        compiler_params=params(4),
        name="prefix",
    )(place, *got)


def join_kernel(place, in_row, in_plane, plane, out):
    y = place[2]
    begun = jnp.where(place[4] > 0, plane[pl.ds(0, 128), :].astype(F32), 0.0)
    begun = in_plane[y, pl.ds(0, 128), :] + two_heads(in_plane[y, pl.ds(128, 16), :]) * begun
    for i in range(4):
        made = in_row[i, pl.ds(0, 128), :] + two_heads(in_row[i, pl.ds(128, 16), :]) * begun
        out[i] = made.astype(BF16)


def join(place, in_row, in_plane, plane):
    return pl.pallas_call(
        join_kernel,
        in_specs=[SMEM_SPEC] + [VMEM_SPEC] * 3,
        out_specs=VMEM_SPEC,
        out_shape=jax.ShapeDtypeStruct((4, 128, STATE), BF16),
        compiler_params=params(4),
        name="join",
    )(place, in_row, in_plane, plane)


def on_device(
    patches, grid_rows, frame_ids, ln_gain, w_qkv, w_out, w_conn, norm_gain,
    w_x, w_b, w_c, w_dt, dt_bias, a_log, d_skip, out_gain,
):
    core, x, y, zl, zh = (lax.axis_index(a) for a in ("c", "x", "y", "zl", "zh"))
    member = lax.rem(x + 2 * lax.rem(y, 2), 4)
    place = jnp.stack([core, x, y, zl, zh, member]).astype(jnp.int32)
    pool = (
        jnp.where(jnp.arange(256)[:, None] // POOL == jnp.arange(64)[None, :], 1.0 / POOL, 0.0)
    ).astype(BF16)

    block = jnp.concatenate([jnp.transpose(w_qkv, (0, 2, 1)), w_out[None]], axis=0)
    piece = lax.dynamic_slice(block, (member, 0, 0), (1, 144, 1152))
    along = [ring_shift(piece, "zl", 4, k).reshape(3, 48, 1152) for k in (1, 2, 3)]
    blocks = jnp.concatenate(along, axis=0)
    some = lax.dynamic_slice(w_conn, ((y * 4 + x) * 72, 0), (72, 512))
    some = jnp.concatenate([some[:, :256], some[:, 256:]], axis=0)
    turned = jnp.transpose(patches, (0, 2, 1)).reshape(4, 432, 256)
    turned = jnp.concatenate([turned, jnp.broadcast_to(some[None], (4, 144, 256))], axis=1)
    own_frames = lax.dynamic_slice(grid_rows, (zl * 3,), (3,))
    block = block.reshape(4, 3, 48, 1152)
    gain = ln_gain[:, None]
    wide_gain = norm_gain[None]
    (turned, blocks, block, gain, wide_gain, pool, place, own_frames) = lax.optimization_barrier(
        (turned, blocks, block, gain, wide_gain, pool, place, own_frames)
    )
    ring = (
        blocks,
        ring_shift(blocks, "x", 4, 1),
        ring_shift(blocks, "x", 4, -1),
        ring_shift(blocks, "y", 4, 1),
    )

    own = spread_out(lambda i: lax.dynamic_index_in_dim(turned, i, 0, False), "zl", 4)
    own, _ = lax.optimization_barrier((own, ring))
    own = jnp.stack(own)
    other = swap_core(own)
    normed, residual, product = norm_frames(
        place, own, other, gain, pool, wide_gain, w_dt.T, w_x, w_b, w_c
    )
    near = [product] + [ring_shift(product, "x", 4, k) for k in (1, 2, 3)]
    rows = []
    for i in range(4):
        away = lax.rem(x + 4 - i, 4)
        found = near[0]
        for k in (1, 2, 3):
            found = jnp.where(away == k, near[k], found)
        rows.append(found)
    near = jnp.concatenate(rows, axis=0)
    before, after = ring_shift(near, "y", 4, 1), ring_shift(near, "y", 4, -1)
    far_lo, far_hi = ring_shift(before[:144], "y", 4, 1), ring_shift(after[144:], "y", 4, -1)
    wide = (near, before, far_lo, far_hi, after)

    keep, give = vision(place, own_frames, normed, pool, block, ring)
    summed = keep + residual + swap_core(give)
    token = jnp.arange(128) % 64
    kept = token[None, :] * POOL < (own_frames * GRID)[:, None]
    seen = jnp.where(kept[None, :, None, :], summed, 0.0).astype(BF16)
    seen = spread_out(lambda i: lax.dynamic_index_in_dim(seen, i, 0, False), "zl", 4)

    seen, _ = lax.optimization_barrier((seen, near))
    outgoing = bucket(place, frame_ids, seen)
    incoming = lax.all_to_all(
        outgoing, ("zh", "y", "x"), split_axis=0, concat_axis=0, tiled=True
    )
    own_features, _ = lax.optimization_barrier((place_frames(incoming), wide))
    line = lax.all_gather(own_features, "zl", axis=0, tiled=True)
    stream, raw, squares = stream_rows(place, line, swap_core(line), w_conn, wide)
    squares = squares + swap_core(squares)
    squares = squares + sum(ring_shift(squares, "zl", 4, k) for k in (1, 2, 3))

    def column(values, repeat):
        return jnp.broadcast_to(values[:, None], (values.shape[0], repeat))

    inner, writers, readers, steps, logs, enter, payload = local_states(
        raw, squares, column(dt_bias, 128), column(a_log, 128)
    )
    local, begun = within(
        inner, writers, readers, steps, logs, enter, jnp.repeat(d_skip, HDIM)[:, None]
    )
    sent = payload.astype(BF16)
    in_row, row = prefix(
        place, 1, spread_out(lambda i: lax.dynamic_index_in_dim(sent, i, 0, False), "x", 4)
    )
    in_plane, plane = prefix(place, 2, spread_out(lambda i: row, "y", 4))
    states = join(place, in_row, in_plane, ring_shift(plane, "zh", 2, 1))
    states = spread_out(lambda i: lax.dynamic_index_in_dim(states, i, 0, False), "x", 4)
    mixed = finish(place, local, begun, readers, states, out_gain[:, None])
    return stream, mixed


def solution(mesh):
    fine = Mesh(mesh.devices.reshape(2, 4, 4, 4, 2), ("zh", "y", "x", "zl", "c"))
    tm, head = ("zh", "y", "x"), ("zl", "c")
    in_specs = (
        P(tm, None, head),
        P(tm),
        P(tm),
        P(),
        P(None, None, head),
        P(head, None),
        P(None, head),
        P(),
        P(None, head),
        P(None, head),
        P(None, head),
        P(None, head),
        P(head),
        P(head),
        P(head),
        P(head),
    )
    out_specs = (P(tm, head), P(tm, head))
    return jax.shard_map(
        on_device, mesh=fine, in_specs=in_specs, out_specs=out_specs, check_vma=False
    )
```

```python
import functools
import jax
import jax.numpy as jnp
from jax import lax
from jax.experimental import pallas as pl
from jax.experimental.pallas import tpu as pltpu
from jax.sharding import Mesh, PartitionSpec as P

GRID = 16
POOL = 4
VHD = 72
HDIM = 64
STATE = 128
Q = 256
XW = 512

F32 = jnp.float32
BF16 = jnp.bfloat16
highest = lax.Precision.HIGHEST
VMEM_SPEC = pl.BlockSpec(memory_space=pltpu.VMEM)
SMEM_SPEC = pl.BlockSpec(memory_space=pltpu.SMEM)
ANY_SPEC = pl.BlockSpec(memory_space=pl.ANY)


def params(mib):
    return pltpu.CompilerParams(vmem_limit_bytes=mib * 2**20)


def dot(a, b, ca, cb, precision=None):
    return lax.dot_general(
        a, b, (((ca,), (cb,)), ((), ())), preferred_element_type=F32, precision=precision
    )


def ring_shift(value, axis, size, shift):
    return lax.ppermute(value, axis, [(i, (i + shift) % size) for i in range(size)])


def swap_core(value):
    return lax.ppermute(value, "c", [(0, 1), (1, 0)])


def spread_out(parts, axis, size):
    position = lax.axis_index(axis)
    own = parts(position)
    return [own] + [
        ring_shift(parts(lax.rem(position + k, size)), axis, size, k) for k in range(1, size)
    ]


def split_kernel(a, b, c, own, blocks, some):
    some[0] = own[...]
    for k, source in enumerate((a, b, c)):
        some[k + 1] = source[:, pl.ds(1152, 256)]
        for third in range(3):
            blocks[3 * k + third] = source[pl.ds(48 * third, 48), pl.ds(0, 1152)]


def split_pieces(pieces, own):
    return pl.pallas_call(
        split_kernel,
        in_specs=[VMEM_SPEC] * 4,
        out_specs=(VMEM_SPEC,) * 2,
        out_shape=(
            jax.ShapeDtypeStruct((9, 48, 1152), BF16),
            jax.ShapeDtypeStruct((4, 144, 256), BF16),
        ),
        compiler_params=params(8),
        name="split",
    )(*pieces, own)


def product_kernel(
    place, own, other, wide_gain, w_dt, w_x, w_b, w_c, product, big_x, big_b, big_c, sems
):
    copies = [
        pltpu.make_async_copy(source, held, sems.at[n])
        for n, (source, held) in enumerate(((w_x, big_x), (w_b, big_b), (w_c, big_c)))
    ]
    for copy in copies:
        copy.start()
    for copy in copies:
        copy.wait()
    first = place[0] == 0
    sums = [jnp.zeros((144, width), F32) for width in (512, 128, 128, 8)]
    for z in range(4):
        k = lax.rem(place[3] + 4 - z, 4)
        a, b = own[k].astype(F32), other[k].astype(F32)
        for i, part in ((2 * z, jnp.where(first, a, b)), (2 * z + 1, jnp.where(first, b, a))):
            span = pl.ds(512 * i, 512)
            part = jnp.concatenate([part[:72], part[72:]], axis=1) * wide_gain[:, span]
            high = part.astype(BF16).astype(F32)
            both = jnp.concatenate([high, part - high], axis=0).astype(BF16)
            made = [dot(both, w[span, :], 1, 0) for w in (big_x, big_b, big_c)]
            made.append(dot(both, w_dt[:, span], 1, 1))
            sums = [total + extra for total, extra in zip(sums, made)]
    product[...] = jnp.zeros_like(product)
    begun = 0
    for total in sums:
        width = total.shape[1]
        product[:, pl.ds(begun, width)] = (total[:72] + total[72:]).astype(BF16)
        begun += width


def weight_product(place, own, other, wide_gain, w_dt, w_x, w_b, w_c):
    return pl.pallas_call(
        product_kernel,
        in_specs=[SMEM_SPEC] + [VMEM_SPEC] * 4 + [ANY_SPEC] * 3,
        out_specs=VMEM_SPEC,
        out_shape=jax.ShapeDtypeStruct((72, 896), BF16),
        scratch_shapes=[
            pltpu.VMEM(w_x.shape, BF16),
            pltpu.VMEM(w_b.shape, BF16),
            pltpu.VMEM(w_c.shape, BF16),
            pltpu.SemaphoreType.DMA((3,)),
        ],
        compiler_params=params(56),
        name="product",
    )(place, own, other, wide_gain, w_dt, w_x, w_b, w_c)


def norm_kernel(place, own, other, gain, pool, normed, residual, x):
    first = place[0] == 0
    for f in range(3):
        frame = pl.ds(144 * f, 144)
        for z in range(4):
            k = lax.rem(place[3] + 4 - z, 4)
            mine = own[k, frame, :]
            a, b = mine.astype(F32), other[k, frame, :].astype(F32)
            x[pl.ds(288 * z, 144), :] = jnp.where(first, a, b)
            x[pl.ds(288 * z + 144, 144), :] = jnp.where(first, b, a)
            pooled = dot(mine, pool[...], 1, 0)
            residual[z, f] = jnp.concatenate([pooled[:72], pooled[72:]], axis=1)
        values = x[...]
        width = values.shape[0]
        centre = jnp.sum(values, axis=0, keepdims=True) * (1.0 / width)
        values = values - centre
        spread = jnp.sum(values * values, axis=0, keepdims=True) * (1.0 / width)
        normed[f] = (values * lax.rsqrt(spread + 1e-06) * gain[...]).astype(BF16)


def norm_frames(place, own, other, ln_gain, pool):
    return pl.pallas_call(
        norm_kernel,
        in_specs=[SMEM_SPEC] + [VMEM_SPEC] * 4,
        out_specs=(VMEM_SPEC, VMEM_SPEC),
        out_shape=(
            jax.ShapeDtypeStruct((3, 1152, 256), BF16),
            jax.ShapeDtypeStruct((4, 3, 72, 128), F32),
        ),
        scratch_shapes=[pltpu.VMEM((1152, 256), F32)],
        compiler_params=params(16),
        name="norm",
    )(place, own, other, ln_gain, pool)


def vision_kernel(place, rows, normed, pool, block, *rest):
    ring = rest[:4]
    keep, give, wx, wy, qkv, ctx, scores, powered, sems = rest[4:]
    frame = pl.program_id(0)
    first = place[0] == 0

    def copies():
        pairs = [
            (block.at[:, :, :, pl.ds(0, XW)], wx.at[:, pl.ds(0, 3)]),
            (block.at[:, :, :, pl.ds(XW, 1152 - XW)], wy.at[:, pl.ds(0, 3)]),
        ]
        for source, ahead in zip(ring, (0, 3, 1, 2)):
            index = lax.rem(place[5] + ahead, 4)
            rows = pl.ds(3, 9)
            pairs.append((source.at[:, :, pl.ds(0, XW)], wx.at[index, rows]))
            pairs.append((source.at[:, :, pl.ds(XW, 1152 - XW)], wy.at[index, rows]))
        return [
            pltpu.make_async_copy(source, held, sems.at[n])
            for n, (source, held) in enumerate(pairs)
        ]

    @pl.when(frame == 0)
    def _():
        for copy in copies():
            copy.start()
        for copy in copies():
            copy.wait()

    width = normed.shape[1]
    for m in range(3):
        left = wx[m].reshape(576, XW)
        right = wy[m].reshape(576, width - XW)
        qkv[m] = dot(left, normed[0, :XW], 1, 0) + dot(right, normed[0, XW:], 1, 0)
    valid = rows[frame] * GRID
    usable = lax.broadcasted_iota(jnp.int32, (256, 256), 0) < valid
    for h in range(8):
        span = pl.ds(h * VHD, VHD)
        q, k = (qkv[m, span, :].astype(BF16) for m in range(2))
        scores[h] = dot(k, q, 0, 0)
    shares = []
    for h in range(8):
        values = jnp.where(usable, scores[h], -1e30)
        top = jnp.max(values, axis=0, keepdims=True)
        values = jnp.exp((values - top) * VHD ** (-0.5))
        shares.append(1.0 / jnp.sum(values, axis=0, keepdims=True))
        powered[h] = values.astype(BF16)
    for h in range(8):
        span = pl.ds(h * VHD, VHD)
        ctx[span, :] = dot(qkv[2, span, :].astype(BF16), powered[h], 1, 0) * shares[h]
    pooled = dot(ctx[...].astype(BF16), pool[...], 1, 0)
    high = pooled.astype(BF16)
    low = (pooled - high.astype(F32)).astype(BF16)
    both = jnp.concatenate([high, low], axis=1)
    out_x = dot(both, wx[3].reshape(576, XW), 0, 0)
    out_y = dot(both, wy[3].reshape(576, width - XW), 0, 0)
    attended = jnp.concatenate([out_x, out_y], axis=1)
    attended = (attended[:64] + attended[64:]).T
    for z in range(4):
        a = attended[(2 * z) * 144 : (2 * z + 1) * 144]
        b = attended[(2 * z + 1) * 144 : (2 * z + 2) * 144]
        own = jnp.where(first, a, b)
        far = jnp.where(first, b, a)
        keep[z, 0] = jnp.concatenate([own[:72], own[72:]], axis=1)
        give[z, 0] = jnp.concatenate([far[:72], far[72:]], axis=1)


def vision(place, rows, normed, pool, block, ring):
    out = pl.BlockSpec((4, 1, 72, 128), lambda f: (0, f, 0, 0))
    shape = jax.ShapeDtypeStruct((4, 3, 72, 128), F32)
    return pl.pallas_call(
        vision_kernel,
        grid=(3,),
        in_specs=[
            SMEM_SPEC,
            SMEM_SPEC,
            pl.BlockSpec((1, 1152, 256), lambda f: (f, 0, 0)),
            VMEM_SPEC,
        ]
        + [ANY_SPEC] * 5,
        out_specs=(out, out),
        out_shape=(shape, shape),
        scratch_shapes=[
            pltpu.VMEM((4, 12, 48, XW), BF16),
            pltpu.VMEM((4, 12, 48, 1152 - XW), BF16),
            pltpu.VMEM((3, 576, 256), F32),
            pltpu.VMEM((576, 256), F32),
            pltpu.VMEM((8, 256, 256), F32),
            pltpu.VMEM((8, 256, 256), BF16),
            pltpu.SemaphoreType.DMA((10,)),
        ],
        compiler_params=params(56),
        name="vision",
    )(place, rows, normed, pool, block, *ring)


def bucket_kernel(place, ids, *refs):
    out = refs[4]
    out[...] = jnp.zeros_like(out)
    for k in range(4):
        z = lax.rem(place[3] + 4 - k, 4)
        for j in range(3):
            frame = ids[3 * z + j]
            spot = lax.rem(frame, 12) + 1
            label = jnp.zeros((8, 128), F32) + spot.astype(F32)
            whole = jnp.concatenate([refs[k][j].astype(F32), label], axis=0)
            out[lax.div(frame, 12)] = whole.astype(BF16)


def bucket(place, ids, seen):
    return pl.pallas_call(
        bucket_kernel,
        in_specs=[SMEM_SPEC, SMEM_SPEC] + [VMEM_SPEC] * 4,
        out_specs=VMEM_SPEC,
        out_shape=jax.ShapeDtypeStruct((32, 80, 128), BF16),
        compiler_params=params(16),
        name="bucket",
    )(place, ids, *seen)


def place_kernel(incoming, out, held):
    held[...] = incoming[...].astype(F32)
    left = lax.broadcasted_iota(jnp.int32, (72, 128), 1) < 64

    def frame(p):
        found = jnp.zeros((72, 128), F32)
        for s in range(32):
            here = held[s, pl.ds(72, 1), :] == float(p + 1)
            found = jnp.where(here, held[s, pl.ds(0, 72), :], found)
        return found

    for pair in range(6):
        a, b = frame(2 * pair), frame(2 * pair + 1)
        lanes = pl.ds(128 * pair, 128)
        top = jnp.where(left, a, pltpu.roll(b, 64, 1))
        bottom = jnp.where(left, pltpu.roll(a, 64, 1), b)
        out[:, lanes] = jnp.concatenate([top, bottom], axis=0).astype(BF16)


def place_frames(incoming):
    return pl.pallas_call(
        place_kernel,
        in_specs=[VMEM_SPEC],
        out_specs=VMEM_SPEC,
        out_shape=jax.ShapeDtypeStruct((144, 768), BF16),
        scratch_shapes=[pltpu.VMEM((32, 80, 128), F32)],
        compiler_params=params(16),
        name="place",
    )(incoming)


def stream_kernel(place, mine, other, w_conn, *rest):
    pieces = rest[:5]
    stream, raw, squares, seen, wide, conn, held, sems = rest[5:]
    copies = [pltpu.make_async_copy(w_conn, conn, sems.at[0])]
    for n, (k, lo, size) in enumerate(
        ((0, 0, 288), (1, 0, 288), (2, 0, 144), (2, 144, 144), (3, 0, 288))
    ):
        begun = pl.multiple_of(lax.rem(place[2] + 4 - k, 4) * 288 + lo, 144)
        held_rows = wide.at[pl.ds(begun, size)]
        copies.append(pltpu.make_async_copy(pieces[n], held_rows, sems.at[n + 1]))
    for copy in copies:
        copy.start()
    first = place[0] == 0
    for z in range(4):
        a, b = mine[pl.ds(144 * z, 144), :], other[pl.ds(144 * z, 144), :]
        seen[pl.ds(288 * z, 144), :] = jnp.where(first, a, b)
        seen[pl.ds(288 * z + 144, 144), :] = jnp.where(first, b, a)
    for copy in copies:
        copy.wait()
    held[pl.ds(0, 768), :] = dot(wide[:, pl.ds(0, 768)], seen[...], 0, 0)
    held[pl.ds(768, 8), :] = dot(wide[:, pl.ds(768, 128)], seen[...], 0, 0)[:8]
    out = pltpu.make_async_copy(held, raw, sems.at[6])
    out.start()
    made = dot(conn[...], seen[...], 0, 0).astype(BF16)
    values = made.astype(F32)
    squares[...] = jnp.broadcast_to(
        jnp.sum(values * values, axis=0, keepdims=True), squares.shape
    )
    stream[...] = values.T.astype(BF16)
    out.wait()


def stream_rows(place, mine, other, w_conn, wide):
    tokens, width = mine.shape[1], w_conn.shape[1]
    return pl.pallas_call(
        stream_kernel,
        in_specs=[SMEM_SPEC] + [VMEM_SPEC] * 2 + [ANY_SPEC] * 6,
        out_specs=(VMEM_SPEC, ANY_SPEC, VMEM_SPEC),
        out_shape=(
            jax.ShapeDtypeStruct((tokens, width), BF16),
            jax.ShapeDtypeStruct((776, tokens), F32),
            jax.ShapeDtypeStruct((8, tokens), F32),
        ),
        scratch_shapes=[
            pltpu.VMEM((1152, tokens), BF16),
            pltpu.VMEM((1152, 896), BF16),
            pltpu.VMEM(w_conn.shape, BF16),
            pltpu.VMEM((776, tokens), F32),
            pltpu.SemaphoreType.DMA((7,)),
        ],
        compiler_params=params(52),
        name="stream",
    )(place, mine, other, w_conn, *wide)


def over_heads(rows, length):
    return jnp.concatenate(
        [jnp.broadcast_to(rows[h : h + 1], (HDIM, length)) for h in range(8)], axis=0
    )


def triangle(transposed):
    a = lax.broadcasted_iota(jnp.int32, (Q, Q), 0)
    b = lax.broadcasted_iota(jnp.int32, (Q, Q), 1)
    return jnp.where(a >= b if transposed else a <= b, 1.0, 0.0).astype(F32)


def state_kernel(
    raw, squares, bias, a_log, inner, writers, readers, steps, logs, enter, payload
):
    scale = lax.rsqrt(squares[0:1, :] * (1.0 / 4096) + 1e-05)
    inner[...] = (raw[:512] * scale).astype(BF16)
    writers[...] = (raw[512:640] * scale).astype(BF16)
    readers[...] = (raw[640:768] * scale).astype(BF16)
    before = raw[768:776] * scale + bias[:, :1]
    step = jnp.maximum(before, 0.0) + jnp.log1p(jnp.exp(-jnp.abs(before)))
    log = -jnp.exp(a_log[:, :1]) * step
    steps[...] = step
    logs[...] = log
    upper = triangle(False)
    count = raw.shape[1] // Q
    state = jnp.zeros((512, STATE), F32)
    whole = jnp.zeros((8, 1), F32)
    for n in range(count):
        lanes = slice(n * Q, (n + 1) * Q)
        cumul = dot(log[:, lanes], upper, 1, 0, highest)
        total = cumul[:, Q - 1 : Q]
        enter[n] = state.astype(BF16)
        left = over_heads(step[:, lanes] * jnp.exp(total - cumul), Q)
        scaled = (inner[:, lanes].astype(F32) * left).astype(BF16)
        fresh = dot(scaled, writers[:, lanes], 1, 1)
        state = state * over_heads(jnp.broadcast_to(jnp.exp(total), (8, STATE)), STATE) + fresh
        whole = whole + total
    for part in range(4):
        payload[part, pl.ds(0, 128), :] = state[128 * part : 128 * (part + 1)]
        for j in range(2):
            row = 2 * part + j
            payload[part, pl.ds(128 + 8 * j, 8), :] = jnp.broadcast_to(
                jnp.exp(whole[row : row + 1]), (8, STATE)
            )


def local_states(raw, squares, bias, a_log):
    tokens = raw.shape[1]
    return pl.pallas_call(
        state_kernel,
        in_specs=[VMEM_SPEC] * 4,
        out_specs=(VMEM_SPEC,) * 7,
        out_shape=(
            jax.ShapeDtypeStruct((512, tokens), BF16),
            jax.ShapeDtypeStruct((STATE, tokens), BF16),
            jax.ShapeDtypeStruct((STATE, tokens), BF16),
            jax.ShapeDtypeStruct((8, tokens), F32),
            jax.ShapeDtypeStruct((8, tokens), F32),
            jax.ShapeDtypeStruct((tokens // Q, 512, STATE), BF16),
            jax.ShapeDtypeStruct((4, 144, STATE), F32),
        ),
        compiler_params=params(16),
        name="states",
    )(raw, squares, bias, a_log)


def within_kernel(inner, writers, readers, steps, logs, enter, d_skip, out, begun):
    upper, lower = triangle(False), triangle(True)
    causal = upper > 0.0
    whole = jnp.zeros((8, 1), F32)
    for n in range(inner.shape[1] // Q):
        lanes = slice(n * Q, (n + 1) * Q)
        log = logs[:, lanes]
        cumul = dot(log, upper, 1, 0, highest)
        column = dot(lower, log, 1, 1, highest)
        begun[:, lanes] = cumul + whole
        whole = whole + cumul[:, Q - 1 : Q]
        meets = dot(writers[:, lanes], readers[:, lanes], 0, 0)
        carried = dot(enter[n], readers[:, lanes], 1, 0)
        grown = jnp.exp(cumul)
        step = steps[:, lanes]
        for h in range(8):
            span = slice(h * HDIM, (h + 1) * HDIM)
            apart = jnp.minimum(cumul[h : h + 1] - column[:, h : h + 1], 0.0)
            mixing = jnp.where(causal, meets * jnp.exp(apart), 0.0).astype(BF16)
            own = inner[span, lanes].astype(F32)
            scaled = (own * step[h : h + 1]).astype(BF16)
            out[span, lanes] = (
                dot(scaled, mixing, 1, 0)
                + carried[span] * grown[h : h + 1]
                + d_skip[span] * own
            )


def within(inner, writers, readers, steps, logs, enter, d_skip):
    tokens = inner.shape[1]
    return pl.pallas_call(
        within_kernel,
        in_specs=[VMEM_SPEC] * 7,
        out_specs=(VMEM_SPEC,) * 2,
        out_shape=(
            jax.ShapeDtypeStruct((512, tokens), F32),
            jax.ShapeDtypeStruct((8, tokens), F32),
        ),
        compiler_params=params(16),
        cost_estimate=pl.CostEstimate(
            flops=6_000_000_000, bytes_accessed=6_000_000, transcendentals=2_000_000
        ),
        name="within",
    )(inner, writers, readers, steps, logs, enter, d_skip)


def finish_kernel(place, local, begun, readers, *refs):
    gain, out, state = refs[4:]
    for k in range(4):
        rows = pl.ds(pl.multiple_of(lax.rem(place[1] + 4 - k, 4) * 128, 128), 128)
        state[rows, :] = refs[k][...]
    for n in range(local.shape[1] // Q):
        lanes = slice(n * Q, (n + 1) * Q)
        carried = dot(state[...], readers[:, lanes], 1, 0)
        y = local[:, lanes] + carried * over_heads(jnp.exp(begun[:, lanes]), Q)
        mean = jnp.sum(y * y, axis=0, keepdims=True) * (1.0 / 512)
        y = y * lax.rsqrt(mean + 1e-05) * gain[...]
        out[lanes, :] = y.T.astype(BF16)


def finish(place, local, begun, readers, states, gain):
    return pl.pallas_call(
        finish_kernel,
        in_specs=[SMEM_SPEC] + [VMEM_SPEC] * 8,
        out_specs=VMEM_SPEC,
        out_shape=jax.ShapeDtypeStruct((local.shape[1], 512), BF16),
        scratch_shapes=[pltpu.VMEM((512, STATE), BF16)],
        compiler_params=params(16),
        name="finish",
    )(place, local, begun, readers, *states, gain)


def two_heads(decays):
    return jnp.concatenate(
        [jnp.broadcast_to(decays[8 * j : 8 * j + 1], (HDIM, STATE)) for j in range(2)], axis=0
    )


def prefix_kernel(size, slot, place, *refs):
    got, (before, total, held) = refs[:size], refs[size:]
    for k in range(size):
        held[lax.rem(place[slot] + size - k, size)] = got[k][...].astype(F32)
    state, decay = jnp.zeros((128, STATE), F32), jnp.ones((16, STATE), F32)
    for i in range(size):
        before[i, pl.ds(0, 128), :] = state
        before[i, pl.ds(128, 16), :] = decay
        left = held[i, pl.ds(128, 16), :]
        state = state * two_heads(left) + held[i, pl.ds(0, 128), :]
        decay = decay * left
    total[...] = jnp.concatenate([state, decay], axis=0).astype(BF16)


def prefix(place, slot, got):
    size = len(got)
    return pl.pallas_call(
        functools.partial(prefix_kernel, size, slot),
        in_specs=[SMEM_SPEC] + [VMEM_SPEC] * size,
        out_specs=(VMEM_SPEC, VMEM_SPEC),
        out_shape=(
            jax.ShapeDtypeStruct((size, 144, STATE), F32),
            jax.ShapeDtypeStruct((144, STATE), BF16),
        ),
        scratch_shapes=[pltpu.VMEM((size, 144, STATE), F32)],
        compiler_params=params(4),
        name="prefix",
    )(place, *got)


def join_kernel(place, in_row, in_plane, plane, out):
    y = place[2]
    begun = jnp.where(place[4] > 0, plane[pl.ds(0, 128), :].astype(F32), 0.0)
    begun = in_plane[y, pl.ds(0, 128), :] + two_heads(in_plane[y, pl.ds(128, 16), :]) * begun
    for i in range(4):
        made = in_row[i, pl.ds(0, 128), :] + two_heads(in_row[i, pl.ds(128, 16), :]) * begun
        out[i] = made.astype(BF16)


def join(place, in_row, in_plane, plane):
    return pl.pallas_call(
        join_kernel,
        in_specs=[SMEM_SPEC] + [VMEM_SPEC] * 3,
        out_specs=VMEM_SPEC,
        out_shape=jax.ShapeDtypeStruct((4, 128, STATE), BF16),
        compiler_params=params(4),
        name="join",
    )(place, in_row, in_plane, plane)


def on_device(
    patches, grid_rows, frame_ids, ln_gain, w_qkv, w_out, w_conn, norm_gain,
    w_x, w_b, w_c, w_dt, dt_bias, a_log, d_skip, out_gain,
):
    core, x, y, zl, zh = (lax.axis_index(a) for a in ("c", "x", "y", "zl", "zh"))
    member = lax.rem(x + 2 * lax.rem(y, 2), 4)
    place = jnp.stack([core, x, y, zl, zh, member]).astype(jnp.int32)
    pool = (
        jnp.where(jnp.arange(256)[:, None] // POOL == jnp.arange(64)[None, :], 1.0 / POOL, 0.0)
    ).astype(BF16)

    block = jnp.concatenate([jnp.transpose(w_qkv, (0, 2, 1)), w_out[None]], axis=0)
    some = lax.dynamic_slice(w_conn, ((y * 4 + x) * 72, 0), (72, 512))
    some = jnp.concatenate([some[:, :256], some[:, 256:]], axis=0)
    piece = lax.dynamic_index_in_dim(block, member, 0, False)
    piece = jnp.concatenate([piece, some], axis=1)
    blocks, some = split_pieces([ring_shift(piece, "zl", 4, k) for k in (1, 2, 3)], some)
    turned = jnp.transpose(patches, (0, 2, 1)).reshape(4, 432, 256)
    own_frames = lax.dynamic_slice(grid_rows, (zl * 3,), (3,))
    block = block.reshape(4, 3, 48, 1152)
    gain = ln_gain[:, None]
    wide_gain = norm_gain[None]
    (turned, blocks, block, some, gain, wide_gain, pool, place, own_frames) = lax.optimization_barrier(
        (turned, blocks, block, some, gain, wide_gain, pool, place, own_frames)
    )
    ring = (
        blocks,
        ring_shift(blocks, "x", 4, 1),
        ring_shift(blocks, "x", 4, -1),
        ring_shift(blocks, "y", 4, 1),
    )

    other_some = swap_core(some)
    turned, _ = lax.optimization_barrier((turned, other_some))
    product = weight_product(place, some, other_some, wide_gain, w_dt.T, w_x, w_b, w_c)

    own = spread_out(lambda i: lax.dynamic_index_in_dim(turned, i, 0, False), "zl", 4)
    own, _ = lax.optimization_barrier((own, (ring, product)))
    own = jnp.stack(own)
    normed, residual = norm_frames(place, own, swap_core(own), gain, pool)
    near = [product] + [ring_shift(product, "x", 4, k) for k in (1, 2, 3)]
    rows = []
    for i in range(4):
        away = lax.rem(x + 4 - i, 4)
        found = near[0]
        for k in (1, 2, 3):
            found = jnp.where(away == k, near[k], found)
        rows.append(found)
    near = jnp.concatenate(rows, axis=0)
    before, after = ring_shift(near, "y", 4, 1), ring_shift(near, "y", 4, -1)
    far_lo, far_hi = ring_shift(before[:144], "y", 4, 1), ring_shift(after[144:], "y", 4, -1)
    wide = (near, before, far_lo, far_hi, after)

    keep, give = vision(place, own_frames, normed, pool, block, ring)
    summed = keep + residual + swap_core(give)
    token = jnp.arange(128) % 64
    kept = token[None, :] * POOL < (own_frames * GRID)[:, None]
    seen = jnp.where(kept[None, :, None, :], summed, 0.0).astype(BF16)
    seen = spread_out(lambda i: lax.dynamic_index_in_dim(seen, i, 0, False), "zl", 4)

    seen, _ = lax.optimization_barrier((seen, near))
    outgoing = bucket(place, frame_ids, seen)
    incoming = lax.all_to_all(
        outgoing, ("zh", "y", "x"), split_axis=0, concat_axis=0, tiled=True
    )
    own_features, _ = lax.optimization_barrier((place_frames(incoming), wide))
    line = lax.all_gather(own_features, "zl", axis=0, tiled=True)
    stream, raw, squares = stream_rows(place, line, swap_core(line), w_conn, wide)
    squares = squares + swap_core(squares)
    squares = squares + sum(ring_shift(squares, "zl", 4, k) for k in (1, 2, 3))

    def column(values, repeat):
        return jnp.broadcast_to(values[:, None], (values.shape[0], repeat))

    inner, writers, readers, steps, logs, enter, payload = local_states(
        raw, squares, column(dt_bias, 128), column(a_log, 128)
    )
    local, begun = within(
        inner, writers, readers, steps, logs, enter, jnp.repeat(d_skip, HDIM)[:, None]
    )
    sent = payload.astype(BF16)
    in_row, row = prefix(
        place, 1, spread_out(lambda i: lax.dynamic_index_in_dim(sent, i, 0, False), "x", 4)
    )
    in_plane, plane = prefix(place, 2, spread_out(lambda i: row, "y", 4))
    states = join(place, in_row, in_plane, ring_shift(plane, "zh", 2, 1))
    states = spread_out(lambda i: lax.dynamic_index_in_dim(states, i, 0, False), "x", 4)
    mixed = finish(place, local, begun, readers, states, out_gain[:, None])
    return stream, mixed


def solution(mesh):
    fine = Mesh(mesh.devices.reshape(2, 4, 4, 4, 2), ("zh", "y", "x", "zl", "c"))
    tm, head = ("zh", "y", "x"), ("zl", "c")
    in_specs = (
        P(tm, None, head),
        P(tm),
        P(tm),
        P(),
        P(None, None, head),
        P(head, None),
        P(None, head),
        P(),
        P(None, head),
        P(None, head),
        P(None, head),
        P(None, head),
        P(head),
        P(head),
        P(head),
        P(head),
    )
    out_specs = (P(tm, head), P(tm, head))
    return jax.shard_map(
        on_device, mesh=fine, in_specs=in_specs, out_specs=out_specs, check_vma=False
    )
```

```python
import functools
import jax
import jax.numpy as jnp
from jax import lax
from jax.experimental import pallas as pl
from jax.experimental.pallas import tpu as pltpu
from jax.sharding import Mesh, PartitionSpec as P

GRID = 16
POOL = 4
VHD = 72
HDIM = 64
STATE = 128
Q = 256
XW = 512

F32 = jnp.float32
BF16 = jnp.bfloat16
highest = lax.Precision.HIGHEST
VMEM_SPEC = pl.BlockSpec(memory_space=pltpu.VMEM)
SMEM_SPEC = pl.BlockSpec(memory_space=pltpu.SMEM)
ANY_SPEC = pl.BlockSpec(memory_space=pl.ANY)


def params(mib):
    return pltpu.CompilerParams(vmem_limit_bytes=mib * 2**20)


def dot(a, b, ca, cb, precision=None):
    return lax.dot_general(
        a, b, (((ca,), (cb,)), ((), ())), preferred_element_type=F32, precision=precision
    )


def ring_shift(value, axis, size, shift):
    return lax.ppermute(value, axis, [(i, (i + shift) % size) for i in range(size)])


def swap_core(value):
    return lax.ppermute(value, "c", [(0, 1), (1, 0)])


def spread_out(parts, axis, size):
    position = lax.axis_index(axis)
    own = parts(position)
    return [own] + [
        ring_shift(parts(lax.rem(position + k, size)), axis, size, k) for k in range(1, size)
    ]


def split_kernel(a, b, c, own, blocks, some):
    some[0] = own[...]
    for k, source in enumerate((a, b, c)):
        some[k + 1] = source[:, pl.ds(1152, 256)]
        for third in range(3):
            blocks[3 * k + third] = source[pl.ds(48 * third, 48), pl.ds(0, 1152)]


def split_pieces(pieces, own):
    return pl.pallas_call(
        split_kernel,
        in_specs=[VMEM_SPEC] * 4,
        out_specs=(VMEM_SPEC,) * 2,
        out_shape=(
            jax.ShapeDtypeStruct((9, 48, 1152), BF16),
            jax.ShapeDtypeStruct((4, 144, 256), BF16),
        ),
        compiler_params=params(8),
        name="split",
    )(*pieces, own)


def product_kernel(
    place, own, other, wide_gain, w_dt, w_x, w_b, w_c, product, big_x, big_b, big_c, sems
):
    copies = [
        pltpu.make_async_copy(source, held, sems.at[n])
        for n, (source, held) in enumerate(((w_x, big_x), (w_b, big_b), (w_c, big_c)))
    ]
    for copy in copies:
        copy.start()
    for copy in copies:
        copy.wait()
    first = place[0] == 0
    sums = [jnp.zeros((144, width), F32) for width in (512, 128, 128, 8)]
    for z in range(4):
        k = lax.rem(place[3] + 4 - z, 4)
        a, b = own[k].astype(F32), other[k].astype(F32)
        for i, part in ((2 * z, jnp.where(first, a, b)), (2 * z + 1, jnp.where(first, b, a))):
            span = pl.ds(512 * i, 512)
            part = jnp.concatenate([part[:72], part[72:]], axis=1) * wide_gain[:, span]
            high = part.astype(BF16).astype(F32)
            both = jnp.concatenate([high, part - high], axis=0).astype(BF16)
            made = [dot(both, w[span, :], 1, 0) for w in (big_x, big_b, big_c)]
            made.append(dot(both, w_dt[:, span], 1, 1))
            sums = [total + extra for total, extra in zip(sums, made)]
    product[...] = jnp.zeros_like(product)
    begun = 0
    for total in sums:
        width = total.shape[1]
        product[:, pl.ds(begun, width)] = (total[:72] + total[72:]).astype(BF16)
        begun += width


def weight_product(place, own, other, wide_gain, w_dt, w_x, w_b, w_c):
    return pl.pallas_call(
        product_kernel,
        in_specs=[SMEM_SPEC] + [VMEM_SPEC] * 4 + [ANY_SPEC] * 3,
        out_specs=VMEM_SPEC,
        out_shape=jax.ShapeDtypeStruct((72, 896), BF16),
        scratch_shapes=[
            pltpu.VMEM(w_x.shape, BF16),
            pltpu.VMEM(w_b.shape, BF16),
            pltpu.VMEM(w_c.shape, BF16),
            pltpu.SemaphoreType.DMA((3,)),
        ],
        compiler_params=params(56),
        name="product",
    )(place, own, other, wide_gain, w_dt, w_x, w_b, w_c)


def norm_kernel(place, own, other, gain, pool, normed, residual, x):
    first = place[0] == 0
    for f in range(3):
        frame = pl.ds(144 * f, 144)
        for z in range(4):
            k = lax.rem(place[3] + 4 - z, 4)
            mine = own[k, frame, :]
            a, b = mine.astype(F32), other[k, frame, :].astype(F32)
            x[pl.ds(288 * z, 144), :] = jnp.where(first, a, b)
            x[pl.ds(288 * z + 144, 144), :] = jnp.where(first, b, a)
            pooled = dot(mine, pool[...], 1, 0)
            residual[z, f] = jnp.concatenate([pooled[:72], pooled[72:]], axis=1)
        values = x[...]
        width = values.shape[0]
        centre = jnp.sum(values, axis=0, keepdims=True) * (1.0 / width)
        values = values - centre
        spread = jnp.sum(values * values, axis=0, keepdims=True) * (1.0 / width)
        normed[f] = (values * lax.rsqrt(spread + 1e-06) * gain[...]).astype(BF16)


def norm_frames(place, own, other, ln_gain, pool):
    return pl.pallas_call(
        norm_kernel,
        in_specs=[SMEM_SPEC] + [VMEM_SPEC] * 4,
        out_specs=(VMEM_SPEC, VMEM_SPEC),
        out_shape=(
            jax.ShapeDtypeStruct((3, 1152, 256), BF16),
            jax.ShapeDtypeStruct((4, 3, 72, 128), F32),
        ),
        scratch_shapes=[pltpu.VMEM((1152, 256), F32)],
        compiler_params=params(16),
        name="norm",
    )(place, own, other, ln_gain, pool)


def vision_kernel(place, rows, normed, pool, block, *rest):
    ring = rest[:4]
    keep, give, wx, wy, qkv, ctx, scores, powered, sems = rest[4:]
    frame = pl.program_id(0)
    first = place[0] == 0

    def copies():
        pairs = [
            (block.at[:, :, :, pl.ds(0, XW)], wx.at[:, pl.ds(0, 3)]),
            (block.at[:, :, :, pl.ds(XW, 1152 - XW)], wy.at[:, pl.ds(0, 3)]),
        ]
        for source, ahead in zip(ring, (0, 3, 1, 2)):
            index = lax.rem(place[5] + ahead, 4)
            rows = pl.ds(3, 9)
            pairs.append((source.at[:, :, pl.ds(0, XW)], wx.at[index, rows]))
            pairs.append((source.at[:, :, pl.ds(XW, 1152 - XW)], wy.at[index, rows]))
        return [
            pltpu.make_async_copy(source, held, sems.at[n])
            for n, (source, held) in enumerate(pairs)
        ]

    @pl.when(frame == 0)
    def _():
        for copy in copies():
            copy.start()
        for copy in copies():
            copy.wait()

    width = normed.shape[1]
    for m in range(3):
        left = wx[m].reshape(576, XW)
        right = wy[m].reshape(576, width - XW)
        qkv[m] = dot(left, normed[0, :XW], 1, 0) + dot(right, normed[0, XW:], 1, 0)
    valid = rows[frame] * GRID
    usable = lax.broadcasted_iota(jnp.int32, (256, 256), 0) < valid
    for h in range(8):
        span = pl.ds(h * VHD, VHD)
        q, k = (qkv[m, span, :].astype(BF16) for m in range(2))
        scores[h] = dot(k, q, 0, 0)
    shares = []
    for h in range(8):
        values = jnp.where(usable, scores[h], -1e30)
        top = jnp.max(values, axis=0, keepdims=True)
        values = jnp.exp((values - top) * VHD ** (-0.5))
        shares.append(1.0 / jnp.sum(values, axis=0, keepdims=True))
        powered[h] = values.astype(BF16)
    for h in range(8):
        span = pl.ds(h * VHD, VHD)
        ctx[span, :] = dot(qkv[2, span, :].astype(BF16), powered[h], 1, 0) * shares[h]
    pooled = dot(ctx[...].astype(BF16), pool[...], 1, 0)
    high = pooled.astype(BF16)
    low = (pooled - high.astype(F32)).astype(BF16)
    both = jnp.concatenate([high, low], axis=1)
    out_x = dot(both, wx[3].reshape(576, XW), 0, 0)
    out_y = dot(both, wy[3].reshape(576, width - XW), 0, 0)
    attended = jnp.concatenate([out_x, out_y], axis=1)
    attended = (attended[:64] + attended[64:]).T
    for z in range(4):
        a = attended[(2 * z) * 144 : (2 * z + 1) * 144]
        b = attended[(2 * z + 1) * 144 : (2 * z + 2) * 144]
        own = jnp.where(first, a, b)
        far = jnp.where(first, b, a)
        keep[z, 0] = jnp.concatenate([own[:72], own[72:]], axis=1)
        give[z, 0] = jnp.concatenate([far[:72], far[72:]], axis=1)


def vision(place, rows, normed, pool, block, ring):
    out = pl.BlockSpec((4, 1, 72, 128), lambda f: (0, f, 0, 0))
    shape = jax.ShapeDtypeStruct((4, 3, 72, 128), F32)
    return pl.pallas_call(
        vision_kernel,
        grid=(3,),
        in_specs=[
            SMEM_SPEC,
            SMEM_SPEC,
            pl.BlockSpec((1, 1152, 256), lambda f: (f, 0, 0)),
            VMEM_SPEC,
        ]
        + [ANY_SPEC] * 5,
        out_specs=(out, out),
        out_shape=(shape, shape),
        scratch_shapes=[
            pltpu.VMEM((4, 12, 48, XW), BF16),
            pltpu.VMEM((4, 12, 48, 1152 - XW), BF16),
            pltpu.VMEM((3, 576, 256), F32),
            pltpu.VMEM((576, 256), F32),
            pltpu.VMEM((8, 256, 256), F32),
            pltpu.VMEM((8, 256, 256), BF16),
            pltpu.SemaphoreType.DMA((10,)),
        ],
        compiler_params=params(56),
        name="vision",
    )(place, rows, normed, pool, block, *ring)


def bucket_kernel(place, ids, *refs):
    out = refs[4]
    out[...] = jnp.zeros_like(out)
    for k in range(4):
        z = lax.rem(place[3] + 4 - k, 4)
        for j in range(3):
            frame = ids[3 * z + j]
            spot = lax.rem(frame, 12) + 1
            label = jnp.zeros((8, 128), F32) + spot.astype(F32)
            whole = jnp.concatenate([refs[k][j].astype(F32), label], axis=0)
            out[lax.div(frame, 12)] = whole.astype(BF16)


def bucket(place, ids, seen):
    return pl.pallas_call(
        bucket_kernel,
        in_specs=[SMEM_SPEC, SMEM_SPEC] + [VMEM_SPEC] * 4,
        out_specs=VMEM_SPEC,
        out_shape=jax.ShapeDtypeStruct((32, 80, 128), BF16),
        compiler_params=params(16),
        name="bucket",
    )(place, ids, *seen)


def place_kernel(incoming, out, held):
    held[...] = incoming[...].astype(F32)
    left = lax.broadcasted_iota(jnp.int32, (72, 128), 1) < 64

    def frame(p):
        found = jnp.zeros((72, 128), F32)
        for s in range(32):
            here = held[s, pl.ds(72, 1), :] == float(p + 1)
            found = jnp.where(here, held[s, pl.ds(0, 72), :], found)
        return found

    for pair in range(6):
        a, b = frame(2 * pair), frame(2 * pair + 1)
        lanes = pl.ds(128 * pair, 128)
        top = jnp.where(left, a, pltpu.roll(b, 64, 1))
        bottom = jnp.where(left, pltpu.roll(a, 64, 1), b)
        out[:, lanes] = jnp.concatenate([top, bottom], axis=0).astype(BF16)


def place_frames(incoming):
    return pl.pallas_call(
        place_kernel,
        in_specs=[VMEM_SPEC],
        out_specs=VMEM_SPEC,
        out_shape=jax.ShapeDtypeStruct((144, 768), BF16),
        scratch_shapes=[pltpu.VMEM((32, 80, 128), F32)],
        compiler_params=params(16),
        name="place",
    )(incoming)


def stream_kernel(place, mine, other, w_conn, *rest):
    pieces = rest[:5]
    stream, raw, squares, seen, wide, conn, held, sems = rest[5:]
    copies = [pltpu.make_async_copy(w_conn, conn, sems.at[0])]
    for n, (k, lo, size) in enumerate(
        ((0, 0, 288), (1, 0, 288), (2, 0, 144), (2, 144, 144), (3, 0, 288))
    ):
        begun = pl.multiple_of(lax.rem(place[2] + 4 - k, 4) * 288 + lo, 144)
        held_rows = wide.at[pl.ds(begun, size)]
        copies.append(pltpu.make_async_copy(pieces[n], held_rows, sems.at[n + 1]))
    for copy in copies:
        copy.start()
    first = place[0] == 0
    for z in range(4):
        a, b = mine[pl.ds(144 * z, 144), :], other[pl.ds(144 * z, 144), :]
        seen[pl.ds(288 * z, 144), :] = jnp.where(first, a, b)
        seen[pl.ds(288 * z + 144, 144), :] = jnp.where(first, b, a)
    for copy in copies:
        copy.wait()
    held[pl.ds(0, 768), :] = dot(wide[:, pl.ds(0, 768)], seen[...], 0, 0)
    held[pl.ds(768, 8), :] = dot(wide[:, pl.ds(768, 128)], seen[...], 0, 0)[:8]
    out = pltpu.make_async_copy(held, raw, sems.at[6])
    out.start()
    made = dot(conn[...], seen[...], 0, 0).astype(BF16)
    values = made.astype(F32)
    squares[...] = jnp.broadcast_to(
        jnp.sum(values * values, axis=0, keepdims=True), squares.shape
    )
    stream[...] = values.T.astype(BF16)
    out.wait()


def stream_rows(place, mine, other, w_conn, wide):
    tokens, width = mine.shape[1], w_conn.shape[1]
    return pl.pallas_call(
        stream_kernel,
        in_specs=[SMEM_SPEC] + [VMEM_SPEC] * 2 + [ANY_SPEC] * 6,
        out_specs=(VMEM_SPEC, ANY_SPEC, VMEM_SPEC),
        out_shape=(
            jax.ShapeDtypeStruct((tokens, width), BF16),
            jax.ShapeDtypeStruct((776, tokens), F32),
            jax.ShapeDtypeStruct((8, tokens), F32),
        ),
        scratch_shapes=[
            pltpu.VMEM((1152, tokens), BF16),
            pltpu.VMEM((1152, 896), BF16),
            pltpu.VMEM(w_conn.shape, BF16),
            pltpu.VMEM((776, tokens), F32),
            pltpu.SemaphoreType.DMA((7,)),
        ],
        compiler_params=params(52),
        name="stream",
    )(place, mine, other, w_conn, *wide)


def over_heads(rows, length):
    return jnp.concatenate(
        [jnp.broadcast_to(rows[h : h + 1], (HDIM, length)) for h in range(8)], axis=0
    )


def triangle(transposed):
    a = lax.broadcasted_iota(jnp.int32, (Q, Q), 0)
    b = lax.broadcasted_iota(jnp.int32, (Q, Q), 1)
    return jnp.where(a >= b if transposed else a <= b, 1.0, 0.0).astype(F32)


def state_kernel(
    raw, squares, bias, a_log, inner, writers, readers, steps, logs, enter, payload
):
    scale = lax.rsqrt(squares[0:1, :] * (1.0 / 4096) + 1e-05)
    inner[...] = (raw[:512] * scale).astype(BF16)
    writers[...] = (raw[512:640] * scale).astype(BF16)
    readers[...] = (raw[640:768] * scale).astype(BF16)
    before = raw[768:776] * scale + bias[:, :1]
    step = jnp.maximum(before, 0.0) + jnp.log1p(jnp.exp(-jnp.abs(before)))
    log = -jnp.exp(a_log[:, :1]) * step
    steps[...] = step
    logs[...] = log
    upper = triangle(False)
    count = raw.shape[1] // Q
    state = jnp.zeros((512, STATE), F32)
    whole = jnp.zeros((8, 1), F32)
    for n in range(count):
        lanes = slice(n * Q, (n + 1) * Q)
        cumul = dot(log[:, lanes], upper, 1, 0, highest)
        total = cumul[:, Q - 1 : Q]
        enter[n] = state.astype(BF16)
        left = over_heads(step[:, lanes] * jnp.exp(total - cumul), Q)
        scaled = (inner[:, lanes].astype(F32) * left).astype(BF16)
        fresh = dot(scaled, writers[:, lanes], 1, 1)
        state = state * over_heads(jnp.broadcast_to(jnp.exp(total), (8, STATE)), STATE) + fresh
        whole = whole + total
    for part in range(4):
        payload[part, pl.ds(0, 128), :] = state[128 * part : 128 * (part + 1)]
        for j in range(2):
            row = 2 * part + j
            payload[part, pl.ds(128 + 8 * j, 8), :] = jnp.broadcast_to(
                jnp.exp(whole[row : row + 1]), (8, STATE)
            )


def local_states(raw, squares, bias, a_log):
    tokens = raw.shape[1]
    return pl.pallas_call(
        state_kernel,
        in_specs=[VMEM_SPEC] * 4,
        out_specs=(VMEM_SPEC,) * 7,
        out_shape=(
            jax.ShapeDtypeStruct((512, tokens), BF16),
            jax.ShapeDtypeStruct((STATE, tokens), BF16),
            jax.ShapeDtypeStruct((STATE, tokens), BF16),
            jax.ShapeDtypeStruct((8, tokens), F32),
            jax.ShapeDtypeStruct((8, tokens), F32),
            jax.ShapeDtypeStruct((tokens // Q, 512, STATE), BF16),
            jax.ShapeDtypeStruct((4, 144, STATE), F32),
        ),
        compiler_params=params(16),
        name="states",
    )(raw, squares, bias, a_log)


def within_kernel(inner, writers, readers, steps, logs, enter, d_skip, out, begun):
    upper, lower = triangle(False), triangle(True)
    causal = upper > 0.0
    whole = jnp.zeros((8, 1), F32)
    for n in range(inner.shape[1] // Q):
        lanes = slice(n * Q, (n + 1) * Q)
        log = logs[:, lanes]
        cumul = dot(log, upper, 1, 0, highest)
        column = dot(lower, log, 1, 1, highest)
        begun[:, lanes] = cumul + whole
        whole = whole + cumul[:, Q - 1 : Q]
        meets = dot(writers[:, lanes], readers[:, lanes], 0, 0)
        carried = dot(enter[n], readers[:, lanes], 1, 0)
        grown = jnp.exp(cumul)
        step = steps[:, lanes]
        for h in range(8):
            span = slice(h * HDIM, (h + 1) * HDIM)
            apart = jnp.minimum(cumul[h : h + 1] - column[:, h : h + 1], 0.0)
            mixing = jnp.where(causal, meets * jnp.exp(apart), 0.0).astype(BF16)
            own = inner[span, lanes].astype(F32)
            scaled = (own * step[h : h + 1]).astype(BF16)
            out[span, lanes] = (
                dot(scaled, mixing, 1, 0)
                + carried[span] * grown[h : h + 1]
                + d_skip[span] * own
            )


def within(inner, writers, readers, steps, logs, enter, d_skip):
    tokens = inner.shape[1]
    return pl.pallas_call(
        within_kernel,
        in_specs=[VMEM_SPEC] * 7,
        out_specs=(VMEM_SPEC,) * 2,
        out_shape=(
            jax.ShapeDtypeStruct((512, tokens), F32),
            jax.ShapeDtypeStruct((8, tokens), F32),
        ),
        compiler_params=params(16),
        cost_estimate=pl.CostEstimate(
            flops=6_000_000_000, bytes_accessed=6_000_000, transcendentals=2_000_000
        ),
        name="within",
    )(inner, writers, readers, steps, logs, enter, d_skip)


def finish_kernel(place, local, begun, readers, *refs):
    gain, out, state = refs[4:]
    for k in range(4):
        rows = pl.ds(pl.multiple_of(lax.rem(place[1] + 4 - k, 4) * 128, 128), 128)
        state[rows, :] = refs[k][...]
    for n in range(local.shape[1] // Q):
        lanes = slice(n * Q, (n + 1) * Q)
        carried = dot(state[...], readers[:, lanes], 1, 0)
        y = local[:, lanes] + carried * over_heads(jnp.exp(begun[:, lanes]), Q)
        mean = jnp.sum(y * y, axis=0, keepdims=True) * (1.0 / 512)
        y = y * lax.rsqrt(mean + 1e-05) * gain[...]
        out[lanes, :] = y.T.astype(BF16)


def finish(place, local, begun, readers, states, gain):
    return pl.pallas_call(
        finish_kernel,
        in_specs=[SMEM_SPEC] + [VMEM_SPEC] * 8,
        out_specs=VMEM_SPEC,
        out_shape=jax.ShapeDtypeStruct((local.shape[1], 512), BF16),
        scratch_shapes=[pltpu.VMEM((512, STATE), BF16)],
        compiler_params=params(16),
        name="finish",
    )(place, local, begun, readers, *states, gain)


def two_heads(decays):
    return jnp.concatenate(
        [jnp.broadcast_to(decays[8 * j : 8 * j + 1], (HDIM, STATE)) for j in range(2)], axis=0
    )


def prefix_kernel(size, slot, place, *refs):
    got, (before, total, held) = refs[:size], refs[size:]
    for k in range(size):
        held[lax.rem(place[slot] + size - k, size)] = got[k][...].astype(F32)
    state, decay = jnp.zeros((128, STATE), F32), jnp.ones((16, STATE), F32)
    for i in range(size):
        before[i, pl.ds(0, 128), :] = state
        before[i, pl.ds(128, 16), :] = decay
        left = held[i, pl.ds(128, 16), :]
        state = state * two_heads(left) + held[i, pl.ds(0, 128), :]
        decay = decay * left
    total[...] = jnp.concatenate([state, decay], axis=0).astype(BF16)


def prefix(place, slot, got):
    size = len(got)
    return pl.pallas_call(
        functools.partial(prefix_kernel, size, slot),
        in_specs=[SMEM_SPEC] + [VMEM_SPEC] * size,
        out_specs=(VMEM_SPEC, VMEM_SPEC),
        out_shape=(
            jax.ShapeDtypeStruct((size, 144, STATE), F32),
            jax.ShapeDtypeStruct((144, STATE), BF16),
        ),
        scratch_shapes=[pltpu.VMEM((size, 144, STATE), F32)],
        compiler_params=params(4),
        name="prefix",
    )(place, *got)


def join_kernel(place, in_row, in_plane, plane, out):
    y = place[2]
    begun = jnp.where(place[4] > 0, plane[pl.ds(0, 128), :].astype(F32), 0.0)
    begun = in_plane[y, pl.ds(0, 128), :] + two_heads(in_plane[y, pl.ds(128, 16), :]) * begun
    for i in range(4):
        made = in_row[i, pl.ds(0, 128), :] + two_heads(in_row[i, pl.ds(128, 16), :]) * begun
        out[i] = made.astype(BF16)


def join(place, in_row, in_plane, plane):
    return pl.pallas_call(
        join_kernel,
        in_specs=[SMEM_SPEC] + [VMEM_SPEC] * 3,
        out_specs=VMEM_SPEC,
        out_shape=jax.ShapeDtypeStruct((4, 128, STATE), BF16),
        compiler_params=params(4),
        name="join",
    )(place, in_row, in_plane, plane)


def on_device(
    patches, grid_rows, frame_ids, ln_gain, w_qkv, w_out, w_conn, norm_gain,
    w_x, w_b, w_c, w_dt, dt_bias, a_log, d_skip, out_gain,
):
    core, x, y, zl, zh = (lax.axis_index(a) for a in ("c", "x", "y", "zl", "zh"))
    member = lax.rem(x + 2 * lax.rem(y, 2), 4)
    place = jnp.stack([core, x, y, zl, zh, member]).astype(jnp.int32)
    pool = (
        jnp.where(jnp.arange(256)[:, None] // POOL == jnp.arange(64)[None, :], 1.0 / POOL, 0.0)
    ).astype(BF16)

    block = jnp.concatenate([jnp.transpose(w_qkv, (0, 2, 1)), w_out[None]], axis=0)
    some = lax.dynamic_slice(w_conn, ((y * 4 + x) * 72, 0), (72, 512))
    some = jnp.concatenate([some[:, :256], some[:, 256:]], axis=0)
    piece = lax.dynamic_index_in_dim(block, member, 0, False)
    piece = jnp.concatenate([piece, some], axis=1)
    blocks, some = split_pieces([ring_shift(piece, "zl", 4, k) for k in (1, 2, 3)], some)
    turned = jnp.transpose(patches, (0, 2, 1)).reshape(4, 432, 256)
    own_frames = lax.dynamic_slice(grid_rows, (zl * 3,), (3,))
    block = block.reshape(4, 3, 48, 1152)
    gain = ln_gain[:, None]
    wide_gain = norm_gain[None]
    (turned, blocks, block, some, gain, wide_gain, pool, place, own_frames) = lax.optimization_barrier(
        (turned, blocks, block, some, gain, wide_gain, pool, place, own_frames)
    )
    ring = (
        blocks,
        ring_shift(blocks, "x", 4, 1),
        ring_shift(blocks, "x", 4, -1),
        ring_shift(blocks, "y", 4, 1),
    )

    other_some = swap_core(some)
    turned, _ = lax.optimization_barrier((turned, other_some))
    product = weight_product(place, some, other_some, wide_gain, w_dt.T, w_x, w_b, w_c)

    own = spread_out(lambda i: lax.dynamic_index_in_dim(turned, i, 0, False), "zl", 4)
    own, _ = lax.optimization_barrier((own, (ring, product)))
    own = jnp.stack(own)
    normed, residual = norm_frames(place, own, swap_core(own), gain, pool)
    near = [product] + [ring_shift(product, "x", 4, k) for k in (1, 2, 3)]
    rows = []
    for i in range(4):
        away = lax.rem(x + 4 - i, 4)
        found = near[0]
        for k in (1, 2, 3):
            found = jnp.where(away == k, near[k], found)
        rows.append(found)
    near = jnp.concatenate(rows, axis=0)
    before, after = ring_shift(near, "y", 4, 1), ring_shift(near, "y", 4, -1)
    far_lo, far_hi = ring_shift(before[:144], "y", 4, 1), ring_shift(after[144:], "y", 4, -1)
    wide = (near, before, far_lo, far_hi, after)

    keep, give = vision(place, own_frames, normed, pool, block, ring)
    summed = keep + residual + swap_core(give)
    token = jnp.arange(128) % 64
    kept = token[None, :] * POOL < (own_frames * GRID)[:, None]
    seen = jnp.where(kept[None, :, None, :], summed, 0.0).astype(BF16)
    seen = spread_out(lambda i: lax.dynamic_index_in_dim(seen, i, 0, False), "zl", 4)

    seen, _ = lax.optimization_barrier((seen, near))
    outgoing = bucket(place, frame_ids, seen)
    incoming = lax.all_to_all(
        outgoing, ("zh", "y", "x"), split_axis=0, concat_axis=0, tiled=True
    )
    own_features, _ = lax.optimization_barrier((place_frames(incoming), wide))
    line = lax.all_gather(own_features, "zl", axis=0, tiled=True)
    stream, raw, squares = stream_rows(place, line, swap_core(line), w_conn, wide)
    squares = squares + swap_core(squares)
    squares = squares + sum(ring_shift(squares, "zl", 4, k) for k in (1, 2, 3))

    def column(values, repeat):
        return jnp.broadcast_to(values[:, None], (values.shape[0], repeat))

    inner, writers, readers, steps, logs, enter, payload = local_states(
        raw, squares, column(dt_bias, 128), column(a_log, 128)
    )
    local, begun = within(
        inner, writers, readers, steps, logs, enter, jnp.repeat(d_skip, HDIM)[:, None]
    )
    sent = payload.astype(BF16)
    in_row, row = prefix(
        place, 1, spread_out(lambda i: lax.dynamic_index_in_dim(sent, i, 0, False), "x", 4)
    )
    in_plane, plane = prefix(place, 2, spread_out(lambda i: row, "y", 4))
    plane = ring_shift(plane, "zh", 2, 1)
    in_plane, local, begun = lax.optimization_barrier((in_plane, local, begun))
    states = join(place, in_row, in_plane, plane)
    states = spread_out(lambda i: lax.dynamic_index_in_dim(states, i, 0, False), "x", 4)
    mixed = finish(place, local, begun, readers, states, out_gain[:, None])
    return stream, mixed


def solution(mesh):
    fine = Mesh(mesh.devices.reshape(2, 4, 4, 4, 2), ("zh", "y", "x", "zl", "c"))
    tm, head = ("zh", "y", "x"), ("zl", "c")
    in_specs = (
        P(tm, None, head),
        P(tm),
        P(tm),
        P(),
        P(None, None, head),
        P(head, None),
        P(None, head),
        P(),
        P(None, head),
        P(None, head),
        P(None, head),
        P(None, head),
        P(head),
        P(head),
        P(head),
        P(head),
    )
    out_specs = (P(tm, head), P(tm, head))
    return jax.shard_map(
        on_device, mesh=fine, in_specs=in_specs, out_specs=out_specs, check_vma=False
    )
```

```python
import functools
import jax
import jax.numpy as jnp
from jax import lax
from jax.experimental import pallas as pl
from jax.experimental.pallas import tpu as pltpu
from jax.sharding import Mesh, PartitionSpec as P

GRID = 16
POOL = 4
VHD = 72
HDIM = 64
STATE = 128
Q = 256
XW = 512

F32 = jnp.float32
BF16 = jnp.bfloat16
highest = lax.Precision.HIGHEST
VMEM_SPEC = pl.BlockSpec(memory_space=pltpu.VMEM)
SMEM_SPEC = pl.BlockSpec(memory_space=pltpu.SMEM)
ANY_SPEC = pl.BlockSpec(memory_space=pl.ANY)


def params(mib):
    return pltpu.CompilerParams(vmem_limit_bytes=mib * 2**20)


def dot(a, b, ca, cb, precision=None):
    return lax.dot_general(
        a, b, (((ca,), (cb,)), ((), ())), preferred_element_type=F32, precision=precision
    )


def ring_shift(value, axis, size, shift):
    return lax.ppermute(value, axis, [(i, (i + shift) % size) for i in range(size)])


def swap_core(value):
    return lax.ppermute(value, "c", [(0, 1), (1, 0)])


def spread_out(parts, axis, size):
    position = lax.axis_index(axis)
    own = parts(position)
    return [own] + [
        ring_shift(parts(lax.rem(position + k, size)), axis, size, k) for k in range(1, size)
    ]


def split_kernel(a, b, c, own, blocks, some):
    some[0] = own[...]
    for k, source in enumerate((a, b, c)):
        some[k + 1] = source[:, pl.ds(1152, 256)]
        for third in range(3):
            blocks[3 * k + third] = source[pl.ds(48 * third, 48), pl.ds(0, 1152)]


def split_pieces(pieces, own):
    return pl.pallas_call(
        split_kernel,
        in_specs=[VMEM_SPEC] * 4,
        out_specs=(VMEM_SPEC,) * 2,
        out_shape=(
            jax.ShapeDtypeStruct((9, 48, 1152), BF16),
            jax.ShapeDtypeStruct((4, 144, 256), BF16),
        ),
        compiler_params=params(8),
        name="split",
    )(*pieces, own)


def product_kernel(
    place, own, other, wide_gain, w_dt, w_x, w_b, w_c, product, big_x, big_b, big_c, sems
):
    copies = [
        pltpu.make_async_copy(source, held, sems.at[n])
        for n, (source, held) in enumerate(((w_x, big_x), (w_b, big_b), (w_c, big_c)))
    ]
    for copy in copies:
        copy.start()
    for copy in copies:
        copy.wait()
    first = place[0] == 0
    sums = [jnp.zeros((144, width), F32) for width in (512, 128, 128, 8)]
    for z in range(4):
        k = lax.rem(place[3] + 4 - z, 4)
        a, b = own[k].astype(F32), other[k].astype(F32)
        for i, part in ((2 * z, jnp.where(first, a, b)), (2 * z + 1, jnp.where(first, b, a))):
            span = pl.ds(512 * i, 512)
            part = jnp.concatenate([part[:72], part[72:]], axis=1) * wide_gain[:, span]
            high = part.astype(BF16).astype(F32)
            both = jnp.concatenate([high, part - high], axis=0).astype(BF16)
            made = [dot(both, w[span, :], 1, 0) for w in (big_x, big_b, big_c)]
            made.append(dot(both, w_dt[:, span], 1, 1))
            sums = [total + extra for total, extra in zip(sums, made)]
    product[...] = jnp.zeros_like(product)
    begun = 0
    for total in sums:
        width = total.shape[1]
        product[:, pl.ds(begun, width)] = (total[:72] + total[72:]).astype(BF16)
        begun += width


def weight_product(place, own, other, wide_gain, w_dt, w_x, w_b, w_c):
    return pl.pallas_call(
        product_kernel,
        in_specs=[SMEM_SPEC] + [VMEM_SPEC] * 4 + [ANY_SPEC] * 3,
        out_specs=VMEM_SPEC,
        out_shape=jax.ShapeDtypeStruct((72, 896), BF16),
        scratch_shapes=[
            pltpu.VMEM(w_x.shape, BF16),
            pltpu.VMEM(w_b.shape, BF16),
            pltpu.VMEM(w_c.shape, BF16),
            pltpu.SemaphoreType.DMA((3,)),
        ],
        compiler_params=params(56),
        name="product",
    )(place, own, other, wide_gain, w_dt, w_x, w_b, w_c)


def norm_kernel(place, own, other, gain, pool, normed, residual, x):
    first = place[0] == 0
    for f in range(3):
        frame = pl.ds(144 * f, 144)
        for z in range(4):
            k = lax.rem(place[3] + 4 - z, 4)
            mine = own[k, frame, :]
            a, b = mine.astype(F32), other[k, frame, :].astype(F32)
            x[pl.ds(288 * z, 144), :] = jnp.where(first, a, b)
            x[pl.ds(288 * z + 144, 144), :] = jnp.where(first, b, a)
            pooled = dot(mine, pool[...], 1, 0)
            residual[z, f] = jnp.concatenate([pooled[:72], pooled[72:]], axis=1)
        values = x[...]
        width = values.shape[0]
        centre = jnp.sum(values, axis=0, keepdims=True) * (1.0 / width)
        values = values - centre
        spread = jnp.sum(values * values, axis=0, keepdims=True) * (1.0 / width)
        normed[f] = (values * lax.rsqrt(spread + 1e-06) * gain[...]).astype(BF16)


def norm_frames(place, own, other, ln_gain, pool):
    return pl.pallas_call(
        norm_kernel,
        in_specs=[SMEM_SPEC] + [VMEM_SPEC] * 4,
        out_specs=(VMEM_SPEC, VMEM_SPEC),
        out_shape=(
            jax.ShapeDtypeStruct((3, 1152, 256), BF16),
            jax.ShapeDtypeStruct((4, 3, 72, 128), F32),
        ),
        scratch_shapes=[pltpu.VMEM((1152, 256), F32)],
        compiler_params=params(16),
        name="norm",
    )(place, own, other, ln_gain, pool)


def vision_kernel(place, rows, normed, pool, block, *rest):
    ring = rest[:4]
    keep, give, wx, wy, qkv, ctx, scores, powered, sems = rest[4:]
    frame = pl.program_id(0)
    first = place[0] == 0

    def copies():
        pairs = [
            (block.at[:, :, :, pl.ds(0, XW)], wx.at[:, pl.ds(0, 3)]),
            (block.at[:, :, :, pl.ds(XW, 1152 - XW)], wy.at[:, pl.ds(0, 3)]),
        ]
        for source, ahead in zip(ring, (0, 3, 1, 2)):
            index = lax.rem(place[5] + ahead, 4)
            rows = pl.ds(3, 9)
            pairs.append((source.at[:, :, pl.ds(0, XW)], wx.at[index, rows]))
            pairs.append((source.at[:, :, pl.ds(XW, 1152 - XW)], wy.at[index, rows]))
        return [
            pltpu.make_async_copy(source, held, sems.at[n])
            for n, (source, held) in enumerate(pairs)
        ]

    @pl.when(frame == 0)
    def _():
        for copy in copies():
            copy.start()
        for copy in copies():
            copy.wait()

    width = normed.shape[1]
    for m in range(3):
        left = wx[m].reshape(576, XW)
        right = wy[m].reshape(576, width - XW)
        qkv[m] = dot(left, normed[0, :XW], 1, 0) + dot(right, normed[0, XW:], 1, 0)
    valid = rows[frame] * GRID
    usable = lax.broadcasted_iota(jnp.int32, (256, 256), 0) < valid
    for h in range(8):
        span = pl.ds(h * VHD, VHD)
        q, k = (qkv[m, span, :].astype(BF16) for m in range(2))
        scores[h] = dot(k, q, 0, 0)
    shares = []
    for h in range(8):
        values = jnp.where(usable, scores[h], -1e30)
        top = jnp.max(values, axis=0, keepdims=True)
        values = jnp.exp((values - top) * VHD ** (-0.5))
        shares.append(1.0 / jnp.sum(values, axis=0, keepdims=True))
        powered[h] = values.astype(BF16)
    for h in range(8):
        span = pl.ds(h * VHD, VHD)
        ctx[span, :] = dot(qkv[2, span, :].astype(BF16), powered[h], 1, 0) * shares[h]
    pooled = dot(ctx[...].astype(BF16), pool[...], 1, 0)
    high = pooled.astype(BF16)
    low = (pooled - high.astype(F32)).astype(BF16)
    both = jnp.concatenate([high, low], axis=1)
    out_x = dot(both, wx[3].reshape(576, XW), 0, 0)
    out_y = dot(both, wy[3].reshape(576, width - XW), 0, 0)
    attended = jnp.concatenate([out_x, out_y], axis=1)
    attended = (attended[:64] + attended[64:]).T
    for z in range(4):
        a = attended[(2 * z) * 144 : (2 * z + 1) * 144]
        b = attended[(2 * z + 1) * 144 : (2 * z + 2) * 144]
        own = jnp.where(first, a, b)
        far = jnp.where(first, b, a)
        keep[z, 0] = jnp.concatenate([own[:72], own[72:]], axis=1)
        give[z, 0] = jnp.concatenate([far[:72], far[72:]], axis=1)


def vision(place, rows, normed, pool, block, ring):
    out = pl.BlockSpec((4, 1, 72, 128), lambda f: (0, f, 0, 0))
    shape = jax.ShapeDtypeStruct((4, 3, 72, 128), F32)
    return pl.pallas_call(
        vision_kernel,
        grid=(3,),
        in_specs=[
            SMEM_SPEC,
            SMEM_SPEC,
            pl.BlockSpec((1, 1152, 256), lambda f: (f, 0, 0)),
            VMEM_SPEC,
        ]
        + [ANY_SPEC] * 5,
        out_specs=(out, out),
        out_shape=(shape, shape),
        scratch_shapes=[
            pltpu.VMEM((4, 12, 48, XW), BF16),
            pltpu.VMEM((4, 12, 48, 1152 - XW), BF16),
            pltpu.VMEM((3, 576, 256), F32),
            pltpu.VMEM((576, 256), F32),
            pltpu.VMEM((8, 256, 256), F32),
            pltpu.VMEM((8, 256, 256), BF16),
            pltpu.SemaphoreType.DMA((10,)),
        ],
        compiler_params=params(40),
        name="vision",
    )(place, rows, normed, pool, block, *ring)


def bucket_kernel(place, ids, *refs):
    out = refs[4]
    out[...] = jnp.zeros_like(out)
    for k in range(4):
        z = lax.rem(place[3] + 4 - k, 4)
        for j in range(3):
            frame = ids[3 * z + j]
            spot = lax.rem(frame, 12) + 1
            label = jnp.zeros((8, 128), F32) + spot.astype(F32)
            whole = jnp.concatenate([refs[k][j].astype(F32), label], axis=0)
            out[lax.div(frame, 12)] = whole.astype(BF16)


def bucket(place, ids, seen):
    return pl.pallas_call(
        bucket_kernel,
        in_specs=[SMEM_SPEC, SMEM_SPEC] + [VMEM_SPEC] * 4,
        out_specs=VMEM_SPEC,
        out_shape=jax.ShapeDtypeStruct((32, 80, 128), BF16),
        compiler_params=params(16),
        name="bucket",
    )(place, ids, *seen)


def place_kernel(incoming, out, held):
    held[...] = incoming[...].astype(F32)
    left = lax.broadcasted_iota(jnp.int32, (72, 128), 1) < 64

    def frame(p):
        found = jnp.zeros((72, 128), F32)
        for s in range(32):
            here = held[s, pl.ds(72, 1), :] == float(p + 1)
            found = jnp.where(here, held[s, pl.ds(0, 72), :], found)
        return found

    for pair in range(6):
        a, b = frame(2 * pair), frame(2 * pair + 1)
        lanes = pl.ds(128 * pair, 128)
        top = jnp.where(left, a, pltpu.roll(b, 64, 1))
        bottom = jnp.where(left, pltpu.roll(a, 64, 1), b)
        out[:, lanes] = jnp.concatenate([top, bottom], axis=0).astype(BF16)


def place_frames(incoming):
    return pl.pallas_call(
        place_kernel,
        in_specs=[VMEM_SPEC],
        out_specs=VMEM_SPEC,
        out_shape=jax.ShapeDtypeStruct((144, 768), BF16),
        scratch_shapes=[pltpu.VMEM((32, 80, 128), F32)],
        compiler_params=params(16),
        name="place",
    )(incoming)


def stream_kernel(place, mine, other, w_conn, *rest):
    pieces = rest[:5]
    stream, raw, squares, seen, wide, conn, held, sems = rest[5:]
    copies = [pltpu.make_async_copy(w_conn, conn, sems.at[0])]
    for n, (k, lo, size) in enumerate(
        ((0, 0, 288), (1, 0, 288), (2, 0, 144), (2, 144, 144), (3, 0, 288))
    ):
        begun = pl.multiple_of(lax.rem(place[2] + 4 - k, 4) * 288 + lo, 144)
        held_rows = wide.at[pl.ds(begun, size)]
        copies.append(pltpu.make_async_copy(pieces[n], held_rows, sems.at[n + 1]))
    for copy in copies:
        copy.start()
    first = place[0] == 0
    for z in range(4):
        a, b = mine[pl.ds(144 * z, 144), :], other[pl.ds(144 * z, 144), :]
        seen[pl.ds(288 * z, 144), :] = jnp.where(first, a, b)
        seen[pl.ds(288 * z + 144, 144), :] = jnp.where(first, b, a)
    for copy in copies:
        copy.wait()
    held[pl.ds(0, 768), :] = dot(wide[:, pl.ds(0, 768)], seen[...], 0, 0)
    held[pl.ds(768, 8), :] = dot(wide[:, pl.ds(768, 128)], seen[...], 0, 0)[:8]
    out = pltpu.make_async_copy(held, raw, sems.at[6])
    out.start()
    made = dot(conn[...], seen[...], 0, 0).astype(BF16)
    values = made.astype(F32)
    squares[...] = jnp.broadcast_to(
        jnp.sum(values * values, axis=0, keepdims=True), squares.shape
    )
    stream[...] = values.T.astype(BF16)
    out.wait()


def stream_rows(place, mine, other, w_conn, wide):
    tokens, width = mine.shape[1], w_conn.shape[1]
    return pl.pallas_call(
        stream_kernel,
        in_specs=[SMEM_SPEC] + [VMEM_SPEC] * 2 + [ANY_SPEC] * 6,
        out_specs=(VMEM_SPEC, ANY_SPEC, VMEM_SPEC),
        out_shape=(
            jax.ShapeDtypeStruct((tokens, width), BF16),
            jax.ShapeDtypeStruct((776, tokens), F32),
            jax.ShapeDtypeStruct((8, tokens), F32),
        ),
        scratch_shapes=[
            pltpu.VMEM((1152, tokens), BF16),
            pltpu.VMEM((1152, 896), BF16),
            pltpu.VMEM(w_conn.shape, BF16),
            pltpu.VMEM((776, tokens), F32),
            pltpu.SemaphoreType.DMA((7,)),
        ],
        compiler_params=params(52),
        name="stream",
    )(place, mine, other, w_conn, *wide)


def over_heads(rows, length):
    return jnp.concatenate(
        [jnp.broadcast_to(rows[h : h + 1], (HDIM, length)) for h in range(8)], axis=0
    )


def triangle(transposed):
    a = lax.broadcasted_iota(jnp.int32, (Q, Q), 0)
    b = lax.broadcasted_iota(jnp.int32, (Q, Q), 1)
    return jnp.where(a >= b if transposed else a <= b, 1.0, 0.0).astype(F32)


def state_kernel(
    raw, squares, bias, a_log, inner, writers, readers, steps, logs, enter, payload
):
    scale = lax.rsqrt(squares[0:1, :] * (1.0 / 4096) + 1e-05)
    inner[...] = (raw[:512] * scale).astype(BF16)
    writers[...] = (raw[512:640] * scale).astype(BF16)
    readers[...] = (raw[640:768] * scale).astype(BF16)
    before = raw[768:776] * scale + bias[:, :1]
    step = jnp.maximum(before, 0.0) + jnp.log1p(jnp.exp(-jnp.abs(before)))
    log = -jnp.exp(a_log[:, :1]) * step
    steps[...] = step
    logs[...] = log
    upper = triangle(False)
    count = raw.shape[1] // Q
    state = jnp.zeros((512, STATE), F32)
    whole = jnp.zeros((8, 1), F32)
    for n in range(count):
        lanes = slice(n * Q, (n + 1) * Q)
        cumul = dot(log[:, lanes], upper, 1, 0, highest)
        total = cumul[:, Q - 1 : Q]
        enter[n] = state.astype(BF16)
        left = over_heads(step[:, lanes] * jnp.exp(total - cumul), Q)
        scaled = (inner[:, lanes].astype(F32) * left).astype(BF16)
        fresh = dot(scaled, writers[:, lanes], 1, 1)
        state = state * over_heads(jnp.broadcast_to(jnp.exp(total), (8, STATE)), STATE) + fresh
        whole = whole + total
    for part in range(4):
        payload[part, pl.ds(0, 128), :] = state[128 * part : 128 * (part + 1)]
        for j in range(2):
            row = 2 * part + j
            payload[part, pl.ds(128 + 8 * j, 8), :] = jnp.broadcast_to(
                jnp.exp(whole[row : row + 1]), (8, STATE)
            )


def local_states(raw, squares, bias, a_log):
    tokens = raw.shape[1]
    return pl.pallas_call(
        state_kernel,
        in_specs=[VMEM_SPEC] * 4,
        out_specs=(VMEM_SPEC,) * 7,
        out_shape=(
            jax.ShapeDtypeStruct((512, tokens), BF16),
            jax.ShapeDtypeStruct((STATE, tokens), BF16),
            jax.ShapeDtypeStruct((STATE, tokens), BF16),
            jax.ShapeDtypeStruct((8, tokens), F32),
            jax.ShapeDtypeStruct((8, tokens), F32),
            jax.ShapeDtypeStruct((tokens // Q, 512, STATE), BF16),
            jax.ShapeDtypeStruct((4, 144, STATE), F32),
        ),
        compiler_params=params(16),
        name="states",
    )(raw, squares, bias, a_log)


def within_kernel(inner, writers, readers, steps, logs, enter, d_skip, out, begun):
    upper, lower = triangle(False), triangle(True)
    causal = upper > 0.0
    whole = jnp.zeros((8, 1), F32)
    for n in range(inner.shape[1] // Q):
        lanes = slice(n * Q, (n + 1) * Q)
        log = logs[:, lanes]
        cumul = dot(log, upper, 1, 0, highest)
        column = dot(lower, log, 1, 1, highest)
        begun[:, lanes] = cumul + whole
        whole = whole + cumul[:, Q - 1 : Q]
        meets = dot(writers[:, lanes], readers[:, lanes], 0, 0)
        carried = dot(enter[n], readers[:, lanes], 1, 0)
        grown = jnp.exp(cumul)
        step = steps[:, lanes]
        for h in range(8):
            span = slice(h * HDIM, (h + 1) * HDIM)
            apart = jnp.minimum(cumul[h : h + 1] - column[:, h : h + 1], 0.0)
            mixing = jnp.where(causal, meets * jnp.exp(apart), 0.0).astype(BF16)
            own = inner[span, lanes].astype(F32)
            scaled = (own * step[h : h + 1]).astype(BF16)
            out[span, lanes] = (
                dot(scaled, mixing, 1, 0)
                + carried[span] * grown[h : h + 1]
                + d_skip[span] * own
            )


def within(inner, writers, readers, steps, logs, enter, d_skip):
    tokens = inner.shape[1]
    return pl.pallas_call(
        within_kernel,
        in_specs=[VMEM_SPEC] * 7,
        out_specs=(VMEM_SPEC,) * 2,
        out_shape=(
            jax.ShapeDtypeStruct((512, tokens), F32),
            jax.ShapeDtypeStruct((8, tokens), F32),
        ),
        compiler_params=params(16),
        cost_estimate=pl.CostEstimate(
            flops=6_000_000_000, bytes_accessed=6_000_000, transcendentals=2_000_000
        ),
        name="within",
    )(inner, writers, readers, steps, logs, enter, d_skip)


def finish_kernel(place, local, begun, readers, *refs):
    gain, out, state = refs[4:]
    for k in range(4):
        rows = pl.ds(pl.multiple_of(lax.rem(place[1] + 4 - k, 4) * 128, 128), 128)
        state[rows, :] = refs[k][...]
    for n in range(local.shape[1] // Q):
        lanes = slice(n * Q, (n + 1) * Q)
        carried = dot(state[...], readers[:, lanes], 1, 0)
        y = local[:, lanes] + carried * over_heads(jnp.exp(begun[:, lanes]), Q)
        mean = jnp.sum(y * y, axis=0, keepdims=True) * (1.0 / 512)
        y = y * lax.rsqrt(mean + 1e-05) * gain[...]
        out[lanes, :] = y.T.astype(BF16)


def finish(place, local, begun, readers, states, gain):
    return pl.pallas_call(
        finish_kernel,
        in_specs=[SMEM_SPEC] + [VMEM_SPEC] * 8,
        out_specs=VMEM_SPEC,
        out_shape=jax.ShapeDtypeStruct((local.shape[1], 512), BF16),
        scratch_shapes=[pltpu.VMEM((512, STATE), BF16)],
        compiler_params=params(16),
        name="finish",
    )(place, local, begun, readers, *states, gain)


def two_heads(decays):
    return jnp.concatenate(
        [jnp.broadcast_to(decays[8 * j : 8 * j + 1], (HDIM, STATE)) for j in range(2)], axis=0
    )


def prefix_kernel(size, slot, place, *refs):
    got, (before, total, held) = refs[:size], refs[size:]
    for k in range(size):
        held[lax.rem(place[slot] + size - k, size)] = got[k][...].astype(F32)
    state, decay = jnp.zeros((128, STATE), F32), jnp.ones((16, STATE), F32)
    for i in range(size):
        before[i, pl.ds(0, 128), :] = state
        before[i, pl.ds(128, 16), :] = decay
        left = held[i, pl.ds(128, 16), :]
        state = state * two_heads(left) + held[i, pl.ds(0, 128), :]
        decay = decay * left
    total[...] = jnp.concatenate([state, decay], axis=0).astype(BF16)


def prefix(place, slot, got):
    size = len(got)
    return pl.pallas_call(
        functools.partial(prefix_kernel, size, slot),
        in_specs=[SMEM_SPEC] + [VMEM_SPEC] * size,
        out_specs=(VMEM_SPEC, VMEM_SPEC),
        out_shape=(
            jax.ShapeDtypeStruct((size, 144, STATE), F32),
            jax.ShapeDtypeStruct((144, STATE), BF16),
        ),
        scratch_shapes=[pltpu.VMEM((size, 144, STATE), F32)],
        compiler_params=params(4),
        name="prefix",
    )(place, *got)


def join_kernel(place, in_row, in_plane, plane, out):
    y = place[2]
    begun = jnp.where(place[4] > 0, plane[pl.ds(0, 128), :].astype(F32), 0.0)
    begun = in_plane[y, pl.ds(0, 128), :] + two_heads(in_plane[y, pl.ds(128, 16), :]) * begun
    for i in range(4):
        made = in_row[i, pl.ds(0, 128), :] + two_heads(in_row[i, pl.ds(128, 16), :]) * begun
        out[i] = made.astype(BF16)


def join(place, in_row, in_plane, plane):
    return pl.pallas_call(
        join_kernel,
        in_specs=[SMEM_SPEC] + [VMEM_SPEC] * 3,
        out_specs=VMEM_SPEC,
        out_shape=jax.ShapeDtypeStruct((4, 128, STATE), BF16),
        compiler_params=params(4),
        name="join",
    )(place, in_row, in_plane, plane)


def on_device(
    patches, grid_rows, frame_ids, ln_gain, w_qkv, w_out, w_conn, norm_gain,
    w_x, w_b, w_c, w_dt, dt_bias, a_log, d_skip, out_gain,
):
    core, x, y, zl, zh = (lax.axis_index(a) for a in ("c", "x", "y", "zl", "zh"))
    member = lax.rem(x + 2 * lax.rem(y, 2), 4)
    place = jnp.stack([core, x, y, zl, zh, member]).astype(jnp.int32)
    pool = (
        jnp.where(jnp.arange(256)[:, None] // POOL == jnp.arange(64)[None, :], 1.0 / POOL, 0.0)
    ).astype(BF16)

    block = jnp.concatenate([jnp.transpose(w_qkv, (0, 2, 1)), w_out[None]], axis=0)
    some = lax.dynamic_slice(w_conn, ((y * 4 + x) * 72, 0), (72, 512))
    some = jnp.concatenate([some[:, :256], some[:, 256:]], axis=0)
    piece = lax.dynamic_index_in_dim(block, member, 0, False)
    piece = jnp.concatenate([piece, some], axis=1)
    blocks, some = split_pieces([ring_shift(piece, "zl", 4, k) for k in (1, 2, 3)], some)
    turned = jnp.transpose(patches, (0, 2, 1)).reshape(4, 432, 256)
    own_frames = lax.dynamic_slice(grid_rows, (zl * 3,), (3,))
    block = block.reshape(4, 3, 48, 1152)
    gain = ln_gain[:, None]
    wide_gain = norm_gain[None]
    (turned, blocks, block, some, gain, wide_gain, pool, place, own_frames) = lax.optimization_barrier(
        (turned, blocks, block, some, gain, wide_gain, pool, place, own_frames)
    )
    ring = (
        blocks,
        ring_shift(blocks, "x", 4, 1),
        ring_shift(blocks, "x", 4, -1),
        ring_shift(blocks, "y", 4, 1),
    )

    other_some = swap_core(some)
    turned, _ = lax.optimization_barrier((turned, other_some))
    product = weight_product(place, some, other_some, wide_gain, w_dt.T, w_x, w_b, w_c)

    own = spread_out(lambda i: lax.dynamic_index_in_dim(turned, i, 0, False), "zl", 4)
    own, _ = lax.optimization_barrier((own, (ring, product)))
    own = jnp.stack(own)
    normed, residual = norm_frames(place, own, swap_core(own), gain, pool)
    near = [product] + [ring_shift(product, "x", 4, k) for k in (1, 2, 3)]
    rows = []
    for i in range(4):
        away = lax.rem(x + 4 - i, 4)
        found = near[0]
        for k in (1, 2, 3):
            found = jnp.where(away == k, near[k], found)
        rows.append(found)
    near = jnp.concatenate(rows, axis=0)
    before, after = ring_shift(near, "y", 4, 1), ring_shift(near, "y", 4, -1)
    far_lo, far_hi = ring_shift(before[:144], "y", 4, 1), ring_shift(after[144:], "y", 4, -1)
    wide = (near, before, far_lo, far_hi, after)

    keep, give = vision(place, own_frames, normed, pool, block, ring)
    summed = keep + residual + swap_core(give)
    token = jnp.arange(128) % 64
    kept = token[None, :] * POOL < (own_frames * GRID)[:, None]
    seen = jnp.where(kept[None, :, None, :], summed, 0.0).astype(BF16)
    seen = spread_out(lambda i: lax.dynamic_index_in_dim(seen, i, 0, False), "zl", 4)

    seen, _ = lax.optimization_barrier((seen, near))
    outgoing = bucket(place, frame_ids, seen)
    incoming = lax.all_to_all(
        outgoing, ("zh", "y", "x"), split_axis=0, concat_axis=0, tiled=True
    )
    own_features, _ = lax.optimization_barrier((place_frames(incoming), wide))
    line = lax.all_gather(own_features, "zl", axis=0, tiled=True)
    stream, raw, squares = stream_rows(place, line, swap_core(line), w_conn, wide)
    squares = squares + swap_core(squares)
    squares = squares + sum(ring_shift(squares, "zl", 4, k) for k in (1, 2, 3))

    def column(values, repeat):
        return jnp.broadcast_to(values[:, None], (values.shape[0], repeat))

    inner, writers, readers, steps, logs, enter, payload = local_states(
        raw, squares, column(dt_bias, 128), column(a_log, 128)
    )
    local, begun = within(
        inner, writers, readers, steps, logs, enter, jnp.repeat(d_skip, HDIM)[:, None]
    )
    sent = payload.astype(BF16)
    in_row, row = prefix(
        place, 1, spread_out(lambda i: lax.dynamic_index_in_dim(sent, i, 0, False), "x", 4)
    )
    in_plane, plane = prefix(place, 2, spread_out(lambda i: row, "y", 4))
    states = join(place, in_row, in_plane, ring_shift(plane, "zh", 2, 1))
    states = spread_out(lambda i: lax.dynamic_index_in_dim(states, i, 0, False), "x", 4)
    mixed = finish(place, local, begun, readers, states, out_gain[:, None])
    return stream, mixed


def solution(mesh):
    fine = Mesh(mesh.devices.reshape(2, 4, 4, 4, 2), ("zh", "y", "x", "zl", "c"))
    tm, head = ("zh", "y", "x"), ("zl", "c")
    in_specs = (
        P(tm, None, head),
        P(tm),
        P(tm),
        P(),
        P(None, None, head),
        P(head, None),
        P(None, head),
        P(),
        P(None, head),
        P(None, head),
        P(None, head),
        P(None, head),
        P(head),
        P(head),
        P(head),
        P(head),
    )
    out_specs = (P(tm, head), P(tm, head))
    return jax.shard_map(
        on_device, mesh=fine, in_specs=in_specs, out_specs=out_specs, check_vma=False
    )
```
